32 devices in a mesh: rep: 8 (over z, core), shard: 4 (over y, x).
Axes of the slice: x: 2, y: 2, z: 4, core: 2. Of those that a mesh axis runs over, the one named last changes fastest.
Arguments:
- tokens: bfloat16 [8192, 2048], P(('rep', 'shard')), may hold values from -6 to 6
- lengths: int32 [32, 4], P(('rep', 'shard')), may hold values from 1 to 128, 256 in all within a row
- ln_gain: bfloat16 [2048], P(('rep', 'shard')), may hold values from 0.5 to 1.5
- ln_bias: bfloat16 [2048], P(('rep', 'shard')), may hold values from -1.1953125 to 1.1953125
- qkv_weight: bfloat16 [2048, 6144], P(('rep', 'shard')), may hold values from -0.125 to 0.125
- qkv_bias: bfloat16 [6144], P(('rep', 'shard')), may hold values from -1.1953125 to 1.1953125
- dense_weight: bfloat16 [2048, 2048], P(('rep', 'shard')), may hold values from -0.375 to 0.375
- dense_bias: bfloat16 [2048], P(('rep', 'shard')), may hold values from -1.1953125 to 1.1953125
- up_weight: bfloat16 [2048, 8192], P(('rep', 'shard')), may hold values from -0.125 to 0.125
- up_bias: bfloat16 [8192], P(('rep', 'shard')), may hold values from -1.1953125 to 1.1953125
- down_weight: bfloat16 [8192, 2048], P(('rep', 'shard')), may hold values from -0.0625 to 0.0625
- down_bias: bfloat16 [2048], P(('rep', 'shard')), may hold values from -1.1953125 to 1.1953125
- cotangent: bfloat16 [8192, 2048], P(('rep', 'shard')), may hold values from -6 to 6
Outputs:
- output: bfloat16 [8192, 2048], P(('rep', 'shard'))
- grad_tokens: bfloat16 [8192, 2048], P(('rep', 'shard'))
- grad_ln_gain: float32 [2048], P(('rep', 'shard'))
- grad_ln_bias: float32 [2048], P(('rep', 'shard'))
- grad_qkv_weight: float32 [2048, 6144], P(('rep', 'shard'))
- grad_qkv_bias: float32 [6144], P(('rep', 'shard'))
- grad_dense_weight: float32 [2048, 2048], P(('rep', 'shard'))
- grad_dense_bias: float32 [2048], P(('rep', 'shard'))
- grad_up_weight: float32 [2048, 8192], P(('rep', 'shard'))
- grad_up_bias: float32 [8192], P(('rep', 'shard'))
- grad_down_weight: float32 [8192, 2048], P(('rep', 'shard'))
- grad_down_bias: float32 [2048], P(('rep', 'shard'))
The draws below stay inside these ranges and needn't reach their ends.
Inputs may be any that keep to these rules, and one draw needn't show every extreme that they name: `lengths`: each row lists the documents of one device; they sum to 256, and the longest is exactly 128 tokens.
All inputs are finite; a program needn't handle non-finite values.
Results may differ from the reference program's by a relative error of at most 0.0091.
Values may be sent and summed in bfloat16 or wider, within the bound.
No kernel may reach another device: no remote copies, remote signals or barrier semaphores. Data moves between devices by JAX's collectives and lax.ppermute only.
A program may use at most 448 MiB of HBM per device.

```python
import math
import jax
import jax.numpy as jnp
import numpy as np
from jax import lax

D = 2048
HEADS = 32
HEAD_DIM = 64
ROT = 32
FF = 8192
TOK_DEV = 256
DOCS = 4
MOST = 128
TOKENS = 8192
N_REP = 8
N_SHARD = 4


def with_spikes(array, own_key, source, target, parts, factor):
    def block_of(axis_at):
        return (jnp.arange(array.shape[axis_at]) // (array.shape[axis_at] // parts)).reshape((-1,) + (1,) * (array.ndim - 1 - axis_at))

    one_side = jax.random.permutation(own_key, parts)[block_of(target)]
    far = (block_of(target) + parts // 2) % parts
    return jnp.where((block_of(source) == one_side) | (block_of(source) == far), factor * array, array)


def shard_levels(own_key, shape, split, low, top_value):
    def one(axis_at, blocks):
        heights = jax.random.uniform(jax.random.fold_in(jax.random.fold_in(own_key, 6), axis_at), (blocks,), jnp.float32, low / len(split), top_value / len(split))
        return jnp.repeat(jnp.exp(heights), shape[axis_at] // blocks).reshape((-1,) + (1,) * (len(shape) - axis_at - 1))

    level = one(*split[0])
    for cut in split[1:]:
        level = level * one(*cut)
    return level


def profile(number_of, total, most, lean):
    loads = [(1 << 20) // math.isqrt(rank ** lean) + 1 for rank in range(2, number_of + 1)]
    surplus, holding = total - most - (number_of - 1), [1] * (number_of - 1)
    while surplus > 0:
        candidates = [i for i in range(number_of - 1) if holding[i] < most]
        mass, budget = sum([loads[i] for i in candidates]), surplus
        for i in candidates:
            more = min(most - holding[i], max(1, budget * loads[i] // mass), surplus)
            holding[i] = holding[i] + more
            surplus = surplus - more
    return np.array([most] + holding)


def uneven_parts(rng, number_of, total, bound, lean):
    if number_of == 2:
        one = jax.random.randint(rng, (), max(1, total - bound), min(bound, total - 1) + 1)
        return jnp.stack([one, total - one])
    tallies = jnp.asarray(profile(number_of, total, bound, lean), jnp.int32)
    pairs = (number_of - 1) // 2
    source_of, taker = tallies[1:1 + 2 * pairs:2], tallies[2:2 + 2 * pairs:2]
    margin = jnp.minimum(source_of - 1, bound - taker)
    moved = jax.random.randint(jax.random.fold_in(rng, 1), (pairs,), 0, 1 << 20) % (margin + 1)
    tallies = tallies.at[1:1 + 2 * pairs:2].set(source_of - moved).at[2:2 + 2 * pairs:2].set(taker + moved)
    return tallies[jax.random.permutation(jax.random.fold_in(rng, 2), number_of)]


def bell_draw(key, shape, scale, most, shards=(), kind=jnp.bfloat16):
    values = jax.random.normal(key, shape, jnp.float32) * scale
    if len(shards) > 0:
        values = shard_levels(key, shape, shards, -0.22, 0.18) * values
    return jnp.clip(values, min=-most, max=most).astype(kind)


def noise_with(key, shape, scale, most, pieces, heavy, kind=jnp.bfloat16):
    array = scale * jax.random.normal(key, shape, jnp.float32)
    if pieces:
        array = array * shard_levels(key, shape, pieces, -0.22, 0.18)
    return jnp.clip(with_spikes(array, jax.random.fold_in(key, 3), *heavy), -most, most).astype(kind)


def setup_inputs(seed: int = 0) -> dict:
    keys = jax.random.split(jax.random.key(seed), 14)
    return {
        "tokens": bell_draw(keys[0], (TOKENS, D), 1.0, 6.0, ((0, 32),)),
        "lengths": jax.vmap(lambda own: uneven_parts(own, DOCS, TOK_DEV, MOST, 1))(jax.random.split(keys[1], (N_REP * N_SHARD))).reshape((N_REP * N_SHARD, DOCS)).astype(jnp.int32),
        "ln_gain": jnp.clip(1.0 + 0.1 * jax.random.normal(keys[2], (D,), jnp.float32), 0.5, 1.5).astype(jnp.bfloat16),
        "ln_bias": bell_draw(keys[3], (D,), 0.2, 1.1953125, ((0, 32),)),
        "qkv_weight": bell_draw(keys[4], (D, 3 * D), D ** -0.5, 0.125, ((0, 32),)),
        "qkv_bias": bell_draw(keys[5], (3 * D,), 0.2, 1.1953125, ((0, 32),)),
        "dense_weight": bell_draw(keys[6], (D, D), (D // 8) ** -0.5, 0.375, ((0, 32),)),
        "dense_bias": bell_draw(keys[7], (D,), 0.2, 1.1953125, ((0, 32),)),
        "up_weight": bell_draw(keys[8], (D, FF), D ** -0.5, 0.125, ((0, 32),)),
        "up_bias": bell_draw(keys[9], (FF,), 0.2, 1.1953125, ((0, 32),)),
        "down_weight": bell_draw(keys[10], (FF, D), FF ** -0.5, 0.0625, ((0, 32),)),
        "down_bias": bell_draw(keys[11], (D,), 0.2, 1.1953125, ((0, 32),)),
        "cotangent": noise_with(keys[12], (TOKENS, D), 1.0, 6.0, ((0, 32),), (0, 1, 32, 2.75)),
    }


EPSILON = 1e-05
HIGHEST = lax.Precision.HIGHEST

@jax.custom_vjp
def low(v):
    return lax.optimization_barrier(v.astype(jnp.bfloat16)).astype(jnp.float32)

@jax.custom_vjp
def low_back(v):
    return v

def low_keep(v):
    return (low(v), None)

def low_pass(kept, grad):
    return (grad,)

def back_keep(v):
    return (v, None)

def back_low(kept, grad):
    return (low(grad),)
low.defvjp(low_keep, low_pass)
low_back.defvjp(back_keep, back_low)

def matmul(left_side, right_side):
    return jnp.dot(left_side, right_side, precision=HIGHEST)

def positions(doc_sizes, row_count):
    ends_at = jnp.cumsum(doc_sizes).astype(jnp.int32)
    starts_at = (ends_at - doc_sizes).astype(jnp.int32)
    indices = jnp.arange(row_count, dtype=jnp.int32)
    doc_ids = lax.optimization_barrier(jnp.sum((indices[:, None] >= ends_at[None, :]).astype(jnp.int32), axis=1)).astype(jnp.int32)
    member = doc_ids[:, None] == jnp.arange(doc_sizes.shape[0], dtype=jnp.int32)[None, :]
    offsets = lax.optimization_barrier(jnp.sum(jnp.where(member, starts_at[None, :], 0), axis=1)).astype(jnp.int32)
    places = (indices - offsets).astype(jnp.float32)
    allowed = (doc_ids[:, None] == doc_ids[None, :]) & (indices[None, :] <= indices[:, None])
    return (places, allowed)

def rotary(places):
    indices = jnp.arange(ROT // 2, dtype=jnp.float32)
    inverse = jnp.power(jnp.float32(10000.0), -2.0 * indices / ROT)
    angles = places[:, None] * inverse[None, :]
    return (jnp.cos(angles)[:, None, :], jnp.sin(angles)[:, None, :])

def rotate(values, cosine, sine):
    lower_half = values[..., :ROT // 2]
    upper_half = values[..., ROT // 2:ROT]
    return jnp.concatenate([lower_half * cosine - upper_half * sine, upper_half * cosine + lower_half * sine, values[..., ROT:]], axis=-1)

def block_forward(params, block_rows, places, allowed):
    gain, shift, qkv_w, qkv_b, dense_w, dense_b, up_w, up_b, down_w, down_b = params
    row_count = block_rows.shape[0]
    average = lax.optimization_barrier(jnp.mean(block_rows, axis=1, keepdims=True))
    centered = block_rows - average
    spread = lax.optimization_barrier(jnp.mean(centered * centered, axis=1, keepdims=True))
    normed = centered * lax.rsqrt(spread + EPSILON)
    hidden = low(normed * gain + shift)
    packed = low_back(matmul(hidden, qkv_w) + qkv_b).reshape(row_count, 3, HEADS, HEAD_DIM)
    cosine, sine = rotary(places)
    queries = low(rotate(packed[:, 0], cosine, sine))
    keys_rot = low(rotate(packed[:, 1], cosine, sine))
    values_low = low(packed[:, 2])
    scaling = 1.0 / math.sqrt(HEAD_DIM)
    scores = low_back(scaling * jnp.einsum('qhd,khd->hqk', queries, keys_rot, precision=HIGHEST))
    scores = jnp.where(allowed[None], scores, -1e+30)
    probs = jax.nn.softmax(scores, axis=-1)
    context = jnp.einsum('hqk,khd->qhd', low(probs), values_low, precision=HIGHEST).reshape(row_count, HEADS * HEAD_DIM)
    context = low(low_back(context))
    attended = matmul(context, dense_w) + dense_b
    upward = low_back(matmul(hidden, up_w) + up_b)
    active = low(jax.nn.gelu(upward, approximate=True))
    downward = matmul(active, down_w) + down_b
    return block_rows + attended + downward

def reference(tokens, lengths, ln_gain, ln_bias, qkv_weight, qkv_bias, dense_weight, dense_bias, up_weight, up_bias, down_weight, down_bias, cotangent):
    params = tuple((tensor.astype(jnp.float32) for tensor in (ln_gain, ln_bias, qkv_weight, qkv_bias, dense_weight, dense_bias, up_weight, up_bias, down_weight, down_bias)))
    devices_all = N_REP * N_SHARD
    blocks_in = tokens.astype(jnp.float32).reshape(devices_all, TOK_DEV, D)
    blocks_cot = cotangent.astype(jnp.float32).reshape(devices_all, TOK_DEV, D)

    def device_step(summed, inputs_now):
        block_rows, doc_sizes, block_cot = inputs_now
        places, allowed = positions(doc_sizes, TOK_DEV)

        def forward_only(weights_now, rows_now):
            return block_forward(weights_now, rows_now, places, allowed)
        result, pullback = jax.vjp(forward_only, params, block_rows)
        grad_params, grad_rows = pullback(block_cot)
        summed = tuple((earlier + extra for earlier, extra in zip(summed, grad_params)))
        return (summed, (result.astype(jnp.bfloat16), grad_rows.astype(jnp.bfloat16)))
    zeros = tuple((jnp.zeros_like(tensor) for tensor in params))
    summed, (results, grads_in) = lax.scan(device_step, zeros, (blocks_in, lengths, blocks_cot))
    return (results.reshape(TOKENS, D), grads_in.reshape(TOKENS, D), summed[0], summed[1], summed[2], summed[3], summed[4], summed[5], summed[6], summed[7], summed[8], summed[9])
```

```python
import math

import jax
import jax.numpy as jnp
from jax import lax
from jax.sharding import PartitionSpec as P

HEADS = 32
HEAD_DIM = 64
ROT = 32
CORES = 2
AXES = ("rep", "shard")
BF16 = jnp.bfloat16
F32 = jnp.float32


EPSILON = 1e-05


def positions(doc_sizes, row_count):
    ends_at = jnp.cumsum(doc_sizes)
    starts_at = ends_at - doc_sizes
    indices = jnp.arange(row_count, dtype=jnp.int32)
    doc_ids = jnp.sum((indices[:, None] >= ends_at[None, :]).astype(jnp.int32), axis=1)
    member = doc_ids[:, None] == jnp.arange(doc_sizes.shape[0], dtype=jnp.int32)[None, :]
    offsets = jnp.sum(jnp.where(member, starts_at[None, :], 0), axis=1)
    places = (indices - offsets).astype(jnp.float32)
    allowed = (doc_ids[:, None] == doc_ids[None, :]) & (indices[None, :] <= indices[:, None])
    return (places, allowed)


def rotary(places):
    indices = jnp.arange(ROT // 2, dtype=jnp.float32)
    inverse = jnp.power(jnp.float32(10000.0), -2.0 * indices / ROT)
    angles = places[:, None] * inverse[None, :]
    return (jnp.cos(angles)[:, None, :], jnp.sin(angles)[:, None, :])


def rotate(values, cosine, sine):
    lower_half = values[..., : ROT // 2]
    upper_half = values[..., ROT // 2 : ROT]
    return jnp.concatenate(
        [
            lower_half * cosine - upper_half * sine,
            upper_half * cosine + lower_half * sine,
            values[..., ROT:],
        ],
        axis=-1,
    )


def unrotate(incoming, cosine, sine):
    lower_half = incoming[..., : ROT // 2]
    upper_half = incoming[..., ROT // 2 : ROT]
    return jnp.concatenate(
        [
            lower_half * cosine + upper_half * sine,
            upper_half * cosine - lower_half * sine,
            incoming[..., ROT:],
        ],
        axis=-1,
    )


def project(weight, left_side):
    whole = lax.all_gather(weight, ("rep", "shard"), axis=0, tiled=True)
    return jnp.dot(left_side, whole, preferred_element_type=jnp.float32)


def back_project(weight, incoming):
    whole = lax.all_gather(weight, ("rep", "shard"), axis=0, tiled=True)
    return lax.dot_general(
        incoming, whole, (((1,), (1,)), ((), ())), preferred_element_type=jnp.float32
    )


def weight_grad(left_side, incoming):
    return lax.psum_scatter(
        lax.dot_general(
            left_side, incoming, (((0,), (0,)), ((), ())), preferred_element_type=jnp.float32
        ),
        ("rep", "shard"),
        scatter_dimension=0,
        tiled=True,
    )


def gathered_whole(
    tokens,
    lengths,
    ln_gain,
    ln_bias,
    qkv_weight,
    qkv_bias,
    dense_weight,
    dense_bias,
    up_weight,
    up_bias,
    down_weight,
    down_bias,
    cotangent,
):
    row_count = tokens.shape[0]
    width = tokens.shape[1]
    small = (
        lax.all_gather(ln_gain, ("rep", "shard"), axis=0, tiled=True),
        lax.all_gather(ln_bias, ("rep", "shard"), axis=0, tiled=True),
        lax.all_gather(qkv_bias, ("rep", "shard"), axis=0, tiled=True),
        lax.all_gather(dense_bias, ("rep", "shard"), axis=0, tiled=True),
        lax.all_gather(up_bias, ("rep", "shard"), axis=0, tiled=True),
        lax.all_gather(down_bias, ("rep", "shard"), axis=0, tiled=True),
    )
    gain, shift, packed_bias, dense_shift, upward_bias, downward_bias = [
        tensor.astype(jnp.float32) for tensor in small
    ]
    places, allowed = positions(lengths[0], row_count)
    cosine, sine = rotary(places)
    scaling = 1.0 / math.sqrt(HEAD_DIM)
    inputs_f = tokens.astype(jnp.float32)
    average = jnp.mean(inputs_f, axis=1, keepdims=True)
    centered = inputs_f - average
    spread = jnp.mean(centered * centered, axis=1, keepdims=True)
    inv_std = lax.rsqrt(spread + EPSILON)
    normed = centered * inv_std
    hidden_low = (normed * gain + shift).astype(jnp.bfloat16)
    packed = (project(qkv_weight, hidden_low) + packed_bias).reshape(row_count, 3, HEADS, HEAD_DIM)
    queries = rotate(packed[:, 0], cosine, sine).astype(jnp.bfloat16)
    keys_rot = rotate(packed[:, 1], cosine, sine).astype(jnp.bfloat16)
    values_low = packed[:, 2].astype(jnp.bfloat16)
    scores = scaling * jnp.einsum(
        "qhd,khd->hqk", queries, keys_rot, preferred_element_type=jnp.float32
    )
    scores = jnp.where(allowed[None], scores, -1e30)
    maximum = jnp.max(scores, axis=-1, keepdims=True)
    raised = jnp.exp(scores - maximum)
    totals = jnp.sum(raised, axis=-1, keepdims=True)
    probs = raised / totals
    log_total = maximum + jnp.log(totals)
    context = jnp.einsum(
        "hqk,khd->qhd", probs.astype(jnp.bfloat16), values_low, preferred_element_type=jnp.float32
    )
    context_low = context.reshape(row_count, width).astype(jnp.bfloat16)
    attended = project(dense_weight, context_low) + dense_shift
    upward = project(up_weight, hidden_low) + upward_bias
    active_low = jax.nn.gelu(upward, approximate=True).astype(jnp.bfloat16)
    downward = project(down_weight, active_low) + downward_bias
    output = (inputs_f + attended + downward).astype(jnp.bfloat16)
    grad_out = cotangent.astype(jnp.float32)
    d_active = back_project(down_weight, cotangent)
    gelu_value, gelu_pull = jax.vjp(lambda inner: jax.nn.gelu(inner, approximate=True), upward)
    d_upward_low = gelu_pull(d_active)[0].astype(jnp.bfloat16)
    d_context_low = (
        back_project(dense_weight, cotangent)
        .astype(jnp.bfloat16)
        .reshape(row_count, HEADS, HEAD_DIM)
    )
    again = scaling * jnp.einsum(
        "qhd,khd->hqk", queries, keys_rot, preferred_element_type=jnp.float32
    )
    again = jnp.where(allowed[None], again, -1e30)
    probs_again = jnp.exp(again - log_total)
    d_values = jnp.einsum(
        "hqk,qhd->khd",
        probs_again.astype(jnp.bfloat16),
        d_context_low,
        preferred_element_type=jnp.float32,
    )
    d_probs = jnp.einsum(
        "qhd,khd->hqk", d_context_low, values_low, preferred_element_type=jnp.float32
    )
    d_scores = probs_again * (d_probs - jnp.sum(d_probs * probs_again, axis=-1, keepdims=True))
    d_scores_low = d_scores.astype(jnp.bfloat16)
    d_queries = scaling * jnp.einsum(
        "hqk,khd->qhd", d_scores_low, keys_rot, preferred_element_type=jnp.float32
    )
    d_keys = scaling * jnp.einsum(
        "hqk,qhd->khd", d_scores_low, queries, preferred_element_type=jnp.float32
    )
    d_packed = jnp.stack(
        [unrotate(d_queries, cosine, sine), unrotate(d_keys, cosine, sine), d_values], axis=1
    )
    d_packed_low = d_packed.reshape(row_count, 3 * width).astype(jnp.bfloat16)
    d_hidden = back_project(qkv_weight, d_packed_low) + back_project(up_weight, d_upward_low)
    d_norm = d_hidden * gain
    d_inputs = inv_std * (
        d_norm
        - jnp.mean(d_norm, axis=1, keepdims=True)
        - normed * jnp.mean(d_norm * normed, axis=1, keepdims=True)
    )
    grad_tokens = (grad_out + d_inputs).astype(jnp.bfloat16)
    grad_qkv_w = weight_grad(hidden_low, d_packed_low)
    grad_dense_w = weight_grad(context_low, cotangent)
    grad_up_w = weight_grad(hidden_low, d_upward_low)
    grad_down_w = weight_grad(active_low, cotangent)
    small_terms = (
        jnp.sum(d_hidden * normed, axis=0),
        jnp.sum(d_hidden, axis=0),
        jnp.sum(d_packed_low.astype(jnp.float32), axis=0),
        jnp.sum(grad_out, axis=0),
        jnp.sum(d_upward_low.astype(jnp.float32), axis=0),
    )
    reduced = (
        lax.psum_scatter(small_terms[0], ("rep", "shard"), scatter_dimension=0, tiled=True),
        lax.psum_scatter(small_terms[1], ("rep", "shard"), scatter_dimension=0, tiled=True),
        lax.psum_scatter(small_terms[2], ("rep", "shard"), scatter_dimension=0, tiled=True),
        lax.psum_scatter(small_terms[3], ("rep", "shard"), scatter_dimension=0, tiled=True),
        lax.psum_scatter(small_terms[4], ("rep", "shard"), scatter_dimension=0, tiled=True),
    )
    grad_gain, grad_shift, grad_packed_b, grad_out_b, grad_up_b = reduced
    return (
        output,
        grad_tokens,
        grad_gain,
        grad_shift,
        grad_qkv_w,
        grad_packed_b,
        grad_dense_w,
        grad_out_b,
        grad_up_w,
        grad_up_b,
        grad_down_w,
        grad_out_b,
    )


def tokens_dot(left_side, incoming):
    return lax.dot_general(
        left_side, incoming, (((0,), (0,)), ((), ())), preferred_element_type=F32
    )


def dot_transposed(left_side, weight):
    return lax.dot_general(
        left_side, weight, (((1,), (1,)), ((), ())), preferred_element_type=F32
    )


def by_planes(
    planes,
    mates,
    tokens,
    lengths,
    ln_gain,
    ln_bias,
    qkv_weight,
    qkv_bias,
    dense_weight,
    dense_bias,
    up_weight,
    up_bias,
    down_weight,
    down_bias,
    cotangent,
):
    row_count, width = tokens.shape
    owners = planes * mates
    rank = lax.axis_index("rep") * (mates // CORES) + lax.axis_index("shard")
    z, m = rank // mates, rank % mates

    def flip(value, r):
        return lax.ppermute(
            value,
            AXES,
            [(p * mates + i, p * mates + (i ^ r)) for p in range(planes) for i in range(mates)],
        )

    def shift(value, step, first, last):
        return lax.ppermute(
            value,
            AXES,
            [
                (p * mates + i, (p + step) * mates + i)
                for p in range(first, last)
                for i in range(mates)
            ],
        )

    def along_planes(piece):
        ups, downs = [piece], [piece]
        for k in range(1, planes):
            ups.append(shift(ups[-1], 1, k - 1, planes - 1))
            downs.append(shift(downs[-1], -1, 1, planes - k + 1))
        return ups, downs

    def newest_first(ups, downs):
        return jnp.concatenate(
            [ups[0]]
            + [jnp.where(z >= k, ups[k], downs[planes - k]) for k in range(1, planes)],
            axis=0,
        )

    def in_order(ups, downs):
        def block(p):
            return lax.select_n(
                z, *[ups[q - p] if q >= p else downs[p - q] for q in range(planes)]
            )

        return jnp.concatenate([block(p) for p in range(planes)], axis=0)

    def back_to_planes(blocks):
        up = down = None
        for s in range(1, planes):
            out_up, out_down = blocks[s], blocks[planes - s]
            if up is not None:
                out_up, out_down = out_up + up.astype(F32), out_down + down.astype(F32)
            up = shift(out_up.astype(BF16), 1, 0, s)
            down = shift(out_down.astype(BF16), -1, planes - s, planes)
        return blocks[0] + up.astype(F32) + down.astype(F32)

    def exchange(pieces):
        result = jnp.zeros(pieces.shape, pieces.dtype)
        for r in range(mates):
            own = lax.dynamic_index_in_dim(pieces, m ^ r, 0, keepdims=False)
            result = lax.dynamic_update_index_in_dim(
                result, own if r == 0 else flip(own, r), m ^ r, 0
            )
        return result

    def gather_rows(block):
        half = block.shape[0] // 2
        by_x, by_y = flip(block, 1), flip(block, 2)
        near = jnp.concatenate(
            [block, by_x, by_y, flip(by_y[:half], 1), flip(by_x[half:], 2)], axis=0
        )
        return jnp.concatenate([near, flip(near, 4)], axis=0)

    def scatter_rows(near, far):
        total = near + flip(far.astype(BF16), 4).astype(F32)
        own, for_x, for_y, diagonal = [
            total[i * row_count : (i + 1) * row_count] for i in range(4)
        ]
        half = row_count // 2
        extra_y = flip(diagonal[:half].astype(BF16), 1).astype(F32)
        extra_x = flip(diagonal[half:].astype(BF16), 2).astype(F32)
        for_x = jnp.concatenate([for_x[:half], for_x[half:] + extra_x], axis=0)
        for_y = jnp.concatenate([for_y[:half] + extra_y, for_y[half:]], axis=0)
        return own + flip(for_x.astype(BF16), 1).astype(F32) + flip(for_y.astype(BF16), 2).astype(F32)

    def everywhere(table):
        for r in (1, 2, 4):
            table = table + flip(table, r)
        for r in (1, 2):
            table = table + lax.ppermute(
                table,
                AXES,
                [(p * mates + i, (p ^ r) * mates + i) for p in range(planes) for i in range(mates)],
            )
        return table

    parts = [ln_gain, ln_bias, qkv_bias, dense_bias, up_bias, down_bias, lengths[0].astype(BF16)]
    sizes = [part.shape[0] for part in parts]
    starts = [sum(sizes[:i]) for i in range(len(sizes))]
    own_row = jnp.concatenate(parts)
    own_row = jnp.pad(own_row, (0, -len(own_row) % 128))
    table = jnp.where(jnp.arange(owners)[:, None] == rank, own_row[None, :], 0)
    table = everywhere(table).astype(F32)

    def column(i):
        return table[:, starts[i] : starts[i] + sizes[i]].reshape(-1)

    gain, shift_by = column(0), column(1)
    heads_here = HEADS // mates
    ff_block = up_bias.shape[0]
    packed_bias = lax.dynamic_index_in_dim(
        column(2).reshape(3, planes, mates, HEAD_DIM), m, 2, keepdims=False
    ).reshape(-1)
    upward_bias = lax.dynamic_index_in_dim(
        column(4).reshape(planes, mates, ff_block), m, 1, keepdims=False
    ).reshape(-1)
    out_bias = column(3) + column(5)
    all_lengths = table[:, starts[6] : starts[6] + sizes[6]].astype(jnp.int32)
    doc_sizes = jnp.stack(
        [
            lax.dynamic_index_in_dim(all_lengths, z * mates + (m ^ r), 0, keepdims=False)
            for r in range(mates)
        ]
    )

    rows_own = qkv_weight.shape[0]
    up_pieces = (
        up_weight.reshape(rows_own, planes, mates, ff_block)
        .transpose(2, 0, 1, 3)
        .reshape(mates, rows_own, planes * ff_block)
    )
    qkv_pieces = (
        qkv_weight.reshape(rows_own, 3, planes, mates, HEAD_DIM)
        .transpose(3, 0, 1, 2, 4)
        .reshape(mates, rows_own, 3 * planes * HEAD_DIM)
    )
    up_w = newest_first(*along_planes(exchange(up_pieces).reshape(mates * rows_own, -1)))
    dense_w = in_order(*along_planes(dense_weight))
    qkv_w = newest_first(*along_planes(exchange(qkv_pieces).reshape(mates * rows_own, -1)))
    down_w = in_order(*along_planes(down_weight))

    def turned(value):
        blocks = value.reshape(value.shape[0], planes, -1)
        return jnp.concatenate(
            [
                lax.dynamic_index_in_dim(blocks, (z - k) % planes, 1, keepdims=False)
                for k in range(planes)
            ],
            axis=1,
        )

    inputs_f = tokens.astype(F32)
    average = jnp.mean(inputs_f, axis=1, keepdims=True)
    centered = inputs_f - average
    spread = jnp.mean(centered * centered, axis=1, keepdims=True)
    inv_std = lax.rsqrt(spread + EPSILON)
    normed = centered * inv_std
    hidden_own = (normed * gain + shift_by).astype(BF16)

    cot = gather_rows(cotangent)
    hidden = gather_rows(turned(hidden_own))

    upward = jnp.dot(hidden, up_w, preferred_element_type=F32) + upward_bias
    active, gelu_pull = jax.vjp(lambda inner: jax.nn.gelu(inner, approximate=True), upward)
    active = active.astype(BF16)

    def rows_by_plane(left_side, incoming, block):
        sliced = left_side.reshape(left_side.shape[0], planes, block)
        return back_to_planes(
            [
                tokens_dot(
                    lax.dynamic_index_in_dim(sliced, (z - k) % planes, 1, keepdims=False), incoming
                )
                for k in range(planes)
            ]
        )

    def rows_by_turn(left_side, incoming):
        block = left_side.shape[1] // planes
        return back_to_planes(
            [
                tokens_dot(left_side[:, k * block : (k + 1) * block], incoming)
                for k in range(planes)
            ]
        )

    grad_down_w = rows_by_plane(active, cot, ff_block)

    places, allowed = jax.vmap(lambda sizes_now: positions(sizes_now, row_count))(doc_sizes)
    cosine, sine = jax.vmap(rotary)(places)
    scaling = 1.0 / math.sqrt(HEAD_DIM)
    packed = (jnp.dot(hidden, qkv_w, preferred_element_type=F32) + packed_bias).reshape(
        mates, row_count, 3, heads_here, HEAD_DIM
    )
    queries = rotate(packed[:, :, 0], cosine, sine).astype(BF16)
    keys_rot = rotate(packed[:, :, 1], cosine, sine).astype(BF16)
    values_low = packed[:, :, 2].astype(BF16)
    scores = scaling * jnp.einsum("rqhd,rkhd->rhqk", queries, keys_rot, preferred_element_type=F32)
    scores = jnp.where(allowed[:, None], scores, -1e30)
    maximum = jnp.max(scores, axis=-1, keepdims=True)
    raised = jnp.exp(scores - maximum)
    probs = raised / jnp.sum(raised, axis=-1, keepdims=True)
    probs_low = probs.astype(BF16)
    context = jnp.einsum("rhqk,rkhd->rqhd", probs_low, values_low, preferred_element_type=F32)
    context = context.astype(BF16).reshape(mates * row_count, heads_here * HEAD_DIM)
    d_context = dot_transposed(cot, dense_w).astype(BF16)
    grad_dense_w = rows_by_plane(context, cot, HEAD_DIM)
    d_context = d_context.reshape(mates, row_count, heads_here, HEAD_DIM)
    d_values = jnp.einsum("rhqk,rqhd->rkhd", probs_low, d_context, preferred_element_type=F32)
    d_probs = jnp.einsum("rqhd,rkhd->rhqk", d_context, values_low, preferred_element_type=F32)
    d_scores = probs * (d_probs - jnp.sum(d_probs * probs, axis=-1, keepdims=True))
    d_scores = d_scores.astype(BF16)
    d_queries = scaling * jnp.einsum(
        "rhqk,rkhd->rqhd", d_scores, keys_rot, preferred_element_type=F32
    )
    d_keys = scaling * jnp.einsum("rhqk,rqhd->rkhd", d_scores, queries, preferred_element_type=F32)
    d_packed = jnp.stack(
        [unrotate(d_queries, cosine, sine), unrotate(d_keys, cosine, sine), d_values], axis=2
    )
    d_packed = d_packed.astype(BF16).reshape(mates * row_count, -1)

    d_active = dot_transposed(cot, down_w)
    d_upward = gelu_pull(d_active)[0].astype(BF16)
    grad_up_rows = rows_by_turn(hidden, d_upward)
    grad_qkv_rows = rows_by_turn(hidden, d_packed)

    near = row_count * mates // 2

    def out_of(part):
        return jnp.dot(context[part], dense_w, preferred_element_type=F32) + jnp.dot(
            active[part], down_w, preferred_element_type=F32
        )

    def d_hidden_of(part):
        return dot_transposed(d_packed[part], qkv_w) + dot_transposed(d_upward[part], up_w)

    summed = scatter_rows(out_of(slice(0, near)), out_of(slice(near, None)))
    output = (inputs_f + summed + out_bias).astype(BF16)

    d_hidden = turned(scatter_rows(d_hidden_of(slice(0, near)), d_hidden_of(slice(near, None))))
    grad_out = cotangent.astype(F32)
    d_norm = d_hidden * gain
    d_inputs = inv_std * (
        d_norm
        - jnp.mean(d_norm, axis=1, keepdims=True)
        - normed * jnp.mean(d_norm * normed, axis=1, keepdims=True)
    )
    grad_tokens = (grad_out + d_inputs).astype(BF16)

    def pieces_of(rows):
        return exchange(rows.astype(BF16).reshape(mates, rows_own, -1)).astype(F32)

    grad_up_w = (
        pieces_of(grad_up_rows)
        .reshape(mates, rows_own, planes, ff_block)
        .transpose(1, 2, 0, 3)
        .reshape(rows_own, -1)
    )
    grad_qkv_w = (
        pieces_of(grad_qkv_rows)
        .reshape(mates, rows_own, 3, planes, HEAD_DIM)
        .transpose(1, 2, 3, 0, 4)
        .reshape(rows_own, -1)
    )

    mine = jnp.arange(mates) == m
    packed_sum = jnp.sum(d_packed.astype(F32), axis=0).reshape(3, planes, 1, HEAD_DIM)
    packed_sum = jnp.where(mine[None, None, :, None], packed_sum, 0.0)
    upward_sum = jnp.sum(d_upward.astype(F32), axis=0).reshape(planes, 1, ff_block)
    upward_sum = jnp.where(mine[None, :, None], upward_sum, 0.0)
    sums = jnp.concatenate(
        [
            jnp.sum(d_hidden * normed, axis=0).reshape(owners, -1),
            jnp.sum(d_hidden, axis=0).reshape(owners, -1),
            jnp.sum(grad_out, axis=0).reshape(owners, -1),
            packed_sum.reshape(owners, -1),
            upward_sum.reshape(owners, -1),
        ],
        axis=1,
    )
    total = lax.dynamic_index_in_dim(everywhere(sums), rank, 0, keepdims=False)
    grad_gain, grad_shift, grad_out_b, grad_packed_b, grad_up_b = jnp.split(
        total,
        [
            sizes[0],
            sizes[0] + sizes[1],
            sizes[0] + sizes[1] + sizes[3],
            sizes[0] + sizes[1] + sizes[3] + sizes[2],
        ],
    )
    return (
        output,
        grad_tokens,
        grad_gain,
        grad_shift,
        grad_qkv_w,
        grad_packed_b,
        grad_dense_w,
        grad_out_b,
        grad_up_w,
        grad_up_b,
        grad_down_w,
        grad_out_b,
    )


def solution(mesh):
    planes, mates = mesh.shape["rep"] // CORES, CORES * mesh.shape["shard"]
    rows, vector = P(AXES, None), P(AXES)

    def layer(*arrays):
        width = arrays[0].shape[1]
        if mesh.shape["shard"] == 4 and planes * mates * HEAD_DIM == width:
            return by_planes(planes, mates, *arrays)
        return gathered_whole(*arrays)

    return jax.shard_map(
        layer,
        mesh=mesh,
        in_specs=(
            rows, rows, vector, vector, rows, vector, rows, vector, rows, vector, rows, vector, rows,
        ),
        out_specs=(
            rows, rows, vector, vector, rows, vector, rows, vector, rows, vector, rows, vector,
        ),
        check_vma=False,
    )
```

```python
import functools
import math

import jax
import jax.numpy as jnp
from jax import lax
from jax.experimental import pallas as pl
from jax.experimental.pallas import tpu as pltpu
from jax.sharding import PartitionSpec as P

HEADS = 32
HEAD_DIM = 64
ROT = 32
CORES = 2
AXES = ("rep", "shard")
BF16 = jnp.bfloat16
F32 = jnp.float32


EPSILON = 1e-05


def positions(doc_sizes, row_count):
    ends_at = jnp.cumsum(doc_sizes)
    starts_at = ends_at - doc_sizes
    indices = jnp.arange(row_count, dtype=jnp.int32)
    doc_ids = jnp.sum((indices[:, None] >= ends_at[None, :]).astype(jnp.int32), axis=1)
    member = doc_ids[:, None] == jnp.arange(doc_sizes.shape[0], dtype=jnp.int32)[None, :]
    offsets = jnp.sum(jnp.where(member, starts_at[None, :], 0), axis=1)
    places = (indices - offsets).astype(jnp.float32)
    allowed = (doc_ids[:, None] == doc_ids[None, :]) & (indices[None, :] <= indices[:, None])
    return (places, allowed)


def rotary(places):
    indices = jnp.arange(ROT // 2, dtype=jnp.float32)
    inverse = jnp.power(jnp.float32(10000.0), -2.0 * indices / ROT)
    angles = places[:, None] * inverse[None, :]
    return (jnp.cos(angles)[:, None, :], jnp.sin(angles)[:, None, :])


def rotate(values, cosine, sine):
    lower_half = values[..., : ROT // 2]
    upper_half = values[..., ROT // 2 : ROT]
    return jnp.concatenate(
        [
            lower_half * cosine - upper_half * sine,
            upper_half * cosine + lower_half * sine,
            values[..., ROT:],
        ],
        axis=-1,
    )


def unrotate(incoming, cosine, sine):
    lower_half = incoming[..., : ROT // 2]
    upper_half = incoming[..., ROT // 2 : ROT]
    return jnp.concatenate(
        [
            lower_half * cosine + upper_half * sine,
            upper_half * cosine - lower_half * sine,
            incoming[..., ROT:],
        ],
        axis=-1,
    )


def project(weight, left_side):
    whole = lax.all_gather(weight, ("rep", "shard"), axis=0, tiled=True)
    return jnp.dot(left_side, whole, preferred_element_type=jnp.float32)


def back_project(weight, incoming):
    whole = lax.all_gather(weight, ("rep", "shard"), axis=0, tiled=True)
    return lax.dot_general(
        incoming, whole, (((1,), (1,)), ((), ())), preferred_element_type=jnp.float32
    )


def weight_grad(left_side, incoming):
    return lax.psum_scatter(
        lax.dot_general(
            left_side, incoming, (((0,), (0,)), ((), ())), preferred_element_type=jnp.float32
        ),
        ("rep", "shard"),
        scatter_dimension=0,
        tiled=True,
    )


def gathered_whole(
    tokens,
    lengths,
    ln_gain,
    ln_bias,
    qkv_weight,
    qkv_bias,
    dense_weight,
    dense_bias,
    up_weight,
    up_bias,
    down_weight,
    down_bias,
    cotangent,
):
    row_count = tokens.shape[0]
    width = tokens.shape[1]
    small = (
        lax.all_gather(ln_gain, ("rep", "shard"), axis=0, tiled=True),
        lax.all_gather(ln_bias, ("rep", "shard"), axis=0, tiled=True),
        lax.all_gather(qkv_bias, ("rep", "shard"), axis=0, tiled=True),
        lax.all_gather(dense_bias, ("rep", "shard"), axis=0, tiled=True),
        lax.all_gather(up_bias, ("rep", "shard"), axis=0, tiled=True),
        lax.all_gather(down_bias, ("rep", "shard"), axis=0, tiled=True),
    )
    gain, shift, packed_bias, dense_shift, upward_bias, downward_bias = [
        tensor.astype(jnp.float32) for tensor in small
    ]
    places, allowed = positions(lengths[0], row_count)
    cosine, sine = rotary(places)
    scaling = 1.0 / math.sqrt(HEAD_DIM)
    inputs_f = tokens.astype(jnp.float32)
    average = jnp.mean(inputs_f, axis=1, keepdims=True)
    centered = inputs_f - average
    spread = jnp.mean(centered * centered, axis=1, keepdims=True)
    inv_std = lax.rsqrt(spread + EPSILON)
    normed = centered * inv_std
    hidden_low = (normed * gain + shift).astype(jnp.bfloat16)
    packed = (project(qkv_weight, hidden_low) + packed_bias).reshape(row_count, 3, HEADS, HEAD_DIM)
    queries = rotate(packed[:, 0], cosine, sine).astype(jnp.bfloat16)
    keys_rot = rotate(packed[:, 1], cosine, sine).astype(jnp.bfloat16)
    values_low = packed[:, 2].astype(jnp.bfloat16)
    scores = scaling * jnp.einsum(
        "qhd,khd->hqk", queries, keys_rot, preferred_element_type=jnp.float32
    )
    scores = jnp.where(allowed[None], scores, -1e30)
    maximum = jnp.max(scores, axis=-1, keepdims=True)
    raised = jnp.exp(scores - maximum)
    totals = jnp.sum(raised, axis=-1, keepdims=True)
    probs = raised / totals
    log_total = maximum + jnp.log(totals)
    context = jnp.einsum(
        "hqk,khd->qhd", probs.astype(jnp.bfloat16), values_low, preferred_element_type=jnp.float32
    )
    context_low = context.reshape(row_count, width).astype(jnp.bfloat16)
    attended = project(dense_weight, context_low) + dense_shift
    upward = project(up_weight, hidden_low) + upward_bias
    active_low = jax.nn.gelu(upward, approximate=True).astype(jnp.bfloat16)
    downward = project(down_weight, active_low) + downward_bias
    output = (inputs_f + attended + downward).astype(jnp.bfloat16)
    grad_out = cotangent.astype(jnp.float32)
    d_active = back_project(down_weight, cotangent)
    gelu_value, gelu_pull = jax.vjp(lambda inner: jax.nn.gelu(inner, approximate=True), upward)
    d_upward_low = gelu_pull(d_active)[0].astype(jnp.bfloat16)
    d_context_low = (
        back_project(dense_weight, cotangent)
        .astype(jnp.bfloat16)
        .reshape(row_count, HEADS, HEAD_DIM)
    )
    again = scaling * jnp.einsum(
        "qhd,khd->hqk", queries, keys_rot, preferred_element_type=jnp.float32
    )
    again = jnp.where(allowed[None], again, -1e30)
    probs_again = jnp.exp(again - log_total)
    d_values = jnp.einsum(
        "hqk,qhd->khd",
        probs_again.astype(jnp.bfloat16),
        d_context_low,
        preferred_element_type=jnp.float32,
    )
    d_probs = jnp.einsum(
        "qhd,khd->hqk", d_context_low, values_low, preferred_element_type=jnp.float32
    )
    d_scores = probs_again * (d_probs - jnp.sum(d_probs * probs_again, axis=-1, keepdims=True))
    d_scores_low = d_scores.astype(jnp.bfloat16)
    d_queries = scaling * jnp.einsum(
        "hqk,khd->qhd", d_scores_low, keys_rot, preferred_element_type=jnp.float32
    )
    d_keys = scaling * jnp.einsum(
        "hqk,qhd->khd", d_scores_low, queries, preferred_element_type=jnp.float32
    )
    d_packed = jnp.stack(
        [unrotate(d_queries, cosine, sine), unrotate(d_keys, cosine, sine), d_values], axis=1
    )
    d_packed_low = d_packed.reshape(row_count, 3 * width).astype(jnp.bfloat16)
    d_hidden = back_project(qkv_weight, d_packed_low) + back_project(up_weight, d_upward_low)
    d_norm = d_hidden * gain
    d_inputs = inv_std * (
        d_norm
        - jnp.mean(d_norm, axis=1, keepdims=True)
        - normed * jnp.mean(d_norm * normed, axis=1, keepdims=True)
    )
    grad_tokens = (grad_out + d_inputs).astype(jnp.bfloat16)
    grad_qkv_w = weight_grad(hidden_low, d_packed_low)
    grad_dense_w = weight_grad(context_low, cotangent)
    grad_up_w = weight_grad(hidden_low, d_upward_low)
    grad_down_w = weight_grad(active_low, cotangent)
    small_terms = (
        jnp.sum(d_hidden * normed, axis=0),
        jnp.sum(d_hidden, axis=0),
        jnp.sum(d_packed_low.astype(jnp.float32), axis=0),
        jnp.sum(grad_out, axis=0),
        jnp.sum(d_upward_low.astype(jnp.float32), axis=0),
    )
    reduced = (
        lax.psum_scatter(small_terms[0], ("rep", "shard"), scatter_dimension=0, tiled=True),
        lax.psum_scatter(small_terms[1], ("rep", "shard"), scatter_dimension=0, tiled=True),
        lax.psum_scatter(small_terms[2], ("rep", "shard"), scatter_dimension=0, tiled=True),
        lax.psum_scatter(small_terms[3], ("rep", "shard"), scatter_dimension=0, tiled=True),
        lax.psum_scatter(small_terms[4], ("rep", "shard"), scatter_dimension=0, tiled=True),
    )
    grad_gain, grad_shift, grad_packed_b, grad_out_b, grad_up_b = reduced
    return (
        output,
        grad_tokens,
        grad_gain,
        grad_shift,
        grad_qkv_w,
        grad_packed_b,
        grad_dense_w,
        grad_out_b,
        grad_up_w,
        grad_up_b,
        grad_down_w,
        grad_out_b,
    )


MIB = 1024 * 1024


def params(vmem=48):
    return pltpu.CompilerParams(
        dimension_semantics=("arbitrary",), vmem_limit_bytes=vmem * MIB
    )


def cost(flops, moved):
    return pl.CostEstimate(flops=flops, bytes_accessed=moved, transcendentals=0)


def fixed(shape, start=0):
    index = (start,) + (0,) * (len(shape) - 1)
    return pl.BlockSpec(shape, lambda *_: index, pipeline_mode=pl.Buffered(buffer_count=1))


def whole(array):
    return fixed(array.shape)


def rows_of(array, rows, start=0):
    return pl.BlockSpec((rows, array.shape[1]), lambda i, *_: (i + start // rows, 0))


ANYWHERE = pl.BlockSpec(memory_space=pl.ANY)


def kernel(body, scalars, operands, in_specs, out_specs, out_shape, grid=(1,), scratch=(), work=(0, 0)):
    return pl.pallas_call(
        body,
        grid_spec=pltpu.PrefetchScalarGridSpec(
            num_scalar_prefetch=1,
            grid=grid,
            in_specs=in_specs,
            out_specs=out_specs,
            scratch_shapes=list(scratch),
        ),
        out_shape=out_shape,
        compiler_params=params(),
        cost_estimate=cost(*work),
    )(scalars, *operands)


def shaped(shape, dtype=BF16):
    return jax.ShapeDtypeStruct(shape, dtype)


def nn(left_side, right_side):
    return lax.dot_general(
        left_side, right_side, (((1,), (0,)), ((), ())), preferred_element_type=F32
    )


def nt(left_side, right_side):
    return lax.dot_general(
        left_side, right_side, (((1,), (1,)), ((), ())), preferred_element_type=F32
    )


def tn(left_side, right_side):
    return lax.dot_general(
        left_side, right_side, (((0,), (0,)), ((), ())), preferred_element_type=F32
    )


HALF, MIDDLE, ODD, CORE, CHIP = range(5)


def copy_all(copies, sems):
    for at, (source, target) in enumerate(copies):
        pltpu.make_async_copy(source, target, sems.at[at]).start()
    for at, (source, target) in enumerate(copies):
        pltpu.make_async_copy(source, target, sems.at[at]).wait()


def copy_either(where, common, if_middle, if_end, sems):
    @pl.when(where[MIDDLE] == 1)
    def _():
        copy_all(common + if_middle, sems)

    @pl.when(where[MIDDLE] == 0)
    def _():
        copy_all(common + if_end, sems)


def multiple(value, size):
    return pl.multiple_of(value * size, size)


def attention_body(parts, merge, where, *refs):
    if merge:
        hidden, cot, pair, middle_left, middle_right, end_left, end_right = refs[:7]
        bias, cosine, sine_a, sine_b, first = refs[7:12]
        prior = ()
        context, d_packed, *grads = refs[12:18]
        qkv_w, dense_w, sum_qkv, sum_dense, sems = refs[18:]
    else:
        hidden, cot, qkv_w, dense_w, bias, cosine, sine_a, sine_b, first = refs[:9]
        prior = refs[9:13]
        context, d_packed, *grads = refs[13:19]
        sum_qkv, sum_dense = refs[19:]
    step = pl.program_id(0)
    run, wide = hidden.shape[0], dense_w.shape[0]
    scaling = 1.0 / math.sqrt(HEAD_DIM)
    block, own = sum_qkv.shape[0] // 4, wide // 4
    across = dense_w.shape[1] // parts
    left_columns = grads[0].shape[1]

    if merge:

        @pl.when(step == 0)
        def _():
            half = where[HALF]

            def dense_copies(source, side, first_column):
                return [
                    (
                        source.at[
                            i * block + j * own : i * block + (j + 1) * own,
                            first_column : first_column + across,
                        ],
                        dense_w.at[
                            pl.ds(multiple(2 * side + i, own), own), j * across : (j + 1) * across
                        ],
                    )
                    for i in range(2)
                    for j in range(parts)
                ]

            rows, rest = 2 * block, 3 * wide - left_columns

            def others(left, right):
                return [
                    (left, qkv_w.at[rows:, :left_columns]),
                    (right.at[:, :rest], qkv_w.at[rows:, left_columns:]),
                ] + dense_copies(right, 1 - half, rest)

            common = [(pair.at[:, : 3 * wide], qkv_w.at[:rows])]
            common += dense_copies(pair, half, 3 * wide)
            copy_either(
                where, common, others(middle_left, middle_right), others(end_left, end_right), sems
            )

    c = jnp.tile(cosine[...], (1, wide // 128))
    sa = jnp.tile(sine_a[...], (1, wide // 128))
    sb = jnp.tile(sine_b[...], (1, wide // 128))

    def turn(value, sign):
        ahead = pltpu.roll(value, wide - ROT // 2, 1)
        behind = pltpu.roll(value, ROT // 2, 1)
        return value * c + sign * (ahead * sa + behind * sb)

    packed = nn(hidden[...], qkv_w[...]) + bias[...]
    queries = (turn(packed[:, :wide], 1.0).astype(BF16).astype(F32) * scaling).astype(BF16)
    keys = turn(packed[:, wide : 2 * wide], 1.0).astype(BF16)
    values = packed[:, 2 * wide :].astype(BF16)
    d_context = nt(cot[...], dense_w[...]).astype(BF16)
    at = lax.broadcasted_iota(jnp.int32, (run, run), 1)
    row = lax.broadcasted_iota(jnp.int32, (run, run), 0)
    seen = (at >= first[:, :1]) & (at <= row)
    out, d_q, d_k, d_v = [], [], [], []
    for h in range(wide // HEAD_DIM):
        part = slice(h * HEAD_DIM, (h + 1) * HEAD_DIM)
        q, k, v, g = queries[:, part], keys[:, part], values[:, part], d_context[:, part]
        scores = jnp.where(seen, nt(q, k), -1e30)
        raised = jnp.exp(scores - jnp.max(scores, axis=1, keepdims=True))
        probs = raised * (1.0 / jnp.sum(raised, axis=1, keepdims=True))
        low = probs.astype(BF16)
        o = nn(low, v)
        out.append(o)
        d_v.append(tn(low, g))
        delta = jnp.sum(o * g.astype(F32), axis=1, keepdims=True)
        d_scores = (probs * (nt(g, v) - delta)).astype(BF16)
        d_q.append(nn(d_scores, k) * scaling)
        d_k.append(tn(d_scores, q))
    context[...] = jnp.concatenate(out, axis=1).astype(BF16)
    d_packed[:, :wide] = turn(jnp.concatenate(d_q, axis=1), -1.0).astype(BF16)
    d_packed[:, wide : 2 * wide] = turn(jnp.concatenate(d_k, axis=1), -1.0).astype(BF16)
    d_packed[:, 2 * wide :] = jnp.concatenate(d_v, axis=1).astype(BF16)

    @pl.when(step == 0)
    def _():
        sum_qkv[...] = jnp.zeros_like(sum_qkv)
        sum_dense[...] = jnp.zeros_like(sum_dense)

    sum_qkv[...] += tn(hidden[...], d_packed[...])
    sum_dense[...] += tn(context[...], cot[...])

    @pl.when(step == pl.num_programs(0) - 1)
    def _():
        for pair_at in range(2):
            for i in range(2):
                half = where[HALF] if pair_at == 0 else 1 - where[HALF]
                rows = slice(i * block, (i + 1) * block)
                start = (2 * pair_at + i) * block
                summed = sum_qkv[start : start + block]
                beside = sum_dense[pl.ds(multiple(2 * half + i, own), own), :]
                beside = jnp.concatenate(
                    [beside[:, j * across : (j + 1) * across] for j in range(parts)], axis=0
                )
                first_half = summed[:, :left_columns]
                second_half = jnp.concatenate([summed[:, left_columns:], beside], axis=1)
                if prior:
                    first_half += prior[2 * pair_at][rows].astype(F32)
                    second_half += prior[2 * pair_at + 1][rows].astype(F32)
                grads[2 * pair_at][rows] = first_half.astype(BF16)
                grads[2 * pair_at + 1][rows] = second_half.astype(BF16)


def attention(where, run, start, count, parts, hidden, cot, weights, streams, prior):
    width = hidden.shape[1]
    merge = len(weights) == 5
    bias = streams[0]
    wide = bias.shape[1] // 3
    grad = shaped((width // 2, (3 * wide + width // parts) // 2))
    sums = [pltpu.VMEM((width, 3 * wide), F32), pltpu.VMEM((wide, width), F32)]
    joined = [shaped((width, 3 * wide)), shaped((wide, width))] if merge else []
    outs = kernel(
        functools.partial(attention_body, parts, merge),
        where,
        [hidden, cot, *weights, *streams, *prior],
        [rows_of(hidden, run, start), rows_of(cot, run, start)]
        + ([ANYWHERE] * 5 if merge else [whole(array) for array in weights])
        + [whole(bias)]
        + [rows_of(array, run, start) for array in streams[1:]]
        + [whole(array) for array in prior],
        [
            pl.BlockSpec((run, wide), lambda i, _: (i, 0)),
            pl.BlockSpec((run, 3 * wide), lambda i, _: (i, 0)),
        ]
        + [fixed(grad.shape)] * 4
        + [fixed(array.shape) for array in joined],
        [shaped((count, wide)), shaped((count, 3 * wide))] + [grad] * 4 + joined,
        grid=(count // run,),
        scratch=sums + ([pltpu.SemaphoreType.DMA((3 + 4 * parts,))] if merge else []),
        work=(18 * 10**9, 20 * MIB),
    )
    return outs[0], outs[1], outs[2:6], outs[6:]


GELU_A = math.sqrt(2.0 / math.pi)
GELU_B = 0.044715


def write_halves(where, total, grads, order):
    rows, columns = grads[0].shape
    for pair_at in range(2):
        if order:
            half = where[HALF] if pair_at == 0 else 1 - where[HALF]
            part = pl.ds(multiple(half, rows), rows)
        else:
            part = slice(pair_at * rows, (pair_at + 1) * rows)
        for side in range(2):
            grads[2 * pair_at + side][...] = total[
                part, side * columns : (side + 1) * columns
            ].astype(BF16)


def forward_body(
    columns,
    where,
    hidden,
    cot,
    pair,
    middle_left,
    middle_right,
    end_left,
    end_right,
    bias,
    active,
    slope,
    up_w,
    *rest,
):
    grads, total, sems = rest[:-2], rest[-2], rest[-1]
    step = pl.program_id(0)

    @pl.when(step == 0)
    def _():
        rows, middle = pair.shape[0], middle_left.shape[1]

        def others(left, right):
            return [(left, up_w.at[rows:, :middle]), (right, up_w.at[rows:, middle:])]

        copy_either(
            where,
            [(pair, up_w.at[:rows])],
            others(middle_left, middle_right),
            others(end_left, end_right),
            sems,
        )
        total[...] = jnp.zeros_like(total)

    for j in range(up_w.shape[1] // columns):
        part = slice(j * columns, (j + 1) * columns)
        v = nn(hidden[...], up_w[:, part]) + bias[:, part]
        square = v * v
        t = jnp.tanh(GELU_A * v * (1.0 + GELU_B * square))
        gate = 0.5 * (1.0 + t)
        low = (v * gate).astype(BF16)
        active[:, part] = low
        slope[:, part] = (
            gate + 0.5 * v * (1.0 - t * t) * (GELU_A + (3.0 * GELU_A * GELU_B) * square)
        ).astype(BF16)
        total[part] += tn(low, cot[...])

    @pl.when(step == pl.num_programs(0) - 1)
    def _():
        write_halves(where, total, grads, True)


def forward(where, hidden, cot, pieces, bias, rows=512, columns=512):
    count, wide = hidden.shape[0], bias.shape[1]
    width = cot.shape[1]
    grad = shaped((wide // 2, width // 2))
    outs = kernel(
        functools.partial(forward_body, columns),
        where,
        [hidden, cot, *pieces, bias],
        [rows_of(hidden, rows), rows_of(cot, rows)] + [ANYWHERE] * 5 + [whole(bias)],
        [pl.BlockSpec((rows, wide), lambda i, _: (i, 0))] * 2
        + [fixed((width, wide))]
        + [fixed(grad.shape)] * 4,
        [shaped((count, wide))] * 2 + [shaped((width, wide))] + [grad] * 4,
        grid=(count // rows,),
        scratch=[pltpu.VMEM((wide, width), F32), pltpu.SemaphoreType.DMA((3,))],
        work=(4 * hidden.size * wide, 32 * MIB),
    )
    return outs[0], outs[1], outs[2], outs[3:]


def backward_body(
    where,
    cot,
    hidden,
    pair,
    middle_left,
    middle_right,
    end_left,
    end_right,
    slope,
    d_upward,
    sums,
    down_w,
    *rest,
):
    grads, total, sems = rest[:-2], rest[-2], rest[-1]
    step = pl.program_id(0)

    @pl.when(step == 0)
    def _():
        rows, middle = middle_left.shape

        def others(left, right):
            part = pl.ds(multiple(1 - where[HALF], rows), rows)
            return [(left, down_w.at[part, :middle]), (right, down_w.at[part, middle:])]

        copy_either(
            where,
            [(pair, down_w.at[pl.ds(multiple(where[HALF], rows), rows)])],
            others(middle_left, middle_right),
            others(end_left, end_right),
            sems,
        )
        sums[...] = jnp.zeros_like(sums)
        total[...] = jnp.zeros_like(total)

    low = (nt(cot[...], down_w[...]) * slope[...].astype(F32)).astype(BF16)
    d_upward[...] = low
    sums[...] += jnp.sum(low.astype(F32), axis=0, keepdims=True)
    total[...] += tn(hidden[...], low)

    @pl.when(step == pl.num_programs(0) - 1)
    def _():
        write_halves(where, total, grads, False)


def backward(where, cot, hidden, pieces, slope, rows=256):
    count, wide = slope.shape
    width = hidden.shape[1]
    grad = shaped((width // 2, wide // 2))
    outs = kernel(
        backward_body,
        where,
        [cot, hidden, *pieces, slope],
        [rows_of(cot, rows), rows_of(hidden, rows)] + [ANYWHERE] * 5 + [rows_of(slope, rows)],
        [
            pl.BlockSpec((rows, wide), lambda i, _: (i, 0)),
            pl.BlockSpec((1, wide), lambda i, _: (0, 0)),
            fixed((wide, width)),
        ]
        + [fixed(grad.shape)] * 4,
        [shaped((count, wide)), shaped((1, wide), F32), shaped((wide, width))] + [grad] * 4,
        grid=(count // rows,),
        scratch=[pltpu.VMEM((width, wide), F32), pltpu.SemaphoreType.DMA((3,))],
        work=(4 * cot.size * wide, 32 * MIB),
    )
    return outs[0], outs[1], outs[2], outs[3:]


def two_dots_body(dot, a, aw, b, bw, far, near):
    result = (dot(a[...], aw[...]) + dot(b[...], bw[...])).astype(BF16)
    step, half = pl.program_id(0), pl.num_programs(0) // 2

    @pl.when(step < half)
    def _():
        far[...] = result

    @pl.when(step >= half)
    def _():
        near[...] = result


def two_dots(dot, a, aw, b, bw, width, rows=256):
    count = a.shape[0]
    steps = count // rows
    half = steps // 2

    def of(array):
        return pl.BlockSpec((rows, array.shape[1]), lambda i: (lax.rem(i + half, steps), 0))

    shape = jax.ShapeDtypeStruct((count // 2, width), BF16)
    return pl.pallas_call(
        functools.partial(two_dots_body, dot),
        grid=(steps,),
        in_specs=[of(a), whole(aw), of(b), whole(bw)],
        out_specs=[
            pl.BlockSpec((rows, width), lambda i: (jnp.minimum(i, half - 1), 0)),
            pl.BlockSpec((rows, width), lambda i: (jnp.maximum(i - half, 0), 0)),
        ],
        out_shape=[shape, shape],
        compiler_params=params(),
        cost_estimate=cost(
            2 * count * (aw.size + bw.size),
            count * 2 * (width + a.shape[1] + b.shape[1]) + 2 * (aw.size + bw.size),
        ),
    )(a, aw, b, bw)


def deal_first_body(planes, chips, where, up, qkv, keep, send):
    mates, n = CORES * chips, up.shape[0]
    block = up.shape[1] // (planes * mates)
    for core in range(CORES):
        for chip in range(chips):
            i = core * chips + chip
            pieces = [
                up[:, (p * mates + i) * block : (p * mates + i + 1) * block] for p in range(planes)
            ] + [
                qkv[:, (t * mates + i) * HEAD_DIM : (t * mates + i + 1) * HEAD_DIM]
                for t in range(3 * planes)
            ]
            value = jnp.concatenate(pieces, axis=1)

            @pl.when(where[CORE] == core)
            def _():
                keep[chip] = value

            @pl.when(where[CORE] != core)
            def _():
                send[chip] = value


def deal_first(where, planes, chips, up, qkv):
    out = shaped((chips, up.shape[0], (up.shape[1] + qkv.shape[1]) // (CORES * chips)))
    return kernel(
        functools.partial(deal_first_body, planes, chips),
        where,
        [up, qkv],
        [whole(up), whole(qkv)],
        [fixed(out.shape)] * 2,
        [out] * 2,
        work=(0, 4 * MIB),
    )


def deal_second_body(where, keep, came, *outs):
    core = where[CORE]
    for r, out in enumerate(outs):
        at = where[CHIP] ^ r
        out[pl.ds(core, 1)] = keep[pl.ds(at, 1)]
        out[pl.ds(1 - core, 1)] = came[pl.ds(at, 1)]


def deal_second(where, keep, came):
    chips, n, columns = keep.shape
    out = shaped((CORES, n, columns))
    return kernel(
        deal_second_body,
        where,
        [keep, came],
        [whole(keep), whole(came)],
        [fixed(out.shape)] * chips,
        [out] * chips,
        work=(0, 4 * MIB),
    )


def deal_last_body(chips, where, *refs):
    blocks, dense, (u, a) = refs[:chips], refs[chips], refs[chips + 1 :]
    n, columns = blocks[0].shape[1:]
    middle = u.shape[1]
    wide = columns - middle
    for r, block in enumerate(blocks):
        for core in range(CORES):
            rows = pl.ds(multiple(core * chips + (where[CHIP] ^ r), n), n)
            u[rows, :] = block[core, :, :middle]
            a[rows, :wide] = block[core, :, middle:]
    across = a.shape[1] - wide
    for j in range(dense.shape[1] // across):
        a[j * n : (j + 1) * n, wide:] = dense[:, j * across : (j + 1) * across]


def deal_last(where, blocks, dense, middle):
    chips = len(blocks)
    n, columns = blocks[0].shape[1:]
    mates = CORES * chips
    shapes = [
        shaped((mates * n, middle)),
        shaped((mates * n, columns - middle + dense.shape[1] // mates)),
    ]
    return kernel(
        functools.partial(deal_last_body, chips),
        where,
        [*blocks, dense],
        [whole(array) for array in (*blocks, dense)],
        [fixed(shape.shape) for shape in shapes],
        shapes,
        work=(0, 4 * MIB),
    )


def finish_body(chips, wide, where, own_left, own_right, came_left, came_right, left, right, *outs):
    keep, send = outs[:2]
    n, columns = left.shape[0], left.shape[1]
    step = n // (CORES * chips)
    total = jnp.concatenate(
        [
            own[...].astype(F32) + came[...].astype(F32) + last[...].astype(F32)
            for own, came, last in (
                (own_left, came_left, left),
                (own_right, came_right, right),
            )
        ],
        axis=1,
    )
    low = total[:, :wide].astype(BF16)
    for core in range(CORES):

        @pl.when(where[CORE] == core)
        def _():
            for chip in range(chips):
                at = (core * chips + chip) * step
                keep[chip] = low[at : at + step]
                at = ((1 - core) * chips + chip) * step
                send[chip] = low[at : at + step]

    if len(outs) == 3:
        beside = outs[2]
        across = total.shape[1] - wide
        for j in range(n // step):
            beside[:, j * across : (j + 1) * across] = total[j * step : (j + 1) * step, wide:]


def finish(where, chips, wide, own_left, own_right, came_left, came_right, left, right):
    n, columns = left.shape
    mine = pl.BlockSpec((n, columns), lambda i, where: (where[ODD], 0))
    step = n // (CORES * chips)
    shapes = [shaped((chips, step, wide))] * 2
    if wide < 2 * columns:
        shapes.append(shaped((step, (2 * columns - wide) * CORES * chips), F32))
    return kernel(
        functools.partial(finish_body, chips, wide),
        where,
        [own_left, own_right, came_left, came_right, left, right],
        [mine] * 4 + [whole(left), whole(right)],
        [fixed(shape.shape) for shape in shapes],
        shapes,
        work=(0, 4 * MIB),
    )


def back_body(groups, where, *refs):
    blocks, out, held = refs[:-2], refs[-2], refs[-1]
    chips = len(blocks)
    n, columns = blocks[0].shape[1:]
    size = columns // groups
    for r, block in enumerate(blocks):
        held[pl.ds(where[CHIP] ^ r, 1)] = block[...][None]
    for group in range(groups):
        for core in range(CORES):
            start = (group * CORES + core) * chips * size
            out[:, start : start + chips * size] = jnp.concatenate(
                [held[chip, core, :, group * size : (group + 1) * size] for chip in range(chips)],
                axis=1,
            ).astype(F32)


def back(where, blocks, groups):
    chips = len(blocks)
    n, columns = blocks[0].shape[1:]
    out = shaped((n, columns * CORES * chips), F32)
    return kernel(
        functools.partial(back_body, groups),
        where,
        blocks,
        [whole(block) for block in blocks],
        fixed(out.shape),
        out,
        scratch=[pltpu.VMEM((chips,) + blocks[0].shape, BF16)],
        work=(0, 4 * MIB),
    )


def corners_body(where, near_a, near_b, came_a, came_b, first, second):
    first[...] = (near_a[...].astype(F32) + came_a[...].astype(F32)).astype(BF16)
    second[...] = (near_b[...].astype(F32) + came_b[...].astype(F32)).astype(BF16)


def corners(where, near, came):
    rows, width = near.shape[0] // 8, near.shape[1]
    blocks = [fixed((rows, width), 6), fixed((rows, width), 7)]
    return kernel(
        corners_body,
        where,
        [near, near, came, came],
        blocks * 2,
        [fixed((rows, width))] * 2,
        [shaped((rows, width))] * 2,
        work=(0, 4 * MIB),
    )


def sides_body(where, near_x, near_y, came_x, came_y, extra_x, extra_y, for_x, for_y):
    half = extra_x.shape[0]
    x = near_x[...].astype(F32) + came_x[...].astype(F32)
    y = near_y[...].astype(F32) + came_y[...].astype(F32)
    for_x[:half] = x[:half].astype(BF16)
    for_x[half:] = (x[half:] + extra_x[...].astype(F32)).astype(BF16)
    for_y[:half] = (y[:half] + extra_y[...].astype(F32)).astype(BF16)
    for_y[half:] = y[half:].astype(BF16)


def sides(where, near, came, extra_y, extra_x):
    rows, width = near.shape[0] // 4, near.shape[1]
    blocks = [fixed((rows, width), 1), fixed((rows, width), 2)]
    return kernel(
        sides_body,
        where,
        [near, near, came, came, extra_x, extra_y],
        blocks * 2 + [whole(extra_x), whole(extra_y)],
        [fixed((rows, width))] * 2,
        [shaped((rows, width))] * 2,
        work=(0, 8 * MIB),
    )


def norm_back_body(
    where, near, came, by_x, by_y, tokens, cot, gain, grad_tokens, gain_sum, shift_sum
):
    parts = [ref[...].astype(F32) for ref in (near, came, by_x, by_y)]
    turned = parts[0] + parts[1] + parts[2] + parts[3]
    middle = turned.shape[1] // 2
    swap = where[HALF] == 1
    lower, upper = turned[:, :middle], turned[:, middle:]
    d_hidden = jnp.concatenate(
        [jnp.where(swap, upper, lower), jnp.where(swap, lower, upper)], axis=1
    )
    inputs = tokens[...].astype(F32)
    centered = inputs - jnp.mean(inputs, axis=1, keepdims=True)
    inv_std = lax.rsqrt(jnp.mean(centered * centered, axis=1, keepdims=True) + EPSILON)
    normed = centered * inv_std
    d_norm = d_hidden * gain[...]
    d_inputs = inv_std * (
        d_norm
        - jnp.mean(d_norm, axis=1, keepdims=True)
        - normed * jnp.mean(d_norm * normed, axis=1, keepdims=True)
    )
    grad_tokens[...] = (cot[...].astype(F32) + d_inputs).astype(BF16)

    @pl.when(pl.program_id(0) == 0)
    def _():
        gain_sum[...] = jnp.zeros_like(gain_sum)
        shift_sum[...] = jnp.zeros_like(shift_sum)

    gain_sum[...] += jnp.sum(d_hidden * normed, axis=0, keepdims=True)
    shift_sum[...] += jnp.sum(d_hidden, axis=0, keepdims=True)


def norm_back(where, near, came, by_x, by_y, tokens, cot, gain, rows=128):
    count, width = tokens.shape
    block = pl.BlockSpec((rows, width), lambda i, _: (i, 0))
    return kernel(
        norm_back_body,
        where,
        [near, came, by_x, by_y, tokens, cot, gain],
        [block] * 6 + [whole(gain)],
        [block, fixed((1, width)), fixed((1, width))],
        [shaped((count, width)), shaped((1, width), F32), shaped((1, width), F32)],
        grid=(count // rows,),
        work=(0, 8 * MIB),
    )


def tied(*groups):
    return lax.optimization_barrier(groups)


def by_planes(
    planes,
    mates,
    tokens,
    lengths,
    ln_gain,
    ln_bias,
    qkv_weight,
    qkv_bias,
    dense_weight,
    dense_bias,
    up_weight,
    up_bias,
    down_weight,
    down_bias,
    cotangent,
):
    row_count, width = tokens.shape
    owners = planes * mates
    chips = mates // CORES
    rank = lax.axis_index("rep") * chips + lax.axis_index("shard")
    z, m = rank // mates, rank % mates
    c, s = m // chips, m % chips
    middle_plane = jnp.where((z == 1) | (z == 2), 1, 0)
    where = jnp.stack([z // 2, middle_plane, z % 2, c, s]).astype(jnp.int32)
    rows_own = qkv_weight.shape[0]
    ff_block = up_bias.shape[0]
    heads_width = planes * HEAD_DIM
    count = mates * row_count

    def flip(value, r):
        return lax.ppermute(
            value,
            AXES,
            [(p * mates + i, p * mates + (i ^ r)) for p in range(planes) for i in range(mates)],
        )

    def between(value, pairs):
        return lax.ppermute(
            value, AXES, [(p * mates + i, q * mates + i) for p, q in pairs for i in range(mates)]
        )

    def to_neighbour(value):
        return between(value, [(p, p ^ 1) for p in range(planes)])

    def over_middle(value):
        return between(value, [(1, 2), (2, 1)])

    def outwards(value):
        return between(value, [(1, 0), (2, 3)])

    def inwards(value):
        return between(value, [(0, 1), (3, 2)])

    def paired(own, came):
        return jnp.where(
            z % 2 == 0,
            jnp.concatenate([own, came], axis=0),
            jnp.concatenate([came, own], axis=0),
        )

    def added(*terms):
        return sum(term.astype(F32) for term in terms)

    def middle_share(other, came):
        return added(other, came).astype(BF16)

    def neighbour_share(own, came):
        size = own.shape[0] // 2
        lower, upper = [added(own[part], came[part]) for part in (slice(0, size), slice(size, None))]
        return jnp.where(z % 2 == 1, lower, upper).astype(BF16)

    def deal_over_chips(keep, send):
        blocks = deal_second(where, keep, flip(send, chips))
        return [blocks[0]] + [flip(blocks[r], r) for r in range(1, chips)]

    def over_planes(table):
        for r in (1, 2):
            table = table + between(table, [(p, p ^ r) for p in range(planes)])
        return table

    def over_mates(table):
        for r in (1, 2, 4):
            table = table + flip(table, r)
        return table

    def left(value):
        return value[:, : value.shape[1] // 2]

    def right(value):
        return value[:, value.shape[1] // 2 :]

    def turned(value):
        middle = value.shape[1] // 2
        lower, upper, first_half = value[:, :middle], value[:, middle:], z < 2
        return jnp.concatenate(
            [jnp.where(first_half, lower, upper), jnp.where(first_half, upper, lower)], axis=1
        )

    half = row_count // 2

    def near_first(block):
        return flip(block, 1), flip(block, 2)

    def near_second(by_x, by_y):
        return flip(by_y[:half], 1), flip(by_x[half:], 2)

    def most_of(block, by_x, by_y):
        return jnp.concatenate([block, by_x, by_y], axis=0)

    parts = [ln_gain, ln_bias, qkv_bias, dense_bias, up_bias, down_bias, lengths[0].astype(BF16)]
    sizes = [part.shape[0] for part in parts]
    starts = [sum(sizes[:i]) for i in range(len(sizes))]
    own_row = jnp.concatenate(parts)
    own_row = jnp.pad(own_row, (0, -len(own_row) % 128))
    table = jnp.where(jnp.arange(owners)[:, None] == rank, own_row[None, :], 0)
    table, down_own = tied(over_planes(table), down_weight)

    wide = 3 * heads_width
    w1 = to_neighbour(down_own)
    dealt = deal_over_chips(*deal_first(where, planes, chips, up_weight, qkv_weight))
    u_own, a_own = deal_last(where, dealt, dense_weight, planes * ff_block)
    table = over_mates(table).astype(F32)

    def column(i):
        return table[:, starts[i] : starts[i] + sizes[i]].reshape(-1)

    gain, shift_by = column(0), column(1)
    packed_bias = lax.dynamic_index_in_dim(
        column(2).reshape(3, planes, mates, HEAD_DIM), m, 2, keepdims=False
    ).reshape(1, -1)
    upward_bias = lax.dynamic_index_in_dim(
        column(4).reshape(planes, mates, ff_block), m, 1, keepdims=False
    ).reshape(1, -1)
    out_bias = column(3) + column(5)
    all_lengths = table[:, starts[6] : starts[6] + sizes[6]].astype(jnp.int32)
    doc_sizes = jnp.stack(
        [
            lax.dynamic_index_in_dim(all_lengths, z * mates + (m ^ r), 0, keepdims=False)
            for r in range(mates)
        ]
    )

    inputs_f = tokens.astype(F32)
    average = jnp.mean(inputs_f, axis=1, keepdims=True)
    centered = inputs_f - average
    spread = jnp.mean(centered * centered, axis=1, keepdims=True)
    inv_std = lax.rsqrt(spread + EPSILON)
    normed = centered * inv_std
    hidden_own = turned((normed * gain + shift_by).astype(BF16))

    ends_at = jnp.cumsum(doc_sizes, axis=1)
    at = jnp.arange(row_count, dtype=jnp.int32)
    offsets = jnp.max(jnp.where(at[None, :, None] >= ends_at[:, None, :], ends_at[:, None, :], 0), axis=2)
    places = (at[None, :] - offsets).astype(F32).reshape(count, 1)
    lane = jnp.arange(2 * HEAD_DIM, dtype=jnp.int32) % HEAD_DIM
    inverse = jnp.power(jnp.float32(10000.0), -2.0 * (lane % (ROT // 2)).astype(F32) / ROT)
    angles = places * inverse[None, :]
    sine = jnp.sin(angles)
    cosine = jnp.where(lane < ROT, jnp.cos(angles), 1.0)
    sine_a = jnp.where(lane < ROT // 2, -sine, 0.0)
    sine_b = jnp.where((lane >= ROT // 2) & (lane < ROT), sine, 0.0)
    first = jnp.broadcast_to(offsets.reshape(count, 1), (count, 2 * HEAD_DIM))

    w1, u_own, a_own, cot_own = tied(w1, u_own, a_own, cotangent)

    w_pair = paired(down_own, w1)
    u1 = to_neighbour(u_own)
    w2_left = over_middle(left(w_pair))
    cot_near = near_first(cot_own)

    u1, w2_left, cot_near, a_own, hidden_own = tied(u1, w2_left, cot_near, a_own, hidden_own)
    u_pair = paired(u_own, u1)
    u2_left = over_middle(left(u_pair))
    a1 = to_neighbour(a_own)
    hidden_near = near_first(hidden_own)
    cot_most = most_of(cot_own, *cot_near)
    cot_across = flip(cot_most, chips)

    u2_left, a1, hidden_near, cot_across, u_pair, cot_near = tied(
        u2_left, a1, hidden_near, cot_across, u_pair, cot_near
    )
    a_pair = paired(a_own, a1)
    u3_left = outwards(u2_left)
    u2_right = over_middle(right(u_pair))
    corner_y = flip(jnp.concatenate([cot_near[1][:half], hidden_near[1][:half]], axis=0), 1)
    corner_x = flip(jnp.concatenate([cot_near[0][half:], hidden_near[0][half:]], axis=0), 2)
    hidden_most = most_of(hidden_own, *hidden_near)
    hidden_across = flip(hidden_most, chips)

    u3_left, u2_right, corner_x, corner_y, a_pair, hidden_across = tied(
        u3_left, u2_right, corner_x, corner_y, a_pair, hidden_across
    )
    u3_right = outwards(u2_right)
    a2_left = over_middle(left(a_pair))
    corner = jnp.concatenate([corner_y, corner_x], axis=0)
    corner_across = flip(corner, chips)

    def all_rows(most, across, at):
        pieces = [most]
        for corners_of in (corner, corner_across):
            pieces += [corners_of[at : at + half], corners_of[at + 2 * half : at + 3 * half]]
        return jnp.concatenate(pieces[:3] + [across] + pieces[3:], axis=0)

    cot, hidden = all_rows(cot_most, cot_across, 0), all_rows(hidden_most, hidden_across, half)
    u3_right, a2_left, a_pair, hidden, cot = tied(u3_right, a2_left, a_pair, hidden, cot)
    a3_left = outwards(a2_left)
    a2_right = over_middle(right(a_pair))
    active, slope, up_w, g_w = forward(
        where, hidden, cot, [u_pair, u2_left, u2_right, u3_left, u3_right], upward_bias
    )

    a3_left, a2_right, g_w, w_pair, cosine, sine_a, sine_b, first = tied(
        a3_left, a2_right, g_w, w_pair, cosine, sine_a, sine_b, first
    )
    a3_right = outwards(a2_right)
    w2_right = over_middle(right(w_pair))
    q1_w_left = inwards(g_w[2])

    a3_right, w2_right, q1_w_left, w2_left, g_w, hidden = tied(
        a3_right, w2_right, q1_w_left, w2_left, g_w, hidden
    )
    w3_left = outwards(w2_left)
    q1_w_right = inwards(g_w[3])
    q2_w_left = over_middle(middle_share(g_w[2], q1_w_left))
    streams = [packed_bias, cosine, sine_a, sine_b, first]
    context_a, d_packed_a, g_a, (qkv_w, dense_w) = attention(
        where,
        row_count,
        0,
        count // 2,
        mates,
        hidden,
        cot,
        [a_pair, a2_left, a2_right, a3_left, a3_right],
        streams,
        [],
    )

    w3_left, q1_w_right, q2_w_left, w2_right, g_a, hidden, g_w = tied(
        w3_left, q1_w_right, q2_w_left, w2_right, g_a, hidden, g_w
    )
    w3_right = outwards(w2_right)
    q2_w_right = over_middle(middle_share(g_w[3], q1_w_right))
    q3_w_left = to_neighbour(neighbour_share(g_w[0], q2_w_left))
    context_b, d_packed_b, g_a, _ = attention(
        where,
        row_count,
        count // 2,
        count // 2,
        mates,
        hidden,
        cot,
        [qkv_w, dense_w],
        streams,
        g_a,
    )

    w3_right, q2_w_right, q3_w_left, g_a, cot, slope, g_w = tied(
        w3_right, q2_w_right, q3_w_left, g_a, cot, slope, g_w
    )
    q1_a_left = inwards(g_a[2])
    q3_w_right = to_neighbour(neighbour_share(g_w[1], q2_w_right))
    d_upward, upward_sum, down_w, g_u = backward(
        where, cot, hidden, [w_pair, w2_left, w2_right, w3_left, w3_right], slope
    )

    q1_a_left, q3_w_right, q3_w_left, g_u, d_upward, g_a = tied(
        q1_a_left, q3_w_right, q3_w_left, g_u, d_upward, g_a
    )
    q1_a_right = inwards(g_a[3])
    q2_a_left = over_middle(middle_share(g_a[2], q1_a_left))
    context = jnp.concatenate([context_a, context_b], axis=0)
    d_packed = jnp.concatenate([d_packed_a, d_packed_b], axis=0)
    d_hidden_far, d_hidden_near = two_dots(nt, d_packed, qkv_w, d_upward, up_w, width)

    q1_a_right, q2_a_left, d_hidden_far, d_hidden_near, g_u, g_a, context = tied(
        q1_a_right, q2_a_left, d_hidden_far, d_hidden_near, g_u, g_a, context
    )
    d_hidden_came = flip(d_hidden_far, chips)
    q1_u_left = inwards(g_u[2])
    q2_a_right = over_middle(middle_share(g_a[3], q1_a_right))
    q3_a_left = to_neighbour(neighbour_share(g_a[0], q2_a_left))
    out_far, out_near = two_dots(nn, context, dense_w, active, down_w, width)
    own_down = jnp.concatenate([added(*both) for both in zip(g_w[:2], (q2_w_left, q2_w_right))], axis=1)
    grad_down_w = lax.dynamic_slice_in_dim(
        own_down, (z % 2) * ff_block, ff_block, 0
    ) + jnp.concatenate([q3_w_left, q3_w_right], axis=1).astype(F32)

    q1_u_left, q2_a_right, q3_a_left, d_hidden_came, out_far, out_near, g_u, g_a = tied(
        q1_u_left, q2_a_right, q3_a_left, d_hidden_came, out_far, out_near, g_u, g_a
    )
    out_came = flip(out_far, chips)
    corner_a, corner_b = corners(where, d_hidden_near, d_hidden_came)
    extra_y, extra_x = flip(corner_a, 1), flip(corner_b, 2)
    for_x, for_y = sides(where, d_hidden_near, d_hidden_came, extra_y, extra_x)
    d_hidden_last = flip(for_x, 1), flip(for_y, 2)
    q1_u_right = inwards(g_u[3])
    q2_u_left = over_middle(middle_share(g_u[2], q1_u_left))
    q3_a_right = to_neighbour(neighbour_share(g_a[1], q2_a_right))

    q1_u_right, q2_u_left, q3_a_right, d_hidden_last, out_came, g_u, q3_a_left = tied(
        q1_u_right, q2_u_left, q3_a_right, d_hidden_last, out_came, g_u, q3_a_left
    )
    corner_a, corner_b = corners(where, out_near, out_came)
    extra_y, extra_x = flip(corner_a, 1), flip(corner_b, 2)
    for_x, for_y = sides(where, out_near, out_came, extra_y, extra_x)
    out_last = flip(for_x, 1), flip(for_y, 2)
    q2_u_right = over_middle(middle_share(g_u[3], q1_u_right))
    q3_u_left = to_neighbour(neighbour_share(g_u[0], q2_u_left))
    grad_tokens, gain_sum, shift_sum = norm_back(
        where,
        d_hidden_near,
        d_hidden_came,
        *d_hidden_last,
        tokens,
        cotangent,
        gain.reshape(1, -1),
    )
    keep, send, grad_dense_w = finish(
        where, chips, wide, g_a[0], g_a[1], q2_a_left, q2_a_right, q3_a_left, q3_a_right
    )
    blocks = deal_second(where, keep, flip(send, chips))

    q2_u_right, q3_u_left, out_last, blocks, grad_tokens, gain_sum, g_u = tied(
        q2_u_right, q3_u_left, out_last, blocks, grad_tokens, gain_sum, g_u
    )
    q3_u_right = to_neighbour(neighbour_share(g_u[1], q2_u_right))
    blocks = [blocks[0]] + [flip(blocks[r], r) for r in range(1, chips)]
    output = added(out_near[:row_count], out_came[:row_count], *out_last)
    output = (inputs_f + output + out_bias).astype(BF16)

    q3_u_right, blocks = tied(q3_u_right, blocks)
    keep, send = finish(
        where,
        chips,
        planes * ff_block,
        g_u[0],
        g_u[1],
        q2_u_left,
        q2_u_right,
        q3_u_left,
        q3_u_right,
    )
    grad_up_w = back(where, deal_over_chips(keep, send), planes)
    grad_qkv_w = back(where, blocks, 3 * planes)

    mine = jnp.arange(mates) == m
    packed_sum = jnp.sum(d_packed.astype(F32), axis=0).reshape(3, planes, 1, HEAD_DIM)
    packed_sum = jnp.where(mine[None, None, :, None], packed_sum, 0.0)
    upward_sum = upward_sum.reshape(planes, 1, ff_block)
    upward_sum = jnp.where(mine[None, :, None], upward_sum, 0.0)
    sums = jnp.concatenate(
        [
            gain_sum.reshape(owners, -1),
            shift_sum.reshape(owners, -1),
            jnp.sum(cotangent.astype(F32), axis=0).reshape(owners, -1),
            packed_sum.reshape(owners, -1),
            upward_sum.reshape(owners, -1),
        ],
        axis=1,
    )
    total = lax.dynamic_index_in_dim(over_mates(over_planes(sums)), rank, 0, keepdims=False)
    grad_gain, grad_shift, grad_out_b, grad_packed_b, grad_up_b = jnp.split(
        total,
        [
            sizes[0],
            sizes[0] + sizes[1],
            sizes[0] + sizes[1] + sizes[3],
            sizes[0] + sizes[1] + sizes[3] + sizes[2],
        ],
    )

    return (
        output,
        grad_tokens,
        grad_gain,
        grad_shift,
        grad_qkv_w,
        grad_packed_b,
        grad_dense_w,
        grad_out_b,
        grad_up_w,
        grad_up_b,
        grad_down_w,
        grad_out_b,
    )


def solution(mesh):
    planes, mates = mesh.shape["rep"] // CORES, CORES * mesh.shape["shard"]
    rows, vector = P(AXES, None), P(AXES)

    def layer(*arrays):
        width = arrays[0].shape[1]
        if mesh.shape["shard"] == 4 and planes * mates * HEAD_DIM == width:
            return by_planes(planes, mates, *arrays)
        return gathered_whole(*arrays)

    return jax.shard_map(
        layer,
        mesh=mesh,
        in_specs=(
            rows, rows, vector, vector, rows, vector, rows, vector, rows, vector, rows, vector, rows,
        ),
        out_specs=(
            rows, rows, vector, vector, rows, vector, rows, vector, rows, vector, rows, vector,
        ),
        check_vma=False,
    )
```

```python
import functools
import math

import jax
import jax.numpy as jnp
from jax import lax
from jax.experimental import pallas as pl
from jax.experimental.pallas import tpu as pltpu
from jax.sharding import PartitionSpec as P

HEADS = 32
HEAD_DIM = 64
ROT = 32
CORES = 2
AXES = ("rep", "shard")
BF16 = jnp.bfloat16
F32 = jnp.float32


EPSILON = 1e-05


def positions(doc_sizes, row_count):
    ends_at = jnp.cumsum(doc_sizes)
    starts_at = ends_at - doc_sizes
    indices = jnp.arange(row_count, dtype=jnp.int32)
    doc_ids = jnp.sum((indices[:, None] >= ends_at[None, :]).astype(jnp.int32), axis=1)
    member = doc_ids[:, None] == jnp.arange(doc_sizes.shape[0], dtype=jnp.int32)[None, :]
    offsets = jnp.sum(jnp.where(member, starts_at[None, :], 0), axis=1)
    places = (indices - offsets).astype(jnp.float32)
    allowed = (doc_ids[:, None] == doc_ids[None, :]) & (indices[None, :] <= indices[:, None])
    return (places, allowed)


def rotary(places):
    indices = jnp.arange(ROT // 2, dtype=jnp.float32)
    inverse = jnp.power(jnp.float32(10000.0), -2.0 * indices / ROT)
    angles = places[:, None] * inverse[None, :]
    return (jnp.cos(angles)[:, None, :], jnp.sin(angles)[:, None, :])


def rotate(values, cosine, sine):
    lower_half = values[..., : ROT // 2]
    upper_half = values[..., ROT // 2 : ROT]
    return jnp.concatenate(
        [
            lower_half * cosine - upper_half * sine,
            upper_half * cosine + lower_half * sine,
            values[..., ROT:],
        ],
        axis=-1,
    )


def unrotate(incoming, cosine, sine):
    lower_half = incoming[..., : ROT // 2]
    upper_half = incoming[..., ROT // 2 : ROT]
    return jnp.concatenate(
        [
            lower_half * cosine + upper_half * sine,
            upper_half * cosine - lower_half * sine,
            incoming[..., ROT:],
        ],
        axis=-1,
    )


def project(weight, left_side):
    whole = lax.all_gather(weight, ("rep", "shard"), axis=0, tiled=True)
    return jnp.dot(left_side, whole, preferred_element_type=jnp.float32)


def back_project(weight, incoming):
    whole = lax.all_gather(weight, ("rep", "shard"), axis=0, tiled=True)
    return lax.dot_general(
        incoming, whole, (((1,), (1,)), ((), ())), preferred_element_type=jnp.float32
    )


def weight_grad(left_side, incoming):
    return lax.psum_scatter(
        lax.dot_general(
            left_side, incoming, (((0,), (0,)), ((), ())), preferred_element_type=jnp.float32
        ),
        ("rep", "shard"),
        scatter_dimension=0,
        tiled=True,
    )


def gathered_whole(
    tokens,
    lengths,
    ln_gain,
    ln_bias,
    qkv_weight,
    qkv_bias,
    dense_weight,
    dense_bias,
    up_weight,
    up_bias,
    down_weight,
    down_bias,
    cotangent,
):
    row_count = tokens.shape[0]
    width = tokens.shape[1]
    small = (
        lax.all_gather(ln_gain, ("rep", "shard"), axis=0, tiled=True),
        lax.all_gather(ln_bias, ("rep", "shard"), axis=0, tiled=True),
        lax.all_gather(qkv_bias, ("rep", "shard"), axis=0, tiled=True),
        lax.all_gather(dense_bias, ("rep", "shard"), axis=0, tiled=True),
        lax.all_gather(up_bias, ("rep", "shard"), axis=0, tiled=True),
        lax.all_gather(down_bias, ("rep", "shard"), axis=0, tiled=True),
    )
    gain, shift, packed_bias, dense_shift, upward_bias, downward_bias = [
        tensor.astype(jnp.float32) for tensor in small
    ]
    places, allowed = positions(lengths[0], row_count)
    cosine, sine = rotary(places)
    scaling = 1.0 / math.sqrt(HEAD_DIM)
    inputs_f = tokens.astype(jnp.float32)
    average = jnp.mean(inputs_f, axis=1, keepdims=True)
    centered = inputs_f - average
    spread = jnp.mean(centered * centered, axis=1, keepdims=True)
    inv_std = lax.rsqrt(spread + EPSILON)
    normed = centered * inv_std
    hidden_low = (normed * gain + shift).astype(jnp.bfloat16)
    packed = (project(qkv_weight, hidden_low) + packed_bias).reshape(row_count, 3, HEADS, HEAD_DIM)
    queries = rotate(packed[:, 0], cosine, sine).astype(jnp.bfloat16)
    keys_rot = rotate(packed[:, 1], cosine, sine).astype(jnp.bfloat16)
    values_low = packed[:, 2].astype(jnp.bfloat16)
    scores = scaling * jnp.einsum(
        "qhd,khd->hqk", queries, keys_rot, preferred_element_type=jnp.float32
    )
    scores = jnp.where(allowed[None], scores, -1e30)
    maximum = jnp.max(scores, axis=-1, keepdims=True)
    raised = jnp.exp(scores - maximum)
    totals = jnp.sum(raised, axis=-1, keepdims=True)
    probs = raised / totals
    log_total = maximum + jnp.log(totals)
    context = jnp.einsum(
        "hqk,khd->qhd", probs.astype(jnp.bfloat16), values_low, preferred_element_type=jnp.float32
    )
    context_low = context.reshape(row_count, width).astype(jnp.bfloat16)
    attended = project(dense_weight, context_low) + dense_shift
    upward = project(up_weight, hidden_low) + upward_bias
    active_low = jax.nn.gelu(upward, approximate=True).astype(jnp.bfloat16)
    downward = project(down_weight, active_low) + downward_bias
    output = (inputs_f + attended + downward).astype(jnp.bfloat16)
    grad_out = cotangent.astype(jnp.float32)
    d_active = back_project(down_weight, cotangent)
    gelu_value, gelu_pull = jax.vjp(lambda inner: jax.nn.gelu(inner, approximate=True), upward)
    d_upward_low = gelu_pull(d_active)[0].astype(jnp.bfloat16)
    d_context_low = (
        back_project(dense_weight, cotangent)
        .astype(jnp.bfloat16)
        .reshape(row_count, HEADS, HEAD_DIM)
    )
    again = scaling * jnp.einsum(
        "qhd,khd->hqk", queries, keys_rot, preferred_element_type=jnp.float32
    )
    again = jnp.where(allowed[None], again, -1e30)
    probs_again = jnp.exp(again - log_total)
    d_values = jnp.einsum(
        "hqk,qhd->khd",
        probs_again.astype(jnp.bfloat16),
        d_context_low,
        preferred_element_type=jnp.float32,
    )
    d_probs = jnp.einsum(
        "qhd,khd->hqk", d_context_low, values_low, preferred_element_type=jnp.float32
    )
    d_scores = probs_again * (d_probs - jnp.sum(d_probs * probs_again, axis=-1, keepdims=True))
    d_scores_low = d_scores.astype(jnp.bfloat16)
    d_queries = scaling * jnp.einsum(
        "hqk,khd->qhd", d_scores_low, keys_rot, preferred_element_type=jnp.float32
    )
    d_keys = scaling * jnp.einsum(
        "hqk,qhd->khd", d_scores_low, queries, preferred_element_type=jnp.float32
    )
    d_packed = jnp.stack(
        [unrotate(d_queries, cosine, sine), unrotate(d_keys, cosine, sine), d_values], axis=1
    )
    d_packed_low = d_packed.reshape(row_count, 3 * width).astype(jnp.bfloat16)
    d_hidden = back_project(qkv_weight, d_packed_low) + back_project(up_weight, d_upward_low)
    d_norm = d_hidden * gain
    d_inputs = inv_std * (
        d_norm
        - jnp.mean(d_norm, axis=1, keepdims=True)
        - normed * jnp.mean(d_norm * normed, axis=1, keepdims=True)
    )
    grad_tokens = (grad_out + d_inputs).astype(jnp.bfloat16)
    grad_qkv_w = weight_grad(hidden_low, d_packed_low)
    grad_dense_w = weight_grad(context_low, cotangent)
    grad_up_w = weight_grad(hidden_low, d_upward_low)
    grad_down_w = weight_grad(active_low, cotangent)
    small_terms = (
        jnp.sum(d_hidden * normed, axis=0),
        jnp.sum(d_hidden, axis=0),
        jnp.sum(d_packed_low.astype(jnp.float32), axis=0),
        jnp.sum(grad_out, axis=0),
        jnp.sum(d_upward_low.astype(jnp.float32), axis=0),
    )
    reduced = (
        lax.psum_scatter(small_terms[0], ("rep", "shard"), scatter_dimension=0, tiled=True),
        lax.psum_scatter(small_terms[1], ("rep", "shard"), scatter_dimension=0, tiled=True),
        lax.psum_scatter(small_terms[2], ("rep", "shard"), scatter_dimension=0, tiled=True),
        lax.psum_scatter(small_terms[3], ("rep", "shard"), scatter_dimension=0, tiled=True),
        lax.psum_scatter(small_terms[4], ("rep", "shard"), scatter_dimension=0, tiled=True),
    )
    grad_gain, grad_shift, grad_packed_b, grad_out_b, grad_up_b = reduced
    return (
        output,
        grad_tokens,
        grad_gain,
        grad_shift,
        grad_qkv_w,
        grad_packed_b,
        grad_dense_w,
        grad_out_b,
        grad_up_w,
        grad_up_b,
        grad_down_w,
        grad_out_b,
    )


MIB = 1024 * 1024
VMEM = 60


def params(vmem=VMEM):
    return pltpu.CompilerParams(
        dimension_semantics=("arbitrary",), vmem_limit_bytes=vmem * MIB
    )


def cost(flops, moved):
    return pl.CostEstimate(flops=flops, bytes_accessed=moved, transcendentals=0)


def fixed(shape, start=0):
    index = (start,) + (0,) * (len(shape) - 1)
    return pl.BlockSpec(shape, lambda *_: index, pipeline_mode=pl.Buffered(buffer_count=1))


def whole(array):
    return fixed(array.shape)


def rows_of(array, rows, start=0):
    return pl.BlockSpec((rows, array.shape[1]), lambda i, *_: (i + start // rows, 0))


ANYWHERE = pl.BlockSpec(memory_space=pl.ANY)


def kernel(body, scalars, operands, in_specs, out_specs, out_shape, grid=(1,), scratch=(), work=(0, 0), vmem=16):
    return pl.pallas_call(
        body,
        grid_spec=pltpu.PrefetchScalarGridSpec(
            num_scalar_prefetch=1,
            grid=grid,
            in_specs=in_specs,
            out_specs=out_specs,
            scratch_shapes=list(scratch),
        ),
        out_shape=out_shape,
        compiler_params=params(vmem),
        cost_estimate=cost(*work),
    )(scalars, *operands)


def shaped(shape, dtype=BF16):
    return jax.ShapeDtypeStruct(shape, dtype)


def nn(left_side, right_side):
    return lax.dot_general(
        left_side, right_side, (((1,), (0,)), ((), ())), preferred_element_type=F32
    )


def nt(left_side, right_side):
    return lax.dot_general(
        left_side, right_side, (((1,), (1,)), ((), ())), preferred_element_type=F32
    )


def tn(left_side, right_side):
    return lax.dot_general(
        left_side, right_side, (((0,), (0,)), ((), ())), preferred_element_type=F32
    )


HALF, MIDDLE, ODD, CORE, CHIP = range(5)


def copy_all(copies, sems):
    for at, (source, target) in enumerate(copies):
        pltpu.make_async_copy(source, target, sems.at[at]).start()
    for at, (source, target) in enumerate(copies):
        pltpu.make_async_copy(source, target, sems.at[at]).wait()


def places(where):
    half, odd = where[HALF], where[ODD]
    return (
        (odd, 2 * half + odd),
        (1 - odd, 2 * half + 1 - odd),
        (2 + half, 2 - half),
        (3 - half, 3 - 3 * half),
    )


def copy_pieces(where, pieces, of, sems):
    own, neighbour, other_middle, other_end = places(where)
    common = of(pieces[0], *own) + of(pieces[1], *neighbour)

    @pl.when(where[MIDDLE] == 1)
    def _():
        copy_all(common + of(pieces[2], *other_middle) + of(pieces[3], *other_end), sems)

    @pl.when(where[MIDDLE] == 0)
    def _():
        copy_all(common + of(pieces[4], *other_middle) + of(pieces[5], *other_end), sems)


def multiple(value, size):
    return pl.multiple_of(value * size, size)


def attention_body(parts, run, merge, where, *refs):
    hidden, cot, *refs = refs
    weights, refs = refs[: 6 if merge else 2], refs[6 if merge else 2 :]
    (bias, cosine, sine_a, sine_b, first), refs = refs[:5], refs[5:]
    prior, refs = ((), refs) if merge else (refs[:4], refs[6:])
    (context, d_packed, *grads), refs = refs[:6], refs[6:]
    if merge:
        qkv_w, dense_w, sum_qkv, sum_dense, sems = refs
    else:
        (qkv_w, dense_w), (sum_qkv, sum_dense) = weights, refs
    step = pl.program_id(0)
    wide = dense_w.shape[0]
    scaling = 1.0 / math.sqrt(HEAD_DIM)
    block, own = sum_qkv.shape[0] // 4, wide // 4
    across = dense_w.shape[1] // parts

    if merge:

        @pl.when(step == 0)
        def _():
            def of(piece, place, plane):
                return [
                    (piece.at[:, : 3 * wide], qkv_w.at[pl.ds(multiple(place, block), block)])
                ] + [
                    (
                        piece.at[j * own : (j + 1) * own, 3 * wide :],
                        dense_w.at[
                            pl.ds(multiple(plane, own), own), j * across : (j + 1) * across
                        ],
                    )
                    for j in range(parts)
                ]

            copy_pieces(where, weights, of, sems)

    c = jnp.tile(cosine[...], (1, wide // 128))
    sa = jnp.tile(sine_a[...], (1, wide // 128))
    sb = jnp.tile(sine_b[...], (1, wide // 128))

    def turn(value, sign):
        ahead = pltpu.roll(value, wide - ROT // 2, 1)
        behind = pltpu.roll(value, ROT // 2, 1)
        return value * c + sign * (ahead * sa + behind * sb)

    packed = nn(hidden[...], qkv_w[...]) + bias[...]
    queries = (turn(packed[:, :wide], 1.0).astype(BF16).astype(F32) * scaling).astype(BF16)
    keys = turn(packed[:, wide : 2 * wide], 1.0).astype(BF16)
    values = packed[:, 2 * wide :].astype(BF16)
    d_context = nt(cot[...], dense_w[...]).astype(BF16)
    at = lax.broadcasted_iota(jnp.int32, (run, run), 1)
    row = lax.broadcasted_iota(jnp.int32, (run, run), 0)
    all_out, all_q, all_k, all_v = [], [], [], []
    for begin in range(0, hidden.shape[0], run):
        rows = slice(begin, begin + run)
        seen = (at >= first[rows, :1]) & (at <= row)
        out, d_q, d_k, d_v = [], [], [], []
        for h in range(wide // HEAD_DIM):
            part = slice(h * HEAD_DIM, (h + 1) * HEAD_DIM)
            q, k, v, g = (x[rows, part] for x in (queries, keys, values, d_context))
            scores = jnp.where(seen, nt(q, k), -1e30)
            raised = jnp.exp(scores - jnp.max(scores, axis=1, keepdims=True))
            probs = raised * (1.0 / jnp.sum(raised, axis=1, keepdims=True))
            low = probs.astype(BF16)
            o = nn(low, v)
            out.append(o)
            d_v.append(tn(low, g))
            delta = jnp.sum(o * g.astype(F32), axis=1, keepdims=True)
            d_scores = (probs * (nt(g, v) - delta)).astype(BF16)
            d_q.append(nn(d_scores, k) * scaling)
            d_k.append(tn(d_scores, q))
        for held, new in ((all_out, out), (all_q, d_q), (all_k, d_k), (all_v, d_v)):
            held.append(jnp.concatenate(new, axis=1))
    context[...] = jnp.concatenate(all_out, axis=0).astype(BF16)
    d_packed[:, :wide] = turn(jnp.concatenate(all_q, axis=0), -1.0).astype(BF16)
    d_packed[:, wide : 2 * wide] = turn(jnp.concatenate(all_k, axis=0), -1.0).astype(BF16)
    d_packed[:, 2 * wide :] = jnp.concatenate(all_v, axis=0).astype(BF16)

    @pl.when(step == 0)
    def _():
        sum_qkv[...] = jnp.zeros_like(sum_qkv)
        sum_dense[...] = jnp.zeros_like(sum_dense)

    sum_qkv[...] += tn(hidden[...], d_packed[...])
    sum_dense[...] += tn(context[...], cot[...])

    @pl.when(step == pl.num_programs(0) - 1)
    def _():
        for at, (out, (place, plane)) in enumerate(zip(grads, places(where))):
            summed = sum_qkv[pl.ds(multiple(place, block), block), :]
            beside = sum_dense[pl.ds(multiple(plane, own), own), :]
            beside = jnp.concatenate(
                [beside[:, j * across : (j + 1) * across] for j in range(parts)], axis=0
            )
            total = jnp.concatenate([summed, beside], axis=1)
            if prior:
                total += prior[at][...].astype(F32)
            out[...] = total.astype(BF16)


def attention(where, run, parts, hidden, cot, weights, streams, prior, filled):
    count, width = 2 * hidden.shape[0], hidden.shape[1]
    merge = not prior
    bias = streams[0]
    wide = bias.shape[1] // 3
    rows = run
    steps = count // rows // 2
    start = 0 if merge else steps
    grad = shaped((width // 4, 3 * wide + width // parts))

    def rows_of_run(columns):
        return pl.BlockSpec((rows, columns), lambda i, _: (i + start, 0))

    joined = [shaped((width, 3 * wide)), shaped((wide, width))] if merge else []
    operands = [hidden, cot, *weights, *streams, *prior, *filled]
    first_filled = 1 + len(operands) - len(filled)
    outs = pl.pallas_call(
        functools.partial(attention_body, parts, run, merge),
        grid_spec=pltpu.PrefetchScalarGridSpec(
            num_scalar_prefetch=1,
            grid=(steps,),
            in_specs=[pl.BlockSpec((rows, width), lambda i, _: (i, 0))] * 2
            + ([ANYWHERE] * 6 if merge else [whole(array) for array in weights])
            + [whole(bias)]
            + [rows_of_run(array.shape[1]) for array in streams[1:]]
            + [whole(array) for array in prior]
            + [ANYWHERE for _ in filled],
            out_specs=[rows_of_run(wide), rows_of_run(3 * wide)]
            + [fixed(grad.shape)] * 4
            + [fixed(array.shape) for array in joined],
            scratch_shapes=[pltpu.VMEM((width, 3 * wide), F32), pltpu.VMEM((wide, width), F32)]
            + ([pltpu.SemaphoreType.DMA((4 * (1 + parts),))] if merge else []),
        ),
        out_shape=[shaped((count, wide)), shaped((count, 3 * wide))] + [grad] * 4 + joined,
        input_output_aliases={first_filled + i: i for i in range(len(filled))},
        compiler_params=params(),
        cost_estimate=cost(18 * 10**9, 20 * MIB),
    )(where, *operands)
    return outs[:2], outs[2:6], outs[6:]


GELU_A = math.sqrt(2.0 / math.pi)
GELU_B = 0.044715


def write_blocks(where, total, grads, by_plane):
    size = grads[0].shape[0]
    for out, (place, plane) in zip(grads, places(where)):
        at = multiple(plane if by_plane else place, size)
        out[...] = total[pl.ds(at, size), :].astype(BF16)


def forward_body(columns, where, hidden, cot, *refs):
    pieces, (bias, active, slope, up_w), (*grads, total, sems) = refs[:6], refs[6:10], refs[10:]
    step = pl.program_id(0)

    @pl.when(step == 0)
    def _():
        size = pieces[0].shape[0]

        def of(piece, place, plane):
            return [(piece, up_w.at[pl.ds(multiple(place, size), size)])]

        copy_pieces(where, pieces, of, sems)
        total[...] = jnp.zeros_like(total)

    for j in range(up_w.shape[1] // columns):
        part = slice(j * columns, (j + 1) * columns)
        v = nn(hidden[...], up_w[:, part]) + bias[:, part]
        square = v * v
        t = jnp.tanh(GELU_A * v * (1.0 + GELU_B * square))
        gate = 0.5 * (1.0 + t)
        low = (v * gate).astype(BF16)
        active[:, part] = low
        slope[:, part] = (
            gate + 0.5 * v * (1.0 - t * t) * (GELU_A + (3.0 * GELU_A * GELU_B) * square)
        ).astype(BF16)
        total[part] += tn(low, cot[...])

    @pl.when(step == pl.num_programs(0) - 1)
    def _():
        write_blocks(where, total, grads, True)


def forward(where, hidden, cot, pieces, bias, rows=512, columns=512):
    count, wide = hidden.shape[0], bias.shape[1]
    width = cot.shape[1]
    grad = shaped((wide // 4, width))
    outs = kernel(
        functools.partial(forward_body, columns),
        where,
        [hidden, cot, *pieces, bias],
        [rows_of(hidden, rows), rows_of(cot, rows)] + [ANYWHERE] * 6 + [whole(bias)],
        [pl.BlockSpec((rows, wide), lambda i, _: (i, 0))] * 2
        + [fixed((width, wide))]
        + [fixed(grad.shape)] * 4,
        [shaped((count, wide))] * 2 + [shaped((width, wide))] + [grad] * 4,
        grid=(count // rows,),
        scratch=[pltpu.VMEM((wide, width), F32), pltpu.SemaphoreType.DMA((4,))],
        work=(4 * count * width * wide, 32 * MIB),
        vmem=VMEM,
    )
    return outs[0], outs[1], outs[2], outs[3:]


def backward_body(where, cot, hidden, *refs):
    pieces, (slope, d_upward, sums, down_w), (*grads, total, sems) = refs[:6], refs[6:10], refs[10:]
    step = pl.program_id(0)

    @pl.when(step == 0)
    def _():
        size = pieces[0].shape[0]

        def of(piece, place, plane):
            return [(piece, down_w.at[pl.ds(multiple(plane, size), size)])]

        copy_pieces(where, pieces, of, sems)
        sums[...] = jnp.zeros_like(sums)
        total[...] = jnp.zeros_like(total)

    low = (nt(cot[...], down_w[...]) * slope[...].astype(F32)).astype(BF16)
    d_upward[...] = low
    sums[...] += jnp.sum(low.astype(F32), axis=0, keepdims=True)
    total[...] += tn(hidden[...], low)

    @pl.when(step == pl.num_programs(0) - 1)
    def _():
        write_blocks(where, total, grads, False)


def backward(where, cot, hidden, pieces, slope, rows=256):
    count, wide = slope.shape
    width = hidden.shape[1]
    grad = shaped((width // 4, wide))
    outs = kernel(
        backward_body,
        where,
        [cot, hidden, *pieces, slope],
        [rows_of(cot, rows), rows_of(hidden, rows)] + [ANYWHERE] * 6 + [rows_of(slope, rows)],
        [
            pl.BlockSpec((rows, wide), lambda i, _: (i, 0)),
            pl.BlockSpec((1, wide), lambda i, _: (0, 0)),
            fixed((wide, width)),
        ]
        + [fixed(grad.shape)] * 4,
        [shaped((count, wide)), shaped((1, wide), F32), shaped((wide, width))] + [grad] * 4,
        grid=(count // rows,),
        scratch=[pltpu.VMEM((width, wide), F32), pltpu.SemaphoreType.DMA((4,))],
        work=(4 * count * width * wide, 32 * MIB),
        vmem=VMEM,
    )
    return outs[0], outs[1], outs[2], outs[3:]


def two_dots_body(dot, a, aw, b, bw, far, near):
    result = (dot(a[...], aw[...]) + dot(b[...], bw[...])).astype(BF16)
    step, half = pl.program_id(0), pl.num_programs(0) // 2

    @pl.when(step < half)
    def _():
        far[...] = result

    @pl.when(step >= half)
    def _():
        near[...] = result


def two_dots(dot, a, aw, b, bw, width, rows=256):
    count = a.shape[0]
    steps = count // rows
    half = steps // 2

    def of(array):
        return pl.BlockSpec((rows, array.shape[1]), lambda i: (lax.rem(i + half, steps), 0))

    shape = jax.ShapeDtypeStruct((count // 2, width), BF16)
    return pl.pallas_call(
        functools.partial(two_dots_body, dot),
        grid=(steps,),
        in_specs=[of(a), whole(aw), of(b), whole(bw)],
        out_specs=[
            pl.BlockSpec((rows, width), lambda i: (jnp.minimum(i, half - 1), 0)),
            pl.BlockSpec((rows, width), lambda i: (jnp.maximum(i - half, 0), 0)),
        ],
        out_shape=[shape, shape],
        compiler_params=params(),
        cost_estimate=cost(
            2 * count * (aw.size + bw.size),
            count * 2 * (width + a.shape[1] + b.shape[1]) + 2 * (aw.size + bw.size),
        ),
    )(a, aw, b, bw)


def deal_first_body(planes, chips, where, up, qkv, keep, send):
    mates, n = CORES * chips, up.shape[0]
    block = up.shape[1] // (planes * mates)
    for core in range(CORES):
        for chip in range(chips):
            i = core * chips + chip
            pieces = [
                up[:, (p * mates + i) * block : (p * mates + i + 1) * block] for p in range(planes)
            ] + [
                qkv[:, (t * mates + i) * HEAD_DIM : (t * mates + i + 1) * HEAD_DIM]
                for t in range(3 * planes)
            ]
            value = jnp.concatenate(pieces, axis=1)

            @pl.when(where[CORE] == core)
            def _():
                keep[chip] = value

            @pl.when(where[CORE] != core)
            def _():
                send[chip] = value


def deal_first(where, planes, chips, up, qkv):
    out = shaped((chips, up.shape[0], (up.shape[1] + qkv.shape[1]) // (CORES * chips)))
    return kernel(
        functools.partial(deal_first_body, planes, chips),
        where,
        [up, qkv],
        [whole(up), whole(qkv)],
        [fixed(out.shape)] * 2,
        [out] * 2,
        work=(0, 4 * MIB),
    )


def deal_second_body(where, keep, came, *outs):
    core = where[CORE]
    for r, out in enumerate(outs):
        at = where[CHIP] ^ r
        out[pl.ds(core, 1)] = keep[pl.ds(at, 1)]
        out[pl.ds(1 - core, 1)] = came[pl.ds(at, 1)]


def deal_second(where, keep, came):
    chips, n, columns = keep.shape
    out = shaped((CORES, n, columns))
    return kernel(
        deal_second_body,
        where,
        [keep, came],
        [whole(keep), whole(came)],
        [fixed(out.shape)] * chips,
        [out] * chips,
        work=(0, 4 * MIB),
    )


def deal_last_body(chips, where, *refs):
    blocks, dense, (u, a) = refs[:chips], refs[chips], refs[chips + 1 :]
    n, columns = blocks[0].shape[1:]
    middle = u.shape[1]
    wide = columns - middle
    for r, block in enumerate(blocks):
        for core in range(CORES):
            rows = pl.ds(multiple(core * chips + (where[CHIP] ^ r), n), n)
            u[rows, :] = block[core, :, :middle]
            a[rows, :wide] = block[core, :, middle:]
    across = a.shape[1] - wide
    for j in range(dense.shape[1] // across):
        a[j * n : (j + 1) * n, wide:] = dense[:, j * across : (j + 1) * across]


def deal_last(where, blocks, dense, middle):
    chips = len(blocks)
    n, columns = blocks[0].shape[1:]
    mates = CORES * chips
    shapes = [
        shaped((mates * n, middle)),
        shaped((mates * n, columns - middle + dense.shape[1] // mates)),
    ]
    return kernel(
        functools.partial(deal_last_body, chips),
        where,
        [*blocks, dense],
        [whole(array) for array in (*blocks, dense)],
        [fixed(shape.shape) for shape in shapes],
        shapes,
        work=(0, 4 * MIB),
    )


def finish_body(chips, wide, where, own, middle, last, *outs):
    keep, send = outs[:2]
    n = own.shape[0]
    step = n // (CORES * chips)
    total = own[...].astype(F32) + middle[...].astype(F32) + last[...].astype(F32)
    low = total[:, :wide].astype(BF16)
    for core in range(CORES):

        @pl.when(where[CORE] == core)
        def _():
            for chip in range(chips):
                at = (core * chips + chip) * step
                keep[chip] = low[at : at + step]
                at = ((1 - core) * chips + chip) * step
                send[chip] = low[at : at + step]

    if len(outs) == 3:
        beside = outs[2]
        across = total.shape[1] - wide
        for j in range(n // step):
            beside[:, j * across : (j + 1) * across] = total[j * step : (j + 1) * step, wide:]


def finish(where, chips, wide, own, middle, last):
    n, columns = own.shape
    step = n // (CORES * chips)
    shapes = [shaped((chips, step, wide))] * 2
    if wide < columns:
        shapes.append(shaped((step, (columns - wide) * CORES * chips), F32))
    return kernel(
        functools.partial(finish_body, chips, wide),
        where,
        [own, middle, last],
        [whole(own)] * 3,
        [fixed(shape.shape) for shape in shapes],
        shapes,
        work=(0, 4 * MIB),
    )


def back_body(groups, where, *refs):
    blocks, out, held = refs[:-2], refs[-2], refs[-1]
    chips = len(blocks)
    n, columns = blocks[0].shape[1:]
    size = columns // groups
    for r, block in enumerate(blocks):
        held[pl.ds(where[CHIP] ^ r, 1)] = block[...][None]
    for group in range(groups):
        for core in range(CORES):
            start = (group * CORES + core) * chips * size
            out[:, start : start + chips * size] = jnp.concatenate(
                [held[chip, core, :, group * size : (group + 1) * size] for chip in range(chips)],
                axis=1,
            ).astype(F32)


def back(where, blocks, groups):
    chips = len(blocks)
    n, columns = blocks[0].shape[1:]
    out = shaped((n, columns * CORES * chips), F32)
    return kernel(
        functools.partial(back_body, groups),
        where,
        blocks,
        [whole(block) for block in blocks],
        fixed(out.shape),
        out,
        scratch=[pltpu.VMEM((chips,) + blocks[0].shape, BF16)],
        work=(0, 4 * MIB),
    )


def corners_body(where, *refs):
    sources, outs = refs[:-2], refs[-2:]
    for at in range(len(sources) // 4):
        for i, out in enumerate(outs):
            near, came = sources[4 * at + 2 * i], sources[4 * at + 2 * i + 1]
            rows = near.shape[0]
            total = near[...].astype(F32) + came[...].astype(F32)
            out[at * rows : (at + 1) * rows] = total.astype(BF16)


def corners(where, *sums):
    rows, width = sums[0][0].shape[0] // 8, sums[0][0].shape[1]
    out = shaped((len(sums) * rows, width))
    return kernel(
        corners_body,
        where,
        [term for terms in sums for _ in range(2) for term in terms],
        [fixed((rows, width), 6 + i) for _ in sums for i in range(2) for _ in range(2)],
        [fixed(out.shape)] * 2,
        [out] * 2,
        work=(0, 4 * MIB),
    )


def pair_halves_body(where, *refs):
    sources, outs = refs[:-2], refs[-2:]
    for at in range(len(sources) // 2):
        for i, out in enumerate(outs):
            rows = sources[0].shape[0]
            out[at * rows : (at + 1) * rows] = sources[2 * at + i][...]


def pair_halves(where, *pairs):
    rows, width = pairs[0][0].shape[0] // 2, pairs[0][0].shape[1]
    out = shaped((len(pairs) * rows, width))
    return kernel(
        pair_halves_body,
        where,
        [array for by_x, by_y in pairs for array in (by_y, by_x)],
        [fixed((rows, width), i) for _ in pairs for i in range(2)],
        [fixed(out.shape)] * 2,
        [out] * 2,
        work=(0, 4 * MIB),
    )


def sides_body(where, near_x, near_y, came_x, came_y, extra_x, extra_y, for_x, for_y):
    half = extra_x.shape[0]
    x = near_x[...].astype(F32) + came_x[...].astype(F32)
    y = near_y[...].astype(F32) + came_y[...].astype(F32)
    for_x[:half] = x[:half].astype(BF16)
    for_x[half:] = (x[half:] + extra_x[...].astype(F32)).astype(BF16)
    for_y[:half] = (y[:half] + extra_y[...].astype(F32)).astype(BF16)
    for_y[half:] = y[half:].astype(BF16)


def sides(where, near, came, extra_y, extra_x, at):
    rows, width = near.shape[0] // 4, near.shape[1]
    blocks = [fixed((rows, width), 1), fixed((rows, width), 2)]
    return kernel(
        sides_body,
        where,
        [near, near, came, came, extra_x, extra_y],
        blocks * 2 + [fixed((rows // 2, width), at)] * 2,
        [fixed((rows, width))] * 2,
        [shaped((rows, width))] * 2,
        work=(0, 8 * MIB),
    )


def norm_back_body(
    where, near, came, by_x, by_y, tokens, cot, gain, grad_tokens, gain_sum, shift_sum
):
    parts = [ref[...].astype(F32) for ref in (near, came, by_x, by_y)]
    turned = parts[0] + parts[1] + parts[2] + parts[3]
    middle = turned.shape[1] // 2
    swap = where[HALF] == 1
    lower, upper = turned[:, :middle], turned[:, middle:]
    d_hidden = jnp.concatenate(
        [jnp.where(swap, upper, lower), jnp.where(swap, lower, upper)], axis=1
    )
    inputs = tokens[...].astype(F32)
    centered = inputs - jnp.mean(inputs, axis=1, keepdims=True)
    inv_std = lax.rsqrt(jnp.mean(centered * centered, axis=1, keepdims=True) + EPSILON)
    normed = centered * inv_std
    d_norm = d_hidden * gain[...]
    d_inputs = inv_std * (
        d_norm
        - jnp.mean(d_norm, axis=1, keepdims=True)
        - normed * jnp.mean(d_norm * normed, axis=1, keepdims=True)
    )
    grad_tokens[...] = (cot[...].astype(F32) + d_inputs).astype(BF16)

    @pl.when(pl.program_id(0) == 0)
    def _():
        gain_sum[...] = jnp.zeros_like(gain_sum)
        shift_sum[...] = jnp.zeros_like(shift_sum)

    gain_sum[...] += jnp.sum(d_hidden * normed, axis=0, keepdims=True)
    shift_sum[...] += jnp.sum(d_hidden, axis=0, keepdims=True)


def norm_back(where, near, came, by_x, by_y, tokens, cot, gain, rows=128):
    count, width = tokens.shape
    block = pl.BlockSpec((rows, width), lambda i, _: (i, 0))
    return kernel(
        norm_back_body,
        where,
        [near, came, by_x, by_y, tokens, cot, gain],
        [block] * 6 + [whole(gain)],
        [block, fixed((1, width)), fixed((1, width))],
        [shaped((count, width)), shaped((1, width), F32), shaped((1, width), F32)],
        grid=(count // rows,),
        work=(0, 8 * MIB),
    )


def tied(*groups):
    return lax.optimization_barrier(groups)


def by_planes(
    planes,
    mates,
    tokens,
    lengths,
    ln_gain,
    ln_bias,
    qkv_weight,
    qkv_bias,
    dense_weight,
    dense_bias,
    up_weight,
    up_bias,
    down_weight,
    down_bias,
    cotangent,
):
    row_count, width = tokens.shape
    owners = planes * mates
    chips = mates // CORES
    rank = lax.axis_index("rep") * chips + lax.axis_index("shard")
    z, m = rank // mates, rank % mates
    c, s = m // chips, m % chips
    middle_plane = jnp.where((z == 1) | (z == 2), 1, 0)
    where = jnp.stack([z // 2, middle_plane, z % 2, c, s]).astype(jnp.int32)
    rows_own = qkv_weight.shape[0]
    ff_block = up_bias.shape[0]
    heads_width = planes * HEAD_DIM
    count = mates * row_count

    def flip(value, r):
        return lax.ppermute(
            value,
            AXES,
            [(p * mates + i, p * mates + (i ^ r)) for p in range(planes) for i in range(mates)],
        )

    def between(value, pairs):
        return lax.ppermute(
            value, AXES, [(p * mates + i, q * mates + i) for p, q in pairs for i in range(mates)]
        )

    def to_neighbour(value):
        return between(value, [(p, p ^ 1) for p in range(planes)])

    def over_middle(value):
        return between(value, [(1, 2), (2, 1)])

    def outwards(value):
        return between(value, [(1, 0), (2, 3)])

    def inwards(value):
        return between(value, [(0, 1), (3, 2)])

    def added(*terms):
        return sum(term.astype(F32) for term in terms)

    def add(*terms, dtype=BF16):
        return added(*terms).astype(dtype)

    def deal_over_chips(keep, send):
        blocks = deal_second(where, keep, flip(send, chips))
        return [blocks[0]] + [flip(blocks[r], r) for r in range(1, chips)]

    def over_planes(table):
        return table + sum(
            between(table, [(p, (p + r) % planes) for p in range(planes)])
            for r in range(1, planes)
        )

    def over_chips(table):
        return table + sum(flip(table, r) for r in range(1, chips))

    def over_chips_in_turn(table):
        for r in (1, 2):
            table = table + flip(table, r)
        return table

    def over_cores(table):
        return table + flip(table, chips)

    def turned(value):
        middle = value.shape[1] // 2
        lower, upper, first_half = value[:, :middle], value[:, middle:], z < 2
        return jnp.concatenate(
            [jnp.where(first_half, lower, upper), jnp.where(first_half, upper, lower)], axis=1
        )

    half = row_count // 2

    def near_first(block):
        return flip(block, 1), flip(block, 2)

    parts = [ln_gain, ln_bias, qkv_bias, dense_bias, up_bias, down_bias, lengths[0].astype(BF16)]
    sizes = [part.shape[0] for part in parts]
    starts = [sum(sizes[:i]) for i in range(len(sizes))]
    own_row = jnp.concatenate(parts)
    own_row = jnp.pad(own_row, (0, -len(own_row) % 128))
    first_pieces = deal_first(where, planes, chips, up_weight, qkv_weight)
    table = jnp.where(jnp.arange(owners)[:, None] == rank, own_row[None, :], 0)
    wide = 3 * heads_width
    keep, send = first_pieces
    table = over_planes(table)
    blocks, table, down_own = tied(deal_second(where, keep, flip(send, chips)), table, down_weight)
    dealt = [blocks[0]] + [flip(blocks[r], r) for r in range(1, chips)]
    w1, w2a = to_neighbour(down_own), over_middle(down_own)
    table = over_cores(over_chips(table))
    u_own, a_own = deal_last(where, dealt, dense_weight, planes * ff_block)
    u_own, a_own, table, w1, w2a, cot_own = tied(
        u_own, a_own, table, w1, w2a, cotangent
    )
    table = table.astype(F32)

    a1, a2a = to_neighbour(a_own), over_middle(a_own)
    cot_near = near_first(cot_own)

    def column(i):
        return table[:, starts[i] : starts[i] + sizes[i]].reshape(-1)

    gain, shift_by = column(0), column(1)
    packed_bias = lax.dynamic_index_in_dim(
        column(2).reshape(3, planes, mates, HEAD_DIM), m, 2, keepdims=False
    ).reshape(1, -1)
    upward_bias = lax.dynamic_index_in_dim(
        column(4).reshape(planes, mates, ff_block), m, 1, keepdims=False
    ).reshape(1, -1)
    out_bias = column(3) + column(5)
    all_lengths = table[:, starts[6] : starts[6] + sizes[6]].astype(jnp.int32)
    doc_sizes = jnp.stack(
        [
            lax.dynamic_index_in_dim(all_lengths, z * mates + (m ^ r), 0, keepdims=False)
            for r in range(mates)
        ]
    )

    inputs_f = tokens.astype(F32)
    average = jnp.mean(inputs_f, axis=1, keepdims=True)
    centered = inputs_f - average
    spread = jnp.mean(centered * centered, axis=1, keepdims=True)
    inv_std = lax.rsqrt(spread + EPSILON)
    normed = centered * inv_std
    hidden_own = turned((normed * gain + shift_by).astype(BF16))

    ends_at = jnp.cumsum(doc_sizes, axis=1)
    at = jnp.arange(row_count, dtype=jnp.int32)
    offsets = jnp.max(jnp.where(at[None, :, None] >= ends_at[:, None, :], ends_at[:, None, :], 0), axis=2)
    places = (at[None, :] - offsets).astype(F32).reshape(count, 1)
    lane = jnp.arange(2 * HEAD_DIM, dtype=jnp.int32) % HEAD_DIM
    inverse = jnp.power(jnp.float32(10000.0), -2.0 * (lane % (ROT // 2)).astype(F32) / ROT)
    angles = places * inverse[None, :]
    sine = jnp.sin(angles)
    cosine = jnp.where(lane < ROT, jnp.cos(angles), 1.0)
    sine_a = jnp.where(lane < ROT // 2, -sine, 0.0)
    sine_b = jnp.where((lane >= ROT // 2) & (lane < ROT), sine, 0.0)
    first = jnp.broadcast_to(offsets.reshape(count, 1), (count, 2 * HEAD_DIM))

    a1, a2a, cot_near, hidden_own, u_own = tied(a1, a2a, cot_near, hidden_own, u_own)
    a3a, a2b = outwards(a2a), over_middle(a1)
    hidden_near = near_first(hidden_own)

    a3a, a2b, hidden_near, cot_near, u_own = tied(a3a, a2b, hidden_near, cot_near, u_own)
    a3b, u2a = outwards(a2b), over_middle(u_own)
    for_x, for_y = pair_halves(where, cot_near, hidden_near)
    corner_y, corner_x = flip(for_x, 1), flip(for_y, 2)
    cot_most = jnp.concatenate([cot_own, *cot_near], axis=0)
    hidden_most = jnp.concatenate([hidden_own, *hidden_near], axis=0)

    a3b, u2a, corner_x, corner_y, hidden_most, cot_most, u_own, w1, cosine, sine_a, sine_b, first = tied(
        a3b, u2a, corner_x, corner_y, hidden_most, cot_most, u_own, w1, cosine, sine_a, sine_b, first
    )
    u1, w2b = to_neighbour(u_own), over_middle(w1)
    cot = jnp.concatenate([cot_most, corner_y[:half], corner_x[:half]], axis=0)
    hidden = jnp.concatenate([hidden_most, corner_y[half:], corner_x[half:]], axis=0)
    hidden, cot = [hidden, flip(hidden, chips)], [cot, flip(cot, chips)]
    streams = [packed_bias, cosine, sine_a, sine_b, first]
    rows_a, g_a, (qkv_w, dense_w) = attention(
        where,
        row_count,
        mates,
        hidden[0],
        cot[0],
        [a_own, a1, a2a, a2b, a3a, a3b],
        streams,
        [],
        [],
    )

    u1, w2b, u2a, rows_a, g_a, hidden, cot = tied(u1, w2b, u2a, rows_a, g_a, hidden, cot)
    u3a, u2b = outwards(u2a), over_middle(u1)
    (context, d_packed), g_a, _ = attention(
        where, row_count, mates, hidden[1], cot[1], [qkv_w, dense_w], streams, g_a, rows_a
    )

    u3a, u2b, g_a, w2a, d_packed, hidden, cot = tied(u3a, u2b, g_a, w2a, d_packed, hidden, cot)
    u3b, q1_a_end = outwards(u2b), inwards(g_a[3])
    hidden, cot = jnp.concatenate(hidden, axis=0), jnp.concatenate(cot, axis=0)
    mine = jnp.arange(mates) == m
    packed_sum = jnp.sum(d_packed.astype(F32), axis=0).reshape(3, planes, 1, HEAD_DIM)
    packed_sum = jnp.where(mine[None, None, :, None], packed_sum, 0.0).reshape(owners, -1)
    cot_sum = jnp.sum(cotangent.astype(F32), axis=0).reshape(owners, -1)

    u3b, q1_a_end, g_a, w2a, hidden, cot, packed_sum, cot_sum = tied(
        u3b, q1_a_end, g_a, w2a, hidden, cot, packed_sum, cot_sum
    )
    w3a, q1_a_mid, q2_a_end = outwards(w2a), inwards(g_a[2]), over_middle(add(g_a[3], q1_a_end))
    active, slope, up_w, g_w = forward(
        where, hidden, cot, [u_own, u1, u2a, u2b, u3a, u3b], upward_bias
    )

    w3a, q1_a_mid, q2_a_end, g_a, g_w, w2b = tied(w3a, q1_a_mid, q2_a_end, g_a, g_w, w2b)
    w3b, q1_w_end, q2_a_mid = outwards(w2b), inwards(g_w[3]), over_middle(add(g_a[2], q1_a_mid))

    w3b, q1_w_end, q2_a_mid, q2_a_end, g_a, g_w, cot = tied(
        w3b, q1_w_end, q2_a_mid, q2_a_end, g_a, g_w, cot
    )
    q3_a, q2_w_end = to_neighbour(add(g_a[1], q2_a_end)), over_middle(add(g_w[3], q1_w_end))
    d_upward, upward_sum, down_w, g_u = backward(
        where, cot, hidden, [down_own, w1, w2a, w2b, w3a, w3b], slope
    )

    q3_a, q2_w_end, g_w, g_u, d_upward, q2_a_mid, upward_sum = tied(
        q3_a, q2_w_end, g_w, g_u, d_upward, q2_a_mid, upward_sum
    )
    q1_u_end = inwards(g_u[3])
    d_hidden_far, d_hidden_near = two_dots(nt, d_packed, qkv_w, d_upward, up_w, width)
    upward_sum = upward_sum.reshape(planes, 1, ff_block)
    upward_sum = jnp.where(mine[None, :, None], upward_sum, 0.0).reshape(owners, -1)
    keep, send, grad_dense_w = finish(where, chips, wide, g_a[0], q2_a_mid, q3_a)
    came = flip(send, chips)

    q1_u_end, d_hidden_far, d_hidden_near, g_u, g_w, context, upward_sum, keep, came = tied(
        q1_u_end, d_hidden_far, d_hidden_near, g_u, g_w, context, upward_sum, keep, came
    )
    q1_u_mid, q2_u_end = inwards(g_u[2]), over_middle(add(g_u[3], q1_u_end))
    d_hidden_came = flip(d_hidden_far, chips)
    out_far, out_near = two_dots(nn, context, dense_w, active, down_w, width)
    corner_y, corner_x = corners(where, (d_hidden_near, d_hidden_came))
    extra_y, extra_x = flip(corner_y, 1), flip(corner_x, 2)

    q1_u_mid, q2_u_end, extra_x, extra_y, out_far, out_near, g_u, g_w, keep = tied(
        q1_u_mid, q2_u_end, extra_x, extra_y, out_far, out_near, g_u, g_w, keep
    )
    q3_u, q2_u_mid = to_neighbour(add(g_u[1], q2_u_end)), over_middle(add(g_u[2], q1_u_mid))
    out_came = flip(out_far, chips)
    corner_y, corner_x = corners(where, (out_near, out_came))
    out_extra_y, out_extra_x = flip(corner_y, 1), flip(corner_x, 2)
    blocks = deal_second(where, keep, came)

    q3_u, q2_u_mid, out_extra_x, out_extra_y, g_u, g_w, blocks = tied(
        q3_u, q2_u_mid, out_extra_x, out_extra_y, g_u, g_w, blocks
    )
    q1_w_mid = inwards(g_w[2])
    for_x, for_y = sides(where, d_hidden_near, d_hidden_came, extra_y, extra_x, 0)
    d_hidden_last = flip(for_x, 1), flip(for_y, 2)
    block_x, block_y, block_xy = [flip(blocks[r], r) for r in range(1, chips)]
    for_x, for_y = sides(where, out_near, out_came, out_extra_y, out_extra_x, 0)
    keep, send = finish(where, chips, planes * ff_block, g_u[0], q2_u_mid, q3_u)

    (
        q1_w_mid,
        q2_w_end,
        d_hidden_last,
        for_x,
        for_y,
        g_w,
        block_x,
        block_y,
        block_xy,
        keep,
        send,
    ) = tied(
        q1_w_mid,
        q2_w_end,
        d_hidden_last,
        for_x,
        for_y,
        g_w,
        block_x,
        block_y,
        block_xy,
        keep,
        send,
    )
    q3_w, q2_w_mid = to_neighbour(add(g_w[1], q2_w_end)), over_middle(add(g_w[2], q1_w_mid))
    out_last = flip(for_x, 1), flip(for_y, 2)
    held = deal_second(where, keep, flip(send, chips))
    grad_tokens, gain_sum, shift_sum = norm_back(
        where,
        d_hidden_near,
        d_hidden_came,
        *d_hidden_last,
        tokens,
        cotangent,
        gain.reshape(1, -1),
    )
    sums = jnp.concatenate(
        [
            gain_sum.reshape(owners, -1),
            shift_sum.reshape(owners, -1),
            cot_sum,
            packed_sum,
            upward_sum,
        ],
        axis=1,
    )

    q3_w, q2_w_mid, g_w, out_last, sums, held = tied(q3_w, q2_w_mid, g_w, out_last, sums, held)
    received = [flip(held[r], r) for r in range(1, chips)]
    for r in (1, 2):
        sums = sums + between(sums, [(p, p ^ r) for p in range(planes)])
    grad_qkv_w = back(where, [blocks[0], block_x, block_y, block_xy], 3 * planes)
    output = added(out_near[:row_count], out_came[:row_count], *out_last)
    output = (inputs_f + output + out_bias).astype(BF16)
    grad_down_w = add(g_w[0], q2_w_mid, q3_w, dtype=F32)
    received, sums, grad_qkv_w, output, grad_down_w = tied(
        received, sums, grad_qkv_w, output, grad_down_w
    )
    sums = over_cores(over_chips(sums))
    grad_up_w = back(where, [held[0]] + received, planes)
    total = lax.dynamic_index_in_dim(sums, rank, 0, keepdims=False)
    grad_gain, grad_shift, grad_out_b, grad_packed_b, grad_up_b = jnp.split(
        total,
        [
            sizes[0],
            sizes[0] + sizes[1],
            sizes[0] + sizes[1] + sizes[3],
            sizes[0] + sizes[1] + sizes[3] + sizes[2],
        ],
    )
    return (
        output,
        grad_tokens,
        grad_gain,
        grad_shift,
        grad_qkv_w,
        grad_packed_b,
        grad_dense_w,
        grad_out_b,
        grad_up_w,
        grad_up_b,
        grad_down_w,
        grad_out_b,
    )


def solution(mesh):
    planes, mates = mesh.shape["rep"] // CORES, CORES * mesh.shape["shard"]
    rows, vector = P(AXES, None), P(AXES)

    def layer(*arrays):
        width = arrays[0].shape[1]
        if mesh.shape["shard"] == 4 and planes * mates * HEAD_DIM == width:
            return by_planes(planes, mates, *arrays)
        return gathered_whole(*arrays)

    return jax.shard_map(
        layer,
        mesh=mesh,
        in_specs=(
            rows, rows, vector, vector, rows, vector, rows, vector, rows, vector, rows, vector, rows,
        ),
        out_specs=(
            rows, rows, vector, vector, rows, vector, rows, vector, rows, vector, rows, vector,
        ),
        check_vma=False,
    )
```

```python
import functools
import math

import jax
import jax.numpy as jnp
from jax import lax
from jax.experimental import pallas as pl
from jax.experimental.pallas import tpu as pltpu
from jax.sharding import PartitionSpec as P

HEADS = 32
HEAD_DIM = 64
ROT = 32
CORES = 2
AXES = ("rep", "shard")
BF16 = jnp.bfloat16
F32 = jnp.float32


EPSILON = 1e-05


def positions(doc_sizes, row_count):
    ends_at = jnp.cumsum(doc_sizes)
    starts_at = ends_at - doc_sizes
    indices = jnp.arange(row_count, dtype=jnp.int32)
    doc_ids = jnp.sum((indices[:, None] >= ends_at[None, :]).astype(jnp.int32), axis=1)
    member = doc_ids[:, None] == jnp.arange(doc_sizes.shape[0], dtype=jnp.int32)[None, :]
    offsets = jnp.sum(jnp.where(member, starts_at[None, :], 0), axis=1)
    places = (indices - offsets).astype(jnp.float32)
    allowed = (doc_ids[:, None] == doc_ids[None, :]) & (indices[None, :] <= indices[:, None])
    return (places, allowed)


def rotary(places):
    indices = jnp.arange(ROT // 2, dtype=jnp.float32)
    inverse = jnp.power(jnp.float32(10000.0), -2.0 * indices / ROT)
    angles = places[:, None] * inverse[None, :]
    return (jnp.cos(angles)[:, None, :], jnp.sin(angles)[:, None, :])


def rotate(values, cosine, sine):
    lower_half = values[..., : ROT // 2]
    upper_half = values[..., ROT // 2 : ROT]
    return jnp.concatenate(
        [
            lower_half * cosine - upper_half * sine,
            upper_half * cosine + lower_half * sine,
            values[..., ROT:],
        ],
        axis=-1,
    )


def unrotate(incoming, cosine, sine):
    lower_half = incoming[..., : ROT // 2]
    upper_half = incoming[..., ROT // 2 : ROT]
    return jnp.concatenate(
        [
            lower_half * cosine + upper_half * sine,
            upper_half * cosine - lower_half * sine,
            incoming[..., ROT:],
        ],
        axis=-1,
    )


def project(weight, left_side):
    whole = lax.all_gather(weight, ("rep", "shard"), axis=0, tiled=True)
    return jnp.dot(left_side, whole, preferred_element_type=jnp.float32)


def back_project(weight, incoming):
    whole = lax.all_gather(weight, ("rep", "shard"), axis=0, tiled=True)
    return lax.dot_general(
        incoming, whole, (((1,), (1,)), ((), ())), preferred_element_type=jnp.float32
    )


def weight_grad(left_side, incoming):
    return lax.psum_scatter(
        lax.dot_general(
            left_side, incoming, (((0,), (0,)), ((), ())), preferred_element_type=jnp.float32
        ),
        ("rep", "shard"),
        scatter_dimension=0,
        tiled=True,
    )


def gathered_whole(
    tokens,
    lengths,
    ln_gain,
    ln_bias,
    qkv_weight,
    qkv_bias,
    dense_weight,
    dense_bias,
    up_weight,
    up_bias,
    down_weight,
    down_bias,
    cotangent,
):
    row_count = tokens.shape[0]
    width = tokens.shape[1]
    small = (
        lax.all_gather(ln_gain, ("rep", "shard"), axis=0, tiled=True),
        lax.all_gather(ln_bias, ("rep", "shard"), axis=0, tiled=True),
        lax.all_gather(qkv_bias, ("rep", "shard"), axis=0, tiled=True),
        lax.all_gather(dense_bias, ("rep", "shard"), axis=0, tiled=True),
        lax.all_gather(up_bias, ("rep", "shard"), axis=0, tiled=True),
        lax.all_gather(down_bias, ("rep", "shard"), axis=0, tiled=True),
    )
    gain, shift, packed_bias, dense_shift, upward_bias, downward_bias = [
        tensor.astype(jnp.float32) for tensor in small
    ]
    places, allowed = positions(lengths[0], row_count)
    cosine, sine = rotary(places)
    scaling = 1.0 / math.sqrt(HEAD_DIM)
    inputs_f = tokens.astype(jnp.float32)
    average = jnp.mean(inputs_f, axis=1, keepdims=True)
    centered = inputs_f - average
    spread = jnp.mean(centered * centered, axis=1, keepdims=True)
    inv_std = lax.rsqrt(spread + EPSILON)
    normed = centered * inv_std
    hidden_low = (normed * gain + shift).astype(jnp.bfloat16)
    packed = (project(qkv_weight, hidden_low) + packed_bias).reshape(row_count, 3, HEADS, HEAD_DIM)
    queries = rotate(packed[:, 0], cosine, sine).astype(jnp.bfloat16)
    keys_rot = rotate(packed[:, 1], cosine, sine).astype(jnp.bfloat16)
    values_low = packed[:, 2].astype(jnp.bfloat16)
    scores = scaling * jnp.einsum(
        "qhd,khd->hqk", queries, keys_rot, preferred_element_type=jnp.float32
    )
    scores = jnp.where(allowed[None], scores, -1e30)
    maximum = jnp.max(scores, axis=-1, keepdims=True)
    raised = jnp.exp(scores - maximum)
    totals = jnp.sum(raised, axis=-1, keepdims=True)
    probs = raised / totals
    log_total = maximum + jnp.log(totals)
    context = jnp.einsum(
        "hqk,khd->qhd", probs.astype(jnp.bfloat16), values_low, preferred_element_type=jnp.float32
    )
    context_low = context.reshape(row_count, width).astype(jnp.bfloat16)
    attended = project(dense_weight, context_low) + dense_shift
    upward = project(up_weight, hidden_low) + upward_bias
    active_low = jax.nn.gelu(upward, approximate=True).astype(jnp.bfloat16)
    downward = project(down_weight, active_low) + downward_bias
    output = (inputs_f + attended + downward).astype(jnp.bfloat16)
    grad_out = cotangent.astype(jnp.float32)
    d_active = back_project(down_weight, cotangent)
    gelu_value, gelu_pull = jax.vjp(lambda inner: jax.nn.gelu(inner, approximate=True), upward)
    d_upward_low = gelu_pull(d_active)[0].astype(jnp.bfloat16)
    d_context_low = (
        back_project(dense_weight, cotangent)
        .astype(jnp.bfloat16)
        .reshape(row_count, HEADS, HEAD_DIM)
    )
    again = scaling * jnp.einsum(
        "qhd,khd->hqk", queries, keys_rot, preferred_element_type=jnp.float32
    )
    again = jnp.where(allowed[None], again, -1e30)
    probs_again = jnp.exp(again - log_total)
    d_values = jnp.einsum(
        "hqk,qhd->khd",
        probs_again.astype(jnp.bfloat16),
        d_context_low,
        preferred_element_type=jnp.float32,
    )
    d_probs = jnp.einsum(
        "qhd,khd->hqk", d_context_low, values_low, preferred_element_type=jnp.float32
    )
    d_scores = probs_again * (d_probs - jnp.sum(d_probs * probs_again, axis=-1, keepdims=True))
    d_scores_low = d_scores.astype(jnp.bfloat16)
    d_queries = scaling * jnp.einsum(
        "hqk,khd->qhd", d_scores_low, keys_rot, preferred_element_type=jnp.float32
    )
    d_keys = scaling * jnp.einsum(
        "hqk,qhd->khd", d_scores_low, queries, preferred_element_type=jnp.float32
    )
    d_packed = jnp.stack(
        [unrotate(d_queries, cosine, sine), unrotate(d_keys, cosine, sine), d_values], axis=1
    )
    d_packed_low = d_packed.reshape(row_count, 3 * width).astype(jnp.bfloat16)
    d_hidden = back_project(qkv_weight, d_packed_low) + back_project(up_weight, d_upward_low)
    d_norm = d_hidden * gain
    d_inputs = inv_std * (
        d_norm
        - jnp.mean(d_norm, axis=1, keepdims=True)
        - normed * jnp.mean(d_norm * normed, axis=1, keepdims=True)
    )
    grad_tokens = (grad_out + d_inputs).astype(jnp.bfloat16)
    grad_qkv_w = weight_grad(hidden_low, d_packed_low)
    grad_dense_w = weight_grad(context_low, cotangent)
    grad_up_w = weight_grad(hidden_low, d_upward_low)
    grad_down_w = weight_grad(active_low, cotangent)
    small_terms = (
        jnp.sum(d_hidden * normed, axis=0),
        jnp.sum(d_hidden, axis=0),
        jnp.sum(d_packed_low.astype(jnp.float32), axis=0),
        jnp.sum(grad_out, axis=0),
        jnp.sum(d_upward_low.astype(jnp.float32), axis=0),
    )
    reduced = (
        lax.psum_scatter(small_terms[0], ("rep", "shard"), scatter_dimension=0, tiled=True),
        lax.psum_scatter(small_terms[1], ("rep", "shard"), scatter_dimension=0, tiled=True),
        lax.psum_scatter(small_terms[2], ("rep", "shard"), scatter_dimension=0, tiled=True),
        lax.psum_scatter(small_terms[3], ("rep", "shard"), scatter_dimension=0, tiled=True),
        lax.psum_scatter(small_terms[4], ("rep", "shard"), scatter_dimension=0, tiled=True),
    )
    grad_gain, grad_shift, grad_packed_b, grad_out_b, grad_up_b = reduced
    return (
        output,
        grad_tokens,
        grad_gain,
        grad_shift,
        grad_qkv_w,
        grad_packed_b,
        grad_dense_w,
        grad_out_b,
        grad_up_w,
        grad_up_b,
        grad_down_w,
        grad_out_b,
    )


MIB = 1024 * 1024
VMEM = 60


def params(vmem=VMEM):
    return pltpu.CompilerParams(
        dimension_semantics=("arbitrary",), vmem_limit_bytes=vmem * MIB
    )


def cost(flops, moved):
    return pl.CostEstimate(flops=flops, bytes_accessed=moved, transcendentals=0)


def fixed(shape, start=0):
    index = (start,) + (0,) * (len(shape) - 1)
    return pl.BlockSpec(shape, lambda *_: index, pipeline_mode=pl.Buffered(buffer_count=1))


def whole(array):
    return fixed(array.shape)


def rows_of(array, rows, start=0):
    return pl.BlockSpec((rows, array.shape[1]), lambda i, *_: (i + start // rows, 0))


ANYWHERE = pl.BlockSpec(memory_space=pl.ANY)


def kernel(body, scalars, operands, in_specs, out_specs, out_shape, grid=(1,), scratch=(), work=(0, 0), vmem=16):
    return pl.pallas_call(
        body,
        grid_spec=pltpu.PrefetchScalarGridSpec(
            num_scalar_prefetch=1,
            grid=grid,
            in_specs=in_specs,
            out_specs=out_specs,
            scratch_shapes=list(scratch),
        ),
        out_shape=out_shape,
        compiler_params=params(vmem),
        cost_estimate=cost(*work),
    )(scalars, *operands)


def shaped(shape, dtype=BF16):
    return jax.ShapeDtypeStruct(shape, dtype)


def nn(left_side, right_side):
    return lax.dot_general(
        left_side, right_side, (((1,), (0,)), ((), ())), preferred_element_type=F32
    )


def nt(left_side, right_side):
    return lax.dot_general(
        left_side, right_side, (((1,), (1,)), ((), ())), preferred_element_type=F32
    )


def tn(left_side, right_side):
    return lax.dot_general(
        left_side, right_side, (((0,), (0,)), ((), ())), preferred_element_type=F32
    )


HALF, MIDDLE, ODD, CORE, CHIP = range(5)


def copy_all(copies, sems):
    for at, (source, target) in enumerate(copies):
        pltpu.make_async_copy(source, target, sems.at[at]).start()
    for at, (source, target) in enumerate(copies):
        pltpu.make_async_copy(source, target, sems.at[at]).wait()


def places(where):
    half, odd = where[HALF], where[ODD]
    return (
        (odd, 2 * half + odd),
        (1 - odd, 2 * half + 1 - odd),
        (2 + half, 2 - half),
        (3 - half, 3 - 3 * half),
    )


def copy_pieces(where, pieces, of, sems):
    own, neighbour, other_middle, other_end = places(where)
    common = of(pieces[0], *own) + of(pieces[1], *neighbour)

    @pl.when(where[MIDDLE] == 1)
    def _():
        copy_all(common + of(pieces[2], *other_middle) + of(pieces[3], *other_end), sems)

    @pl.when(where[MIDDLE] == 0)
    def _():
        copy_all(common + of(pieces[4], *other_middle) + of(pieces[5], *other_end), sems)


def multiple(value, size):
    return pl.multiple_of(value * size, size)


def attention_body(parts, run, merge, where, *refs):
    hidden, cot, *refs = refs
    weights, refs = refs[: 6 if merge else 2], refs[6 if merge else 2 :]
    (bias, cosine, sine_a, sine_b, first), refs = refs[:5], refs[5:]
    prior, refs = ((), refs) if merge else (refs[:4], refs[6:])
    (context, d_packed, *grads), refs = refs[:6], refs[6:]
    if merge:
        joined, (sum_qkv, sum_dense, held, out_sems, qkv_w, dense_w, sems) = refs[:2], refs[2:]
        kept = [
            pltpu.make_async_copy(source, target, out_sems.at[4 + i])
            for i, (source, target) in enumerate(zip((qkv_w, dense_w), joined))
        ]
    else:
        (qkv_w, dense_w), (sum_qkv, sum_dense, held, out_sems, before) = weights, refs
        kept = [
            pltpu.make_async_copy(source, before.at[i], out_sems.at[4 + i])
            for i, source in enumerate(prior)
        ]
    step = pl.program_id(0)
    wide = dense_w.shape[0]
    scaling = 1.0 / math.sqrt(HEAD_DIM)
    block, own = sum_qkv.shape[0] // 4, wide // 4
    across = dense_w.shape[1] // parts

    if merge:

        @pl.when(step == 0)
        def _():
            def of(piece, place, plane):
                return [
                    (piece.at[:, : 3 * wide], qkv_w.at[pl.ds(multiple(place, block), block)])
                ] + [
                    (
                        piece.at[j * own : (j + 1) * own, 3 * wide :],
                        dense_w.at[
                            pl.ds(multiple(plane, own), own), j * across : (j + 1) * across
                        ],
                    )
                    for j in range(parts)
                ]

            copy_pieces(where, weights, of, sems)

    @pl.when(step == 0)
    def _():
        for copy in kept:
            copy.start()

    c = jnp.tile(cosine[...], (1, wide // 128))
    sa = jnp.tile(sine_a[...], (1, wide // 128))
    sb = jnp.tile(sine_b[...], (1, wide // 128))

    def turn(value, sign):
        ahead = pltpu.roll(value, wide - ROT // 2, 1)
        behind = pltpu.roll(value, ROT // 2, 1)
        return value * c + sign * (ahead * sa + behind * sb)

    packed = nn(hidden[...], qkv_w[...]) + bias[...]
    queries = (turn(packed[:, :wide], 1.0).astype(BF16).astype(F32) * scaling).astype(BF16)
    keys = turn(packed[:, wide : 2 * wide], 1.0).astype(BF16)
    values = packed[:, 2 * wide :].astype(BF16)
    d_context = nt(cot[...], dense_w[...]).astype(BF16)
    at = lax.broadcasted_iota(jnp.int32, (run, run), 1)
    row = lax.broadcasted_iota(jnp.int32, (run, run), 0)
    all_out, all_q, all_k, all_v = [], [], [], []
    for begin in range(0, hidden.shape[0], run):
        rows = slice(begin, begin + run)
        seen = (at >= first[rows, :1]) & (at <= row)
        out, d_q, d_k, d_v = [], [], [], []
        for h in range(wide // HEAD_DIM):
            part = slice(h * HEAD_DIM, (h + 1) * HEAD_DIM)
            q, k, v, g = (x[rows, part] for x in (queries, keys, values, d_context))
            scores = jnp.where(seen, nt(q, k), -1e30)
            raised = jnp.exp(scores - jnp.max(scores, axis=1, keepdims=True))
            probs = raised * (1.0 / jnp.sum(raised, axis=1, keepdims=True))
            low = probs.astype(BF16)
            o = nn(low, v)
            out.append(o)
            d_v.append(tn(low, g))
            delta = jnp.sum(o * g.astype(F32), axis=1, keepdims=True)
            d_scores = (probs * (nt(g, v) - delta)).astype(BF16)
            d_q.append(nn(d_scores, k) * scaling)
            d_k.append(tn(d_scores, q))
        for rows_of_all, new in ((all_out, out), (all_q, d_q), (all_k, d_k), (all_v, d_v)):
            rows_of_all.append(jnp.concatenate(new, axis=1))
    context[...] = jnp.concatenate(all_out, axis=0).astype(BF16)
    d_packed[:, :wide] = turn(jnp.concatenate(all_q, axis=0), -1.0).astype(BF16)
    d_packed[:, wide : 2 * wide] = turn(jnp.concatenate(all_k, axis=0), -1.0).astype(BF16)
    d_packed[:, 2 * wide :] = jnp.concatenate(all_v, axis=0).astype(BF16)

    @pl.when(step == 0)
    def _():
        sum_qkv[...] = jnp.zeros_like(sum_qkv)
        sum_dense[...] = jnp.zeros_like(sum_dense)

    sum_qkv[...] += tn(hidden[...], d_packed[...])
    sum_dense[...] += tn(context[...], cot[...])

    @pl.when(step == pl.num_programs(0) - 1)
    def _():
        for copy in kept:
            copy.wait()

        def value(at, place, plane):
            summed = sum_qkv[pl.ds(multiple(place, block), block), :]
            beside = sum_dense[pl.ds(multiple(plane, own), own), :]
            beside = jnp.concatenate(
                [beside[:, j * across : (j + 1) * across] for j in range(parts)], axis=0
            )
            total = jnp.concatenate([summed, beside], axis=1)
            return total + before[at].astype(F32) if prior else total

        write_blocks(where, value, grads, held, out_sems)


def attention(where, run, parts, hidden, cot, weights, streams, prior, filled):
    count, width = 2 * hidden.shape[0], hidden.shape[1]
    merge = not prior
    bias = streams[0]
    wide = bias.shape[1] // 3
    rows = run
    steps = count // rows // 2
    start = 0 if merge else steps
    grad = shaped((width // 4, 3 * wide + width // parts))

    def rows_of_run(columns):
        return pl.BlockSpec((rows, columns), lambda i, _: (i + start, 0))

    joined = [shaped((width, 3 * wide)), shaped((wide, width))] if merge else []
    operands = [hidden, cot, *weights, *streams, *prior, *filled]
    first_filled = 1 + len(operands) - len(filled)
    outs = pl.pallas_call(
        functools.partial(attention_body, parts, run, merge),
        grid_spec=pltpu.PrefetchScalarGridSpec(
            num_scalar_prefetch=1,
            grid=(steps,),
            in_specs=[pl.BlockSpec((rows, width), lambda i, _: (i, 0))] * 2
            + ([ANYWHERE] * 6 if merge else [whole(array) for array in weights])
            + [whole(bias)]
            + [rows_of_run(array.shape[1]) for array in streams[1:]]
            + [ANYWHERE for _ in (*prior, *filled)],
            out_specs=[rows_of_run(wide), rows_of_run(3 * wide)]
            + [ANYWHERE] * (4 + len(joined)),
            scratch_shapes=[
                pltpu.VMEM((width, 3 * wide), F32),
                pltpu.VMEM((wide, width), F32),
                pltpu.VMEM((4,) + grad.shape, BF16),
                pltpu.SemaphoreType.DMA((8,)),
            ]
            + [pltpu.VMEM(array.shape, BF16) for array in joined]
            + (
                [pltpu.SemaphoreType.DMA((4 * (1 + parts),))]
                if merge
                else [pltpu.VMEM((4,) + grad.shape, BF16)]
            ),
        ),
        out_shape=[shaped((count, wide)), shaped((count, 3 * wide))] + [grad] * 4 + joined,
        input_output_aliases={first_filled + i: i for i in range(len(filled))},
        compiler_params=params(),
        cost_estimate=cost(18 * 10**9, 20 * MIB),
    )(where, *operands)
    return outs[:2], outs[2:6], outs[6:]


GELU_A = math.sqrt(2.0 / math.pi)
GELU_B = 0.044715


def write_blocks(where, values, grads, held, sems):
    copies = []
    for at, (out, place) in enumerate(zip(grads, places(where))):
        held[at] = values(at, *place).astype(BF16)
        copies.append(pltpu.make_async_copy(held.at[at], out, sems.at[at]))
        copies[-1].start()
    for copy in copies:
        copy.wait()


def forward_body(columns, where, hidden, cot, *refs):
    pieces, (bias, active, slope, joined), refs = refs[:6], refs[6:10], refs[10:]
    (*grads, total, up_w, held, sems, out_sems) = refs
    step, last = pl.program_id(0), pl.num_programs(0) - 1
    join = pltpu.make_async_copy(up_w, joined, out_sems.at[4])

    @pl.when(step == 0)
    def _():
        size = pieces[0].shape[0]

        def of(piece, place, plane):
            return [(piece, up_w.at[pl.ds(multiple(place, size), size)])]

        copy_pieces(where, pieces, of, sems)
        join.start()
        total[...] = jnp.zeros_like(total)

    for j in range(up_w.shape[1] // columns):
        part = slice(j * columns, (j + 1) * columns)
        v = nn(hidden[...], up_w[:, part]) + bias[:, part]
        square = v * v
        t = jnp.tanh(GELU_A * v * (1.0 + GELU_B * square))
        gate = 0.5 * (1.0 + t)
        low = (v * gate).astype(BF16)
        active[:, part] = low
        slope[:, part] = (
            gate + 0.5 * v * (1.0 - t * t) * (GELU_A + (3.0 * GELU_A * GELU_B) * square)
        ).astype(BF16)
        total[part] += tn(low, cot[...])

    @pl.when(step == last)
    def _():
        size = grads[0].shape[0]

        def block(at, place, plane):
            return total[pl.ds(multiple(plane, size), size), :]

        write_blocks(where, block, grads, held, out_sems)
        join.wait()


def forward(where, hidden, cot, pieces, bias, rows=512, columns=512):
    count, wide = hidden.shape[0], bias.shape[1]
    width = cot.shape[1]
    grad = shaped((wide // 4, width))
    outs = kernel(
        functools.partial(forward_body, columns),
        where,
        [hidden, cot, *pieces, bias],
        [rows_of(hidden, rows), rows_of(cot, rows)] + [ANYWHERE] * 6 + [whole(bias)],
        [pl.BlockSpec((rows, wide), lambda i, _: (i, 0))] * 2
        + [ANYWHERE] * 5,
        [shaped((count, wide))] * 2 + [shaped((width, wide))] + [grad] * 4,
        grid=(count // rows,),
        scratch=[
            pltpu.VMEM((wide, width), F32),
            pltpu.VMEM((width, wide), BF16),
            pltpu.VMEM((4,) + grad.shape, BF16),
            pltpu.SemaphoreType.DMA((4,)),
            pltpu.SemaphoreType.DMA((5,)),
        ],
        work=(4 * count * width * wide, 32 * MIB),
        vmem=VMEM,
    )
    return outs[0], outs[1], outs[2], outs[3:]


def backward_body(where, cot, hidden, *refs):
    pieces, (slope, d_upward, sums, joined), refs = refs[:6], refs[6:10], refs[10:]
    (*grads, total, down_w, held, sems, out_sems) = refs
    step, last = pl.program_id(0), pl.num_programs(0) - 1
    join = pltpu.make_async_copy(down_w, joined, out_sems.at[4])

    @pl.when(step == 0)
    def _():
        size = pieces[0].shape[0]

        def of(piece, place, plane):
            return [(piece, down_w.at[pl.ds(multiple(plane, size), size)])]

        copy_pieces(where, pieces, of, sems)
        join.start()
        sums[...] = jnp.zeros_like(sums)
        total[...] = jnp.zeros_like(total)

    low = (nt(cot[...], down_w[...]) * slope[...].astype(F32)).astype(BF16)
    d_upward[...] = low
    sums[...] += jnp.sum(low.astype(F32), axis=0, keepdims=True)
    total[...] += tn(hidden[...], low)

    @pl.when(step == last)
    def _():
        size = grads[0].shape[0]

        def block(at, place, plane):
            return total[pl.ds(multiple(place, size), size), :]

        write_blocks(where, block, grads, held, out_sems)
        join.wait()


def backward(where, cot, hidden, pieces, slope, rows=256):
    count, wide = slope.shape
    width = hidden.shape[1]
    grad = shaped((width // 4, wide))
    outs = kernel(
        backward_body,
        where,
        [cot, hidden, *pieces, slope],
        [rows_of(cot, rows), rows_of(hidden, rows)] + [ANYWHERE] * 6 + [rows_of(slope, rows)],
        [
            pl.BlockSpec((rows, wide), lambda i, _: (i, 0)),
            pl.BlockSpec((1, wide), lambda i, _: (0, 0)),
        ]
        + [ANYWHERE] * 5,
        [shaped((count, wide)), shaped((1, wide), F32), shaped((wide, width))] + [grad] * 4,
        grid=(count // rows,),
        scratch=[
            pltpu.VMEM((width, wide), F32),
            pltpu.VMEM((wide, width), BF16),
            pltpu.VMEM((4,) + grad.shape, BF16),
            pltpu.SemaphoreType.DMA((4,)),
            pltpu.SemaphoreType.DMA((5,)),
        ],
        work=(4 * count * width * wide, 32 * MIB),
        vmem=VMEM,
    )
    return outs[0], outs[1], outs[2], outs[3:]


def two_dots_body(dot, a, aw, b, bw, far, near):
    result = (dot(a[...], aw[...]) + dot(b[...], bw[...])).astype(BF16)
    step, half = pl.program_id(0), pl.num_programs(0) // 2

    @pl.when(step < half)
    def _():
        far[...] = result

    @pl.when(step >= half)
    def _():
        near[...] = result


def two_dots(dot, a, aw, b, bw, width, rows=256):
    count = a.shape[0]
    steps = count // rows
    half = steps // 2

    def of(array):
        return pl.BlockSpec((rows, array.shape[1]), lambda i: (lax.rem(i + half, steps), 0))

    shape = jax.ShapeDtypeStruct((count // 2, width), BF16)
    return pl.pallas_call(
        functools.partial(two_dots_body, dot),
        grid=(steps,),
        in_specs=[of(a), whole(aw), of(b), whole(bw)],
        out_specs=[
            pl.BlockSpec((rows, width), lambda i: (jnp.minimum(i, half - 1), 0)),
            pl.BlockSpec((rows, width), lambda i: (jnp.maximum(i - half, 0), 0)),
        ],
        out_shape=[shape, shape],
        compiler_params=params(),
        cost_estimate=cost(
            2 * count * (aw.size + bw.size),
            count * 2 * (width + a.shape[1] + b.shape[1]) + 2 * (aw.size + bw.size),
        ),
    )(a, aw, b, bw)


def deal_first_body(planes, chips, where, up, qkv, keep, send):
    mates, n = CORES * chips, up.shape[0]
    block = up.shape[1] // (planes * mates)
    for core in range(CORES):
        for chip in range(chips):
            i = core * chips + chip
            pieces = [
                up[:, (p * mates + i) * block : (p * mates + i + 1) * block] for p in range(planes)
            ] + [
                qkv[:, (t * mates + i) * HEAD_DIM : (t * mates + i + 1) * HEAD_DIM]
                for t in range(3 * planes)
            ]
            value = jnp.concatenate(pieces, axis=1)

            @pl.when(where[CORE] == core)
            def _():
                keep[chip] = value

            @pl.when(where[CORE] != core)
            def _():
                send[chip] = value


def deal_first(where, planes, chips, up, qkv):
    out = shaped((chips, up.shape[0], (up.shape[1] + qkv.shape[1]) // (CORES * chips)))
    return kernel(
        functools.partial(deal_first_body, planes, chips),
        where,
        [up, qkv],
        [whole(up), whole(qkv)],
        [fixed(out.shape)] * 2,
        [out] * 2,
        work=(0, 4 * MIB),
    )


def deal_second_body(where, keep, came, *outs):
    core = where[CORE]
    for r, out in enumerate(outs):
        at = where[CHIP] ^ r
        out[pl.ds(core, 1)] = keep[pl.ds(at, 1)]
        out[pl.ds(1 - core, 1)] = came[pl.ds(at, 1)]


def deal_second(where, keep, came):
    chips, n, columns = keep.shape
    out = shaped((CORES, n, columns))
    return kernel(
        deal_second_body,
        where,
        [keep, came],
        [whole(keep), whole(came)],
        [fixed(out.shape)] * chips,
        [out] * chips,
        work=(0, 4 * MIB),
    )


def deal_last_body(chips, where, *refs):
    blocks, dense, (u, a) = refs[:chips], refs[chips], refs[chips + 1 :]
    n, columns = blocks[0].shape[1:]
    middle = u.shape[1]
    wide = columns - middle
    for r, block in enumerate(blocks):
        for core in range(CORES):
            rows = pl.ds(multiple(core * chips + (where[CHIP] ^ r), n), n)
            u[rows, :] = block[core, :, :middle]
            a[rows, :wide] = block[core, :, middle:]
    across = a.shape[1] - wide
    for j in range(dense.shape[1] // across):
        a[j * n : (j + 1) * n, wide:] = dense[:, j * across : (j + 1) * across]


def deal_last(where, blocks, dense, middle):
    chips = len(blocks)
    n, columns = blocks[0].shape[1:]
    mates = CORES * chips
    shapes = [
        shaped((mates * n, middle)),
        shaped((mates * n, columns - middle + dense.shape[1] // mates)),
    ]
    return kernel(
        functools.partial(deal_last_body, chips),
        where,
        [*blocks, dense],
        [whole(array) for array in (*blocks, dense)],
        [fixed(shape.shape) for shape in shapes],
        shapes,
        work=(0, 4 * MIB),
    )


def finish_body(chips, wide, where, own, middle, last, *outs):
    keep, send = outs[:2]
    n = own.shape[0]
    step = n // (CORES * chips)
    total = own[...].astype(F32) + middle[...].astype(F32) + last[...].astype(F32)
    low = total[:, :wide].astype(BF16)
    for core in range(CORES):

        @pl.when(where[CORE] == core)
        def _():
            for chip in range(chips):
                at = (core * chips + chip) * step
                keep[chip] = low[at : at + step]
                at = ((1 - core) * chips + chip) * step
                send[chip] = low[at : at + step]

    if len(outs) == 3:
        beside = outs[2]
        across = total.shape[1] - wide
        for j in range(n // step):
            beside[:, j * across : (j + 1) * across] = total[j * step : (j + 1) * step, wide:]


def finish(where, chips, wide, own, middle, last):
    n, columns = own.shape
    step = n // (CORES * chips)
    shapes = [shaped((chips, step, wide))] * 2
    if wide < columns:
        shapes.append(shaped((step, (columns - wide) * CORES * chips), F32))
    return kernel(
        functools.partial(finish_body, chips, wide),
        where,
        [own, middle, last],
        [whole(own)] * 3,
        [fixed(shape.shape) for shape in shapes],
        shapes,
        work=(0, 4 * MIB),
    )


def back_body(groups, where, *refs):
    blocks, out, held = refs[:-2], refs[-2], refs[-1]
    chips = len(blocks)
    n, columns = blocks[0].shape[1:]
    size = columns // groups
    for r, block in enumerate(blocks):
        held[pl.ds(where[CHIP] ^ r, 1)] = block[...][None]
    for group in range(groups):
        for core in range(CORES):
            start = (group * CORES + core) * chips * size
            out[:, start : start + chips * size] = jnp.concatenate(
                [held[chip, core, :, group * size : (group + 1) * size] for chip in range(chips)],
                axis=1,
            ).astype(F32)


def back(where, blocks, groups):
    chips = len(blocks)
    n, columns = blocks[0].shape[1:]
    out = shaped((n, columns * CORES * chips), F32)
    return kernel(
        functools.partial(back_body, groups),
        where,
        blocks,
        [whole(block) for block in blocks],
        fixed(out.shape),
        out,
        scratch=[pltpu.VMEM((chips,) + blocks[0].shape, BF16)],
        work=(0, 4 * MIB),
    )


def corners_body(where, *refs):
    sources, outs = refs[:-2], refs[-2:]
    for at in range(len(sources) // 4):
        for i, out in enumerate(outs):
            near, came = sources[4 * at + 2 * i], sources[4 * at + 2 * i + 1]
            rows = near.shape[0]
            total = near[...].astype(F32) + came[...].astype(F32)
            out[at * rows : (at + 1) * rows] = total.astype(BF16)


def corners(where, *sums):
    rows, width = sums[0][0].shape[0] // 8, sums[0][0].shape[1]
    out = shaped((len(sums) * rows, width))
    return kernel(
        corners_body,
        where,
        [term for terms in sums for _ in range(2) for term in terms],
        [fixed((rows, width), 6 + i) for _ in sums for i in range(2) for _ in range(2)],
        [fixed(out.shape)] * 2,
        [out] * 2,
        work=(0, 4 * MIB),
    )


def pair_halves_body(where, *refs):
    sources, outs = refs[:-2], refs[-2:]
    for at in range(len(sources) // 2):
        for i, out in enumerate(outs):
            rows = sources[0].shape[0]
            out[at * rows : (at + 1) * rows] = sources[2 * at + i][...]


def pair_halves(where, *pairs):
    rows, width = pairs[0][0].shape[0] // 2, pairs[0][0].shape[1]
    out = shaped((len(pairs) * rows, width))
    return kernel(
        pair_halves_body,
        where,
        [array for by_x, by_y in pairs for array in (by_y, by_x)],
        [fixed((rows, width), i) for _ in pairs for i in range(2)],
        [fixed(out.shape)] * 2,
        [out] * 2,
        work=(0, 4 * MIB),
    )


def sides_body(where, near_x, near_y, came_x, came_y, extra_x, extra_y, for_x, for_y):
    half = extra_x.shape[0]
    x = near_x[...].astype(F32) + came_x[...].astype(F32)
    y = near_y[...].astype(F32) + came_y[...].astype(F32)
    for_x[:half] = x[:half].astype(BF16)
    for_x[half:] = (x[half:] + extra_x[...].astype(F32)).astype(BF16)
    for_y[:half] = (y[:half] + extra_y[...].astype(F32)).astype(BF16)
    for_y[half:] = y[half:].astype(BF16)


def sides(where, near, came, extra_y, extra_x, at):
    rows, width = near.shape[0] // 4, near.shape[1]
    blocks = [fixed((rows, width), 1), fixed((rows, width), 2)]
    return kernel(
        sides_body,
        where,
        [near, near, came, came, extra_x, extra_y],
        blocks * 2 + [fixed((rows // 2, width), at)] * 2,
        [fixed((rows, width))] * 2,
        [shaped((rows, width))] * 2,
        work=(0, 8 * MIB),
    )


def norm_back_body(
    where, near, came, by_x, by_y, tokens, cot, gain, grad_tokens, gain_sum, shift_sum
):
    parts = [ref[...].astype(F32) for ref in (near, came, by_x, by_y)]
    turned = parts[0] + parts[1] + parts[2] + parts[3]
    middle = turned.shape[1] // 2
    swap = where[HALF] == 1
    lower, upper = turned[:, :middle], turned[:, middle:]
    d_hidden = jnp.concatenate(
        [jnp.where(swap, upper, lower), jnp.where(swap, lower, upper)], axis=1
    )
    inputs = tokens[...].astype(F32)
    centered = inputs - jnp.mean(inputs, axis=1, keepdims=True)
    inv_std = lax.rsqrt(jnp.mean(centered * centered, axis=1, keepdims=True) + EPSILON)
    normed = centered * inv_std
    d_norm = d_hidden * gain[...]
    d_inputs = inv_std * (
        d_norm
        - jnp.mean(d_norm, axis=1, keepdims=True)
        - normed * jnp.mean(d_norm * normed, axis=1, keepdims=True)
    )
    grad_tokens[...] = (cot[...].astype(F32) + d_inputs).astype(BF16)

    @pl.when(pl.program_id(0) == 0)
    def _():
        gain_sum[...] = jnp.zeros_like(gain_sum)
        shift_sum[...] = jnp.zeros_like(shift_sum)

    gain_sum[...] += jnp.sum(d_hidden * normed, axis=0, keepdims=True)
    shift_sum[...] += jnp.sum(d_hidden, axis=0, keepdims=True)


def norm_back(where, near, came, by_x, by_y, tokens, cot, gain, rows=128):
    count, width = tokens.shape
    block = pl.BlockSpec((rows, width), lambda i, _: (i, 0))
    return kernel(
        norm_back_body,
        where,
        [near, came, by_x, by_y, tokens, cot, gain],
        [block] * 6 + [whole(gain)],
        [block, fixed((1, width)), fixed((1, width))],
        [shaped((count, width)), shaped((1, width), F32), shaped((1, width), F32)],
        grid=(count // rows,),
        work=(0, 8 * MIB),
    )


def tied(*groups):
    return lax.optimization_barrier(groups)


def by_planes(
    planes,
    mates,
    tokens,
    lengths,
    ln_gain,
    ln_bias,
    qkv_weight,
    qkv_bias,
    dense_weight,
    dense_bias,
    up_weight,
    up_bias,
    down_weight,
    down_bias,
    cotangent,
):
    row_count, width = tokens.shape
    owners = planes * mates
    chips = mates // CORES
    rank = lax.axis_index("rep") * chips + lax.axis_index("shard")
    z, m = rank // mates, rank % mates
    c, s = m // chips, m % chips
    middle_plane = jnp.where((z == 1) | (z == 2), 1, 0)
    where = jnp.stack([z // 2, middle_plane, z % 2, c, s]).astype(jnp.int32)
    rows_own = qkv_weight.shape[0]
    ff_block = up_bias.shape[0]
    heads_width = planes * HEAD_DIM
    count = mates * row_count

    def flip(value, r):
        return lax.ppermute(
            value,
            AXES,
            [(p * mates + i, p * mates + (i ^ r)) for p in range(planes) for i in range(mates)],
        )

    def between(value, pairs):
        return lax.ppermute(
            value, AXES, [(p * mates + i, q * mates + i) for p, q in pairs for i in range(mates)]
        )

    def to_neighbour(value):
        return between(value, [(p, p ^ 1) for p in range(planes)])

    def over_middle(value):
        return between(value, [(1, 2), (2, 1)])

    def outwards(value):
        return between(value, [(1, 0), (2, 3)])

    def inwards(value):
        return between(value, [(0, 1), (3, 2)])

    def added(*terms):
        return sum(term.astype(F32) for term in terms)

    def add(*terms, dtype=BF16):
        return added(*terms).astype(dtype)

    def deal_over_chips(keep, send):
        blocks = deal_second(where, keep, flip(send, chips))
        return [blocks[0]] + [flip(blocks[r], r) for r in range(1, chips)]

    def over_planes(table):
        return table + sum(
            between(table, [(p, (p + r) % planes) for p in range(planes)])
            for r in range(1, planes)
        )

    def over_chips(table):
        return table + sum(flip(table, r) for r in range(1, chips))

    def over_chips_in_turn(table):
        for r in (1, 2):
            table = table + flip(table, r)
        return table

    def over_cores(table):
        return table + flip(table, chips)

    def turned(value):
        middle = value.shape[1] // 2
        lower, upper, first_half = value[:, :middle], value[:, middle:], z < 2
        return jnp.concatenate(
            [jnp.where(first_half, lower, upper), jnp.where(first_half, upper, lower)], axis=1
        )

    half = row_count // 2

    def near_first(block):
        return flip(block, 1), flip(block, 2)

    parts = [ln_gain, ln_bias, qkv_bias, dense_bias, up_bias, down_bias, lengths[0].astype(BF16)]
    sizes = [part.shape[0] for part in parts]
    starts = [sum(sizes[:i]) for i in range(len(sizes))]
    own_row = jnp.concatenate(parts)
    own_row = jnp.pad(own_row, (0, -len(own_row) % 128))
    first_pieces = deal_first(where, planes, chips, up_weight, qkv_weight)
    table = jnp.where(jnp.arange(owners)[:, None] == rank, own_row[None, :], 0)
    wide = 3 * heads_width
    keep, send = first_pieces
    table = over_planes(table)
    blocks, table, down_own = tied(deal_second(where, keep, flip(send, chips)), table, down_weight)
    dealt = [blocks[0]] + [flip(blocks[r], r) for r in range(1, chips)]
    w1, w2a = to_neighbour(down_own), over_middle(down_own)
    table, dealt[1], dealt[2] = tied(table, dealt[1], dealt[2])
    table = over_cores(over_chips(table))
    u_own, a_own = deal_last(where, dealt, dense_weight, planes * ff_block)
    u_own, a_own, table, w1, w2a, cot_own = tied(
        u_own, a_own, table, w1, w2a, cotangent
    )
    table = table.astype(F32)

    a1, a2a = to_neighbour(a_own), over_middle(a_own)
    cot_near = near_first(cot_own)

    def column(i):
        return table[:, starts[i] : starts[i] + sizes[i]].reshape(-1)

    gain, shift_by = column(0), column(1)
    packed_bias = lax.dynamic_index_in_dim(
        column(2).reshape(3, planes, mates, HEAD_DIM), m, 2, keepdims=False
    ).reshape(1, -1)
    upward_bias = lax.dynamic_index_in_dim(
        column(4).reshape(planes, mates, ff_block), m, 1, keepdims=False
    ).reshape(1, -1)
    out_bias = column(3) + column(5)
    all_lengths = table[:, starts[6] : starts[6] + sizes[6]].astype(jnp.int32)
    doc_sizes = jnp.stack(
        [
            lax.dynamic_index_in_dim(all_lengths, z * mates + (m ^ r), 0, keepdims=False)
            for r in range(mates)
        ]
    )

    inputs_f = tokens.astype(F32)
    average = jnp.mean(inputs_f, axis=1, keepdims=True)
    centered = inputs_f - average
    spread = jnp.mean(centered * centered, axis=1, keepdims=True)
    inv_std = lax.rsqrt(spread + EPSILON)
    normed = centered * inv_std
    hidden_own = turned((normed * gain + shift_by).astype(BF16))

    ends_at = jnp.cumsum(doc_sizes, axis=1)
    at = jnp.arange(row_count, dtype=jnp.int32)
    offsets = jnp.max(jnp.where(at[None, :, None] >= ends_at[:, None, :], ends_at[:, None, :], 0), axis=2)
    places = (at[None, :] - offsets).astype(F32).reshape(count, 1)
    lane = jnp.arange(2 * HEAD_DIM, dtype=jnp.int32) % HEAD_DIM
    inverse = jnp.power(jnp.float32(10000.0), -2.0 * (lane % (ROT // 2)).astype(F32) / ROT)
    angles = places * inverse[None, :]
    sine = jnp.sin(angles)
    cosine = jnp.where(lane < ROT, jnp.cos(angles), 1.0)
    sine_a = jnp.where(lane < ROT // 2, -sine, 0.0)
    sine_b = jnp.where((lane >= ROT // 2) & (lane < ROT), sine, 0.0)
    first = jnp.broadcast_to(offsets.reshape(count, 1), (count, 2 * HEAD_DIM))

    a1, a2a, cot_near, hidden_own, u_own = tied(a1, a2a, cot_near, hidden_own, u_own)
    a3a, a2b = outwards(a2a), over_middle(a1)
    hidden_near = near_first(hidden_own)

    a3a, a2b, hidden_near, cot_near, u_own = tied(a3a, a2b, hidden_near, cot_near, u_own)
    a3b, u2a = outwards(a2b), over_middle(u_own)
    for_x, for_y = pair_halves(where, cot_near, hidden_near)
    corner_y, corner_x = flip(for_x, 1), flip(for_y, 2)
    room = jnp.zeros((row_count, width), BF16)
    cot_most = jnp.concatenate([cot_own, *cot_near, room], axis=0)
    hidden_most = jnp.concatenate([hidden_own, *hidden_near, room], axis=0)

    a3b, u2a, corner_x, corner_y, hidden_most, cot_most, u_own, w1, cosine, sine_a, sine_b, first = tied(
        a3b, u2a, corner_x, corner_y, hidden_most, cot_most, u_own, w1, cosine, sine_a, sine_b, first
    )
    u1, w2b = to_neighbour(u_own), over_middle(w1)
    def with_corners(most, at):
        for i, corner in enumerate((corner_y, corner_x)):
            most = lax.dynamic_update_slice_in_dim(
                most, corner[at : at + half], 3 * row_count + i * half, 0
            )
        return most

    cot, hidden = with_corners(cot_most, 0), with_corners(hidden_most, half)
    hidden, cot = [hidden, flip(hidden, chips)], [cot, flip(cot, chips)]
    streams = [packed_bias, cosine, sine_a, sine_b, first]
    rows_a, g_a, (qkv_w, dense_w) = attention(
        where,
        row_count,
        mates,
        hidden[0],
        cot[0],
        [a_own, a1, a2a, a2b, a3a, a3b],
        streams,
        [],
        [],
    )

    u1, w2b, u2a, rows_a, g_a, hidden, cot = tied(u1, w2b, u2a, rows_a, g_a, hidden, cot)
    u3a, u2b = outwards(u2a), over_middle(u1)
    (context, d_packed), g_a, _ = attention(
        where, row_count, mates, hidden[1], cot[1], [qkv_w, dense_w], streams, g_a, rows_a
    )

    u3a, u2b, g_a, w2a, d_packed, hidden, cot = tied(u3a, u2b, g_a, w2a, d_packed, hidden, cot)
    u3b, q1_a_end = outwards(u2b), inwards(g_a[3])
    hidden, cot = jnp.concatenate(hidden, axis=0), jnp.concatenate(cot, axis=0)
    mine = jnp.arange(mates) == m
    packed_sum = jnp.sum(d_packed.astype(F32), axis=0).reshape(3, planes, 1, HEAD_DIM)
    packed_sum = jnp.where(mine[None, None, :, None], packed_sum, 0.0).reshape(owners, -1)
    cot_sum = jnp.sum(cotangent.astype(F32), axis=0).reshape(owners, -1)

    u3b, q1_a_end, g_a, w2a, hidden, cot, packed_sum, cot_sum = tied(
        u3b, q1_a_end, g_a, w2a, hidden, cot, packed_sum, cot_sum
    )
    w3a, q1_a_mid = outwards(w2a), inwards(g_a[2])
    active, slope, up_w, g_w = forward(
        where, hidden, cot, [u_own, u1, u2a, u2b, u3a, u3b], upward_bias
    )

    w3a, q1_a_mid, q1_a_end, g_a, g_w, w2b = tied(w3a, q1_a_mid, q1_a_end, g_a, g_w, w2b)
    w3b, q1_w_end, q2_a_end = outwards(w2b), inwards(g_w[3]), over_middle(add(g_a[3], q1_a_end))
    share_a_mid = add(g_a[2], q1_a_mid)

    w3b, q1_w_end, q2_a_end, share_a_mid, g_a, g_w, cot = tied(
        w3b, q1_w_end, q2_a_end, share_a_mid, g_a, g_w, cot
    )
    q3_a, q2_a_mid = to_neighbour(add(g_a[1], q2_a_end)), over_middle(share_a_mid)
    d_upward, upward_sum, down_w, g_u = backward(
        where, cot, hidden, [down_own, w1, w2a, w2b, w3a, w3b], slope
    )

    q3_a, q2_a_mid, g_w, g_u, d_upward, upward_sum = tied(
        q3_a, q2_a_mid, g_w, g_u, d_upward, upward_sum
    )
    q1_u_end = inwards(g_u[3])
    d_hidden_far, d_hidden_near = two_dots(nt, d_packed, qkv_w, d_upward, up_w, width)
    upward_sum = upward_sum.reshape(planes, 1, ff_block)
    upward_sum = jnp.where(mine[None, :, None], upward_sum, 0.0).reshape(owners, -1)
    keep, send, grad_dense_w = finish(where, chips, wide, g_a[0], q2_a_mid, q3_a)
    came = flip(send, chips)

    q1_u_end, d_hidden_far, d_hidden_near, g_u, g_w, context, upward_sum, keep, came = tied(
        q1_u_end, d_hidden_far, d_hidden_near, g_u, g_w, context, upward_sum, keep, came
    )
    q1_u_mid, q2_u_end = inwards(g_u[2]), over_middle(add(g_u[3], q1_u_end))
    d_hidden_came = flip(d_hidden_far, chips)
    out_far, out_near = two_dots(nn, context, dense_w, active, down_w, width)
    corner_y, corner_x = corners(where, (d_hidden_near, d_hidden_came))
    extra_y, extra_x = flip(corner_y, 1), flip(corner_x, 2)

    q1_u_mid, q2_u_end, extra_x, extra_y, out_far, out_near, g_u, g_w, keep = tied(
        q1_u_mid, q2_u_end, extra_x, extra_y, out_far, out_near, g_u, g_w, keep
    )
    q3_u, q2_u_mid = to_neighbour(add(g_u[1], q2_u_end)), over_middle(add(g_u[2], q1_u_mid))
    out_came = flip(out_far, chips)
    corner_y, corner_x = corners(where, (out_near, out_came))
    out_extra_y, out_extra_x = flip(corner_y, 1), flip(corner_x, 2)
    blocks = deal_second(where, keep, came)

    q3_u, q2_u_mid, out_extra_x, out_extra_y, g_u, g_w, q1_w_end, blocks = tied(
        q3_u, q2_u_mid, out_extra_x, out_extra_y, g_u, g_w, q1_w_end, blocks
    )
    q1_w_mid, q2_w_end = inwards(g_w[2]), over_middle(add(g_w[3], q1_w_end))
    for_x, for_y = sides(where, d_hidden_near, d_hidden_came, extra_y, extra_x, 0)
    d_hidden_last = flip(for_x, 1), flip(for_y, 2)
    block_x, block_y, block_xy = [flip(blocks[r], r) for r in range(1, chips)]
    for_x, for_y = sides(where, out_near, out_came, out_extra_y, out_extra_x, 0)
    keep, send = finish(where, chips, planes * ff_block, g_u[0], q2_u_mid, q3_u)

    (
        q1_w_mid,
        q2_w_end,
        d_hidden_last,
        for_x,
        for_y,
        g_w,
        block_x,
        block_y,
        block_xy,
        keep,
        send,
    ) = tied(
        q1_w_mid,
        q2_w_end,
        d_hidden_last,
        for_x,
        for_y,
        g_w,
        block_x,
        block_y,
        block_xy,
        keep,
        send,
    )
    q3_w, q2_w_mid = to_neighbour(add(g_w[1], q2_w_end)), over_middle(add(g_w[2], q1_w_mid))
    out_last = flip(for_x, 1), flip(for_y, 2)
    held = deal_second(where, keep, flip(send, chips))
    grad_tokens, gain_sum, shift_sum = norm_back(
        where,
        d_hidden_near,
        d_hidden_came,
        *d_hidden_last,
        tokens,
        cotangent,
        gain.reshape(1, -1),
    )
    sums = jnp.concatenate(
        [
            gain_sum.reshape(owners, -1),
            shift_sum.reshape(owners, -1),
            cot_sum,
            packed_sum,
            upward_sum,
        ],
        axis=1,
    )

    sums = over_cores(sums)
    q3_w, q2_w_mid, g_w, out_last, sums, held = tied(q3_w, q2_w_mid, g_w, out_last, sums, held)
    received = [flip(held[r], r) for r in range(1, chips)]
    for r in (1, 2):
        sums = sums + between(sums, [(p, p ^ r) for p in range(planes)])
    grad_qkv_w = back(where, [blocks[0], block_x, block_y, block_xy], 3 * planes)
    output = added(out_near[:row_count], out_came[:row_count], *out_last)
    output = (inputs_f + output + out_bias).astype(BF16)
    grad_down_w = add(g_w[0], q2_w_mid, q3_w, dtype=F32)
    received, sums, grad_qkv_w, output, grad_down_w = tied(
        received, sums, grad_qkv_w, output, grad_down_w
    )
    sums = over_chips(sums)
    grad_up_w = back(where, [held[0]] + received, planes)
    total = lax.dynamic_index_in_dim(sums, rank, 0, keepdims=False)
    grad_gain, grad_shift, grad_out_b, grad_packed_b, grad_up_b = jnp.split(
        total,
        [
            sizes[0],
            sizes[0] + sizes[1],
            sizes[0] + sizes[1] + sizes[3],
            sizes[0] + sizes[1] + sizes[3] + sizes[2],
        ],
    )
    return (
        output,
        grad_tokens,
        grad_gain,
        grad_shift,
        grad_qkv_w,
        grad_packed_b,
        grad_dense_w,
        grad_out_b,
        grad_up_w,
        grad_up_b,
        grad_down_w,
        grad_out_b,
    )


def solution(mesh):
    planes, mates = mesh.shape["rep"] // CORES, CORES * mesh.shape["shard"]
    rows, vector = P(AXES, None), P(AXES)

    def layer(*arrays):
        width = arrays[0].shape[1]
        if mesh.shape["shard"] == 4 and planes * mates * HEAD_DIM == width:
            return by_planes(planes, mates, *arrays)
        return gathered_whole(*arrays)

    return jax.shard_map(
        layer,
        mesh=mesh,
        in_specs=(
            rows, rows, vector, vector, rows, vector, rows, vector, rows, vector, rows, vector, rows,
        ),
        out_specs=(
            rows, rows, vector, vector, rows, vector, rows, vector, rows, vector, rows, vector,
        ),
        check_vma=False,
    )
```

```python
import functools
import math

import jax
import jax.numpy as jnp
from jax import lax
from jax.experimental import pallas as pl
from jax.experimental.pallas import tpu as pltpu
from jax.sharding import PartitionSpec as P

HEADS = 32
HEAD_DIM = 64
ROT = 32
CORES = 2
AXES = ("rep", "shard")
BF16 = jnp.bfloat16
F32 = jnp.float32


EPSILON = 1e-05


def positions(doc_sizes, row_count):
    ends_at = jnp.cumsum(doc_sizes)
    starts_at = ends_at - doc_sizes
    indices = jnp.arange(row_count, dtype=jnp.int32)
    doc_ids = jnp.sum((indices[:, None] >= ends_at[None, :]).astype(jnp.int32), axis=1)
    member = doc_ids[:, None] == jnp.arange(doc_sizes.shape[0], dtype=jnp.int32)[None, :]
    offsets = jnp.sum(jnp.where(member, starts_at[None, :], 0), axis=1)
    places = (indices - offsets).astype(jnp.float32)
    allowed = (doc_ids[:, None] == doc_ids[None, :]) & (indices[None, :] <= indices[:, None])
    return (places, allowed)


def rotary(places):
    indices = jnp.arange(ROT // 2, dtype=jnp.float32)
    inverse = jnp.power(jnp.float32(10000.0), -2.0 * indices / ROT)
    angles = places[:, None] * inverse[None, :]
    return (jnp.cos(angles)[:, None, :], jnp.sin(angles)[:, None, :])


def rotate(values, cosine, sine):
    lower_half = values[..., : ROT // 2]
    upper_half = values[..., ROT // 2 : ROT]
    return jnp.concatenate(
        [
            lower_half * cosine - upper_half * sine,
            upper_half * cosine + lower_half * sine,
            values[..., ROT:],
        ],
        axis=-1,
    )


def unrotate(incoming, cosine, sine):
    lower_half = incoming[..., : ROT // 2]
    upper_half = incoming[..., ROT // 2 : ROT]
    return jnp.concatenate(
        [
            lower_half * cosine + upper_half * sine,
            upper_half * cosine - lower_half * sine,
            incoming[..., ROT:],
        ],
        axis=-1,
    )


def project(weight, left_side):
    whole = lax.all_gather(weight, ("rep", "shard"), axis=0, tiled=True)
    return jnp.dot(left_side, whole, preferred_element_type=jnp.float32)


def back_project(weight, incoming):
    whole = lax.all_gather(weight, ("rep", "shard"), axis=0, tiled=True)
    return lax.dot_general(
        incoming, whole, (((1,), (1,)), ((), ())), preferred_element_type=jnp.float32
    )


def weight_grad(left_side, incoming):
    return lax.psum_scatter(
        lax.dot_general(
            left_side, incoming, (((0,), (0,)), ((), ())), preferred_element_type=jnp.float32
        ),
        ("rep", "shard"),
        scatter_dimension=0,
        tiled=True,
    )


def gathered_whole(
    tokens,
    lengths,
    ln_gain,
    ln_bias,
    qkv_weight,
    qkv_bias,
    dense_weight,
    dense_bias,
    up_weight,
    up_bias,
    down_weight,
    down_bias,
    cotangent,
):
    row_count = tokens.shape[0]
    width = tokens.shape[1]
    small = (
        lax.all_gather(ln_gain, ("rep", "shard"), axis=0, tiled=True),
        lax.all_gather(ln_bias, ("rep", "shard"), axis=0, tiled=True),
        lax.all_gather(qkv_bias, ("rep", "shard"), axis=0, tiled=True),
        lax.all_gather(dense_bias, ("rep", "shard"), axis=0, tiled=True),
        lax.all_gather(up_bias, ("rep", "shard"), axis=0, tiled=True),
        lax.all_gather(down_bias, ("rep", "shard"), axis=0, tiled=True),
    )
    gain, shift, packed_bias, dense_shift, upward_bias, downward_bias = [
        tensor.astype(jnp.float32) for tensor in small
    ]
    places, allowed = positions(lengths[0], row_count)
    cosine, sine = rotary(places)
    scaling = 1.0 / math.sqrt(HEAD_DIM)
    inputs_f = tokens.astype(jnp.float32)
    average = jnp.mean(inputs_f, axis=1, keepdims=True)
    centered = inputs_f - average
    spread = jnp.mean(centered * centered, axis=1, keepdims=True)
    inv_std = lax.rsqrt(spread + EPSILON)
    normed = centered * inv_std
    hidden_low = (normed * gain + shift).astype(jnp.bfloat16)
    packed = (project(qkv_weight, hidden_low) + packed_bias).reshape(row_count, 3, HEADS, HEAD_DIM)
    queries = rotate(packed[:, 0], cosine, sine).astype(jnp.bfloat16)
    keys_rot = rotate(packed[:, 1], cosine, sine).astype(jnp.bfloat16)
    values_low = packed[:, 2].astype(jnp.bfloat16)
    scores = scaling * jnp.einsum(
        "qhd,khd->hqk", queries, keys_rot, preferred_element_type=jnp.float32
    )
    scores = jnp.where(allowed[None], scores, -1e30)
    maximum = jnp.max(scores, axis=-1, keepdims=True)
    raised = jnp.exp(scores - maximum)
    totals = jnp.sum(raised, axis=-1, keepdims=True)
    probs = raised / totals
    log_total = maximum + jnp.log(totals)
    context = jnp.einsum(
        "hqk,khd->qhd", probs.astype(jnp.bfloat16), values_low, preferred_element_type=jnp.float32
    )
    context_low = context.reshape(row_count, width).astype(jnp.bfloat16)
    attended = project(dense_weight, context_low) + dense_shift
    upward = project(up_weight, hidden_low) + upward_bias
    active_low = jax.nn.gelu(upward, approximate=True).astype(jnp.bfloat16)
    downward = project(down_weight, active_low) + downward_bias
    output = (inputs_f + attended + downward).astype(jnp.bfloat16)
    grad_out = cotangent.astype(jnp.float32)
    d_active = back_project(down_weight, cotangent)
    gelu_value, gelu_pull = jax.vjp(lambda inner: jax.nn.gelu(inner, approximate=True), upward)
    d_upward_low = gelu_pull(d_active)[0].astype(jnp.bfloat16)
    d_context_low = (
        back_project(dense_weight, cotangent)
        .astype(jnp.bfloat16)
        .reshape(row_count, HEADS, HEAD_DIM)
    )
    again = scaling * jnp.einsum(
        "qhd,khd->hqk", queries, keys_rot, preferred_element_type=jnp.float32
    )
    again = jnp.where(allowed[None], again, -1e30)
    probs_again = jnp.exp(again - log_total)
    d_values = jnp.einsum(
        "hqk,qhd->khd",
        probs_again.astype(jnp.bfloat16),
        d_context_low,
        preferred_element_type=jnp.float32,
    )
    d_probs = jnp.einsum(
        "qhd,khd->hqk", d_context_low, values_low, preferred_element_type=jnp.float32
    )
    d_scores = probs_again * (d_probs - jnp.sum(d_probs * probs_again, axis=-1, keepdims=True))
    d_scores_low = d_scores.astype(jnp.bfloat16)
    d_queries = scaling * jnp.einsum(
        "hqk,khd->qhd", d_scores_low, keys_rot, preferred_element_type=jnp.float32
    )
    d_keys = scaling * jnp.einsum(
        "hqk,qhd->khd", d_scores_low, queries, preferred_element_type=jnp.float32
    )
    d_packed = jnp.stack(
        [unrotate(d_queries, cosine, sine), unrotate(d_keys, cosine, sine), d_values], axis=1
    )
    d_packed_low = d_packed.reshape(row_count, 3 * width).astype(jnp.bfloat16)
    d_hidden = back_project(qkv_weight, d_packed_low) + back_project(up_weight, d_upward_low)
    d_norm = d_hidden * gain
    d_inputs = inv_std * (
        d_norm
        - jnp.mean(d_norm, axis=1, keepdims=True)
        - normed * jnp.mean(d_norm * normed, axis=1, keepdims=True)
    )
    grad_tokens = (grad_out + d_inputs).astype(jnp.bfloat16)
    grad_qkv_w = weight_grad(hidden_low, d_packed_low)
    grad_dense_w = weight_grad(context_low, cotangent)
    grad_up_w = weight_grad(hidden_low, d_upward_low)
    grad_down_w = weight_grad(active_low, cotangent)
    small_terms = (
        jnp.sum(d_hidden * normed, axis=0),
        jnp.sum(d_hidden, axis=0),
        jnp.sum(d_packed_low.astype(jnp.float32), axis=0),
        jnp.sum(grad_out, axis=0),
        jnp.sum(d_upward_low.astype(jnp.float32), axis=0),
    )
    reduced = (
        lax.psum_scatter(small_terms[0], ("rep", "shard"), scatter_dimension=0, tiled=True),
        lax.psum_scatter(small_terms[1], ("rep", "shard"), scatter_dimension=0, tiled=True),
        lax.psum_scatter(small_terms[2], ("rep", "shard"), scatter_dimension=0, tiled=True),
        lax.psum_scatter(small_terms[3], ("rep", "shard"), scatter_dimension=0, tiled=True),
        lax.psum_scatter(small_terms[4], ("rep", "shard"), scatter_dimension=0, tiled=True),
    )
    grad_gain, grad_shift, grad_packed_b, grad_out_b, grad_up_b = reduced
    return (
        output,
        grad_tokens,
        grad_gain,
        grad_shift,
        grad_qkv_w,
        grad_packed_b,
        grad_dense_w,
        grad_out_b,
        grad_up_w,
        grad_up_b,
        grad_down_w,
        grad_out_b,
    )


MIB = 1024 * 1024
VMEM = 60


def params(vmem=VMEM):
    return pltpu.CompilerParams(
        dimension_semantics=("arbitrary",), vmem_limit_bytes=vmem * MIB
    )


def cost(flops, moved):
    return pl.CostEstimate(flops=flops, bytes_accessed=moved, transcendentals=0)


def fixed(shape, start=0):
    index = (start,) + (0,) * (len(shape) - 1)
    return pl.BlockSpec(shape, lambda *_: index, pipeline_mode=pl.Buffered(buffer_count=1))


def whole(array):
    return fixed(array.shape)


def rows_of(array, rows, start=0):
    return pl.BlockSpec((rows, array.shape[1]), lambda i, *_: (i + start // rows, 0))


ANYWHERE = pl.BlockSpec(memory_space=pl.ANY)


def kernel(body, scalars, operands, in_specs, out_specs, out_shape, grid=(1,), scratch=(), work=(0, 0), vmem=16):
    return pl.pallas_call(
        body,
        grid_spec=pltpu.PrefetchScalarGridSpec(
            num_scalar_prefetch=1,
            grid=grid,
            in_specs=in_specs,
            out_specs=out_specs,
            scratch_shapes=list(scratch),
        ),
        out_shape=out_shape,
        compiler_params=params(vmem),
        cost_estimate=cost(*work),
    )(scalars, *operands)


def shaped(shape, dtype=BF16):
    return jax.ShapeDtypeStruct(shape, dtype)


def nn(left_side, right_side):
    return lax.dot_general(
        left_side, right_side, (((1,), (0,)), ((), ())), preferred_element_type=F32
    )


def nt(left_side, right_side):
    return lax.dot_general(
        left_side, right_side, (((1,), (1,)), ((), ())), preferred_element_type=F32
    )


def tn(left_side, right_side):
    return lax.dot_general(
        left_side, right_side, (((0,), (0,)), ((), ())), preferred_element_type=F32
    )


HALF, MIDDLE, ODD, CORE, CHIP = range(5)


def copy_all(copies, sems):
    for at, (source, target) in enumerate(copies):
        pltpu.make_async_copy(source, target, sems.at[at]).start()
    for at, (source, target) in enumerate(copies):
        pltpu.make_async_copy(source, target, sems.at[at]).wait()


def places(where):
    half, odd = where[HALF], where[ODD]
    return (
        (odd, 2 * half + odd),
        (1 - odd, 2 * half + 1 - odd),
        (2 + half, 2 - half),
        (3 - half, 3 - 3 * half),
    )


def copy_pieces(where, pieces, of, sems):
    own, neighbour, other_middle, other_end = places(where)
    common = of(pieces[0], *own) + of(pieces[1], *neighbour)

    @pl.when(where[MIDDLE] == 1)
    def _():
        copy_all(common + of(pieces[2], *other_middle) + of(pieces[3], *other_end), sems)

    @pl.when(where[MIDDLE] == 0)
    def _():
        copy_all(common + of(pieces[4], *other_middle) + of(pieces[5], *other_end), sems)


def multiple(value, size):
    return pl.multiple_of(value * size, size)


def attention_body(parts, run, merge, where, *refs):
    hidden, cot, *refs = refs
    weights, refs = refs[: 6 if merge else 2], refs[6 if merge else 2 :]
    (bias, cosine, sine_a, sine_b, first), refs = refs[:5], refs[5:]
    prior, refs = ((), refs) if merge else (refs[:4], refs[6:])
    (context, d_packed, *grads), refs = refs[:6], refs[6:]
    if merge:
        joined, (sum_qkv, sum_dense, held, out_sems, qkv_w, dense_w, sems) = refs[:2], refs[2:]
        kept = [
            pltpu.make_async_copy(source, target, out_sems.at[4 + i])
            for i, (source, target) in enumerate(zip((qkv_w, dense_w), joined))
        ]
    else:
        (qkv_w, dense_w), (sum_qkv, sum_dense, held, out_sems, before) = weights, refs
        kept = [
            pltpu.make_async_copy(source, before.at[i], out_sems.at[4 + i])
            for i, source in enumerate(prior)
        ]
    step = pl.program_id(0)
    wide = dense_w.shape[0]
    scaling = 1.0 / math.sqrt(HEAD_DIM)
    block, own = sum_qkv.shape[0] // 4, wide // 4
    across = dense_w.shape[1] // parts

    if merge:

        @pl.when(step == 0)
        def _():
            def of(piece, place, plane):
                return [
                    (piece.at[:, : 3 * wide], qkv_w.at[pl.ds(multiple(place, block), block)])
                ] + [
                    (
                        piece.at[j * own : (j + 1) * own, 3 * wide :],
                        dense_w.at[
                            pl.ds(multiple(plane, own), own), j * across : (j + 1) * across
                        ],
                    )
                    for j in range(parts)
                ]

            copy_pieces(where, weights, of, sems)

    @pl.when(step == 0)
    def _():
        for copy in kept:
            copy.start()

    c = jnp.tile(cosine[...], (1, wide // 128))
    sa = jnp.tile(sine_a[...], (1, wide // 128))
    sb = jnp.tile(sine_b[...], (1, wide // 128))

    def turn(value, sign):
        ahead = pltpu.roll(value, wide - ROT // 2, 1)
        behind = pltpu.roll(value, ROT // 2, 1)
        return value * c + sign * (ahead * sa + behind * sb)

    packed = nn(hidden[...], qkv_w[...]) + bias[...]
    queries = (turn(packed[:, :wide], 1.0).astype(BF16).astype(F32) * scaling).astype(BF16)
    keys = turn(packed[:, wide : 2 * wide], 1.0).astype(BF16)
    values = packed[:, 2 * wide :].astype(BF16)
    d_context = nt(cot[...], dense_w[...]).astype(BF16)
    half = run // 2

    def attend(q, k, v, g, begin, after):
        shape = (q.shape[0], k.shape[0])
        at = lax.broadcasted_iota(jnp.int32, shape, 1)
        row = lax.broadcasted_iota(jnp.int32, shape, 0) + after
        starts = first[begin + after : begin + after + q.shape[0], :1]
        seen = (at >= starts) & (at <= row)
        scores = jnp.where(seen, nt(q, k), -1e30)
        raised = jnp.exp(scores - jnp.max(scores, axis=1, keepdims=True))
        probs = raised * (1.0 / jnp.sum(raised, axis=1, keepdims=True))
        low = probs.astype(BF16)
        o = nn(low, v)
        delta = jnp.sum(o * g.astype(F32), axis=1, keepdims=True)
        d_scores = (probs * (nt(g, v) - delta)).astype(BF16)
        return o, nn(d_scores, k) * scaling, tn(d_scores, q), tn(low, g)

    all_out, all_q, all_k, all_v = [], [], [], []
    for begin in range(0, hidden.shape[0], run):
        rows = slice(begin, begin + run)
        out, d_q, d_k, d_v = [], [], [], []
        for h in range(wide // HEAD_DIM):
            part = slice(h * HEAD_DIM, (h + 1) * HEAD_DIM)
            q, k, v, g = (x[rows, part] for x in (queries, keys, values, d_context))
            upper = attend(q[:half], k[:half], v[:half], g[:half], begin, 0)
            lower = attend(q[half:], k, v, g[half:], begin, half)
            out.append(jnp.concatenate([upper[0], lower[0]], axis=0))
            d_q.append(jnp.concatenate([upper[1], lower[1]], axis=0))
            for held_back, i in ((d_k, 2), (d_v, 3)):
                held_back.append(
                    jnp.concatenate([upper[i] + lower[i][:half], lower[i][half:]], axis=0)
                )
        for rows_of_all, new in ((all_out, out), (all_q, d_q), (all_k, d_k), (all_v, d_v)):
            rows_of_all.append(jnp.concatenate(new, axis=1))
    context[...] = jnp.concatenate(all_out, axis=0).astype(BF16)
    d_packed[:, :wide] = turn(jnp.concatenate(all_q, axis=0), -1.0).astype(BF16)
    d_packed[:, wide : 2 * wide] = turn(jnp.concatenate(all_k, axis=0), -1.0).astype(BF16)
    d_packed[:, 2 * wide :] = jnp.concatenate(all_v, axis=0).astype(BF16)

    @pl.when(step == 0)
    def _():
        sum_qkv[...] = jnp.zeros_like(sum_qkv)
        sum_dense[...] = jnp.zeros_like(sum_dense)

    sum_qkv[...] += tn(hidden[...], d_packed[...])
    sum_dense[...] += tn(context[...], cot[...])

    @pl.when(step == pl.num_programs(0) - 1)
    def _():
        for copy in kept:
            copy.wait()

        def value(at, place, plane):
            summed = sum_qkv[pl.ds(multiple(place, block), block), :]
            beside = sum_dense[pl.ds(multiple(plane, own), own), :]
            beside = jnp.concatenate(
                [beside[:, j * across : (j + 1) * across] for j in range(parts)], axis=0
            )
            total = jnp.concatenate([summed, beside], axis=1)
            return total + before[at].astype(F32) if prior else total

        write_blocks(where, value, grads, held, out_sems)


def attention(where, run, parts, hidden, cot, weights, streams, prior, filled):
    count, width = 2 * hidden.shape[0], hidden.shape[1]
    merge = not prior
    bias = streams[0]
    wide = bias.shape[1] // 3
    rows = run
    steps = count // rows // 2
    start = 0 if merge else steps
    grad = shaped((width // 4, 3 * wide + width // parts))

    def rows_of_run(columns):
        return pl.BlockSpec((rows, columns), lambda i, _: (i + start, 0))

    joined = [shaped((width, 3 * wide)), shaped((wide, width))] if merge else []
    operands = [hidden, cot, *weights, *streams, *prior, *filled]
    first_filled = 1 + len(operands) - len(filled)
    outs = pl.pallas_call(
        functools.partial(attention_body, parts, run, merge),
        grid_spec=pltpu.PrefetchScalarGridSpec(
            num_scalar_prefetch=1,
            grid=(steps,),
            in_specs=[pl.BlockSpec((rows, width), lambda i, _: (i, 0))] * 2
            + ([ANYWHERE] * 6 if merge else [whole(array) for array in weights])
            + [whole(bias)]
            + [rows_of_run(array.shape[1]) for array in streams[1:]]
            + [ANYWHERE for _ in (*prior, *filled)],
            out_specs=[rows_of_run(wide), rows_of_run(3 * wide)]
            + [ANYWHERE] * (4 + len(joined)),
            scratch_shapes=[
                pltpu.VMEM((width, 3 * wide), F32),
                pltpu.VMEM((wide, width), F32),
                pltpu.VMEM((4,) + grad.shape, BF16),
                pltpu.SemaphoreType.DMA((8,)),
            ]
            + [pltpu.VMEM(array.shape, BF16) for array in joined]
            + (
                [pltpu.SemaphoreType.DMA((4 * (1 + parts),))]
                if merge
                else [pltpu.VMEM((4,) + grad.shape, BF16)]
            ),
        ),
        out_shape=[shaped((count, wide)), shaped((count, 3 * wide))] + [grad] * 4 + joined,
        input_output_aliases={first_filled + i: i for i in range(len(filled))},
        compiler_params=params(),
        cost_estimate=cost(18 * 10**9, 20 * MIB),
    )(where, *operands)
    return outs[:2], outs[2:6], outs[6:]


GELU_A = math.sqrt(2.0 / math.pi)
GELU_B = 0.044715


def write_blocks(where, values, grads, held, sems):
    copies = []
    for at, (out, place) in enumerate(zip(grads, places(where))):
        held[at] = values(at, *place).astype(BF16)
        copies.append(pltpu.make_async_copy(held.at[at], out, sems.at[at]))
        copies[-1].start()
    for copy in copies:
        copy.wait()


def forward_body(columns, where, hidden, cot, *refs):
    pieces, (bias, active, slope, joined), refs = refs[:6], refs[6:10], refs[10:]
    (*grads, total, up_w, held, sems, out_sems) = refs
    step, last = pl.program_id(0), pl.num_programs(0) - 1
    join = pltpu.make_async_copy(up_w, joined, out_sems.at[4])

    @pl.when(step == 0)
    def _():
        size = pieces[0].shape[0]

        def of(piece, place, plane):
            return [(piece, up_w.at[pl.ds(multiple(place, size), size)])]

        copy_pieces(where, pieces, of, sems)
        join.start()
        total[...] = jnp.zeros_like(total)

    for j in range(up_w.shape[1] // columns):
        part = slice(j * columns, (j + 1) * columns)
        v = nn(hidden[...], up_w[:, part]) + bias[:, part]
        square = v * v
        t = jnp.tanh(GELU_A * v * (1.0 + GELU_B * square))
        gate = 0.5 * (1.0 + t)
        low = (v * gate).astype(BF16)
        active[:, part] = low
        slope[:, part] = (
            gate + 0.5 * v * (1.0 - t * t) * (GELU_A + (3.0 * GELU_A * GELU_B) * square)
        ).astype(BF16)
        total[part] += tn(low, cot[...])

    @pl.when(step == last)
    def _():
        size = grads[0].shape[0]

        def block(at, place, plane):
            return total[pl.ds(multiple(plane, size), size), :]

        write_blocks(where, block, grads, held, out_sems)
        join.wait()


def forward(where, hidden, cot, pieces, bias, rows=512, columns=512):
    count, wide = hidden.shape[0], bias.shape[1]
    width = cot.shape[1]
    grad = shaped((wide // 4, width))
    outs = kernel(
        functools.partial(forward_body, columns),
        where,
        [hidden, cot, *pieces, bias],
        [rows_of(hidden, rows), rows_of(cot, rows)] + [ANYWHERE] * 6 + [whole(bias)],
        [pl.BlockSpec((rows, wide), lambda i, _: (i, 0))] * 2
        + [ANYWHERE] * 5,
        [shaped((count, wide))] * 2 + [shaped((width, wide))] + [grad] * 4,
        grid=(count // rows,),
        scratch=[
            pltpu.VMEM((wide, width), F32),
            pltpu.VMEM((width, wide), BF16),
            pltpu.VMEM((4,) + grad.shape, BF16),
            pltpu.SemaphoreType.DMA((4,)),
            pltpu.SemaphoreType.DMA((5,)),
        ],
        work=(4 * count * width * wide, 32 * MIB),
        vmem=VMEM,
    )
    return outs[0], outs[1], outs[2], outs[3:]


def backward_body(where, cot, hidden, *refs):
    pieces, (slope, d_upward, sums, joined), refs = refs[:6], refs[6:10], refs[10:]
    (*grads, total, down_w, held, sems, out_sems) = refs
    step, last = pl.program_id(0), pl.num_programs(0) - 1
    join = pltpu.make_async_copy(down_w, joined, out_sems.at[4])

    @pl.when(step == 0)
    def _():
        size = pieces[0].shape[0]

        def of(piece, place, plane):
            return [(piece, down_w.at[pl.ds(multiple(plane, size), size)])]

        copy_pieces(where, pieces, of, sems)
        join.start()
        sums[...] = jnp.zeros_like(sums)
        total[...] = jnp.zeros_like(total)

    low = (nt(cot[...], down_w[...]) * slope[...].astype(F32)).astype(BF16)
    d_upward[...] = low
    sums[...] += jnp.sum(low.astype(F32), axis=0, keepdims=True)
    total[...] += tn(hidden[...], low)

    @pl.when(step == last)
    def _():
        size = grads[0].shape[0]

        def block(at, place, plane):
            return total[pl.ds(multiple(place, size), size), :]

        write_blocks(where, block, grads, held, out_sems)
        join.wait()


def backward(where, cot, hidden, pieces, slope, rows=256):
    count, wide = slope.shape
    width = hidden.shape[1]
    grad = shaped((width // 4, wide))
    outs = kernel(
        backward_body,
        where,
        [cot, hidden, *pieces, slope],
        [rows_of(cot, rows), rows_of(hidden, rows)] + [ANYWHERE] * 6 + [rows_of(slope, rows)],
        [
            pl.BlockSpec((rows, wide), lambda i, _: (i, 0)),
            pl.BlockSpec((1, wide), lambda i, _: (0, 0)),
        ]
        + [ANYWHERE] * 5,
        [shaped((count, wide)), shaped((1, wide), F32), shaped((wide, width))] + [grad] * 4,
        grid=(count // rows,),
        scratch=[
            pltpu.VMEM((width, wide), F32),
            pltpu.VMEM((wide, width), BF16),
            pltpu.VMEM((4,) + grad.shape, BF16),
            pltpu.SemaphoreType.DMA((4,)),
            pltpu.SemaphoreType.DMA((5,)),
        ],
        work=(4 * count * width * wide, 32 * MIB),
        vmem=VMEM,
    )
    return outs[0], outs[1], outs[2], outs[3:]


def two_dots_body(dot, a, aw, b, bw, far, near):
    result = (dot(a[...], aw[...]) + dot(b[...], bw[...])).astype(BF16)
    step, half = pl.program_id(0), pl.num_programs(0) // 2

    @pl.when(step < half)
    def _():
        far[...] = result

    @pl.when(step >= half)
    def _():
        near[...] = result


def two_dots(dot, a, aw, b, bw, width, rows=256):
    count = a.shape[0]
    steps = count // rows
    half = steps // 2

    def of(array):
        return pl.BlockSpec((rows, array.shape[1]), lambda i: (lax.rem(i + half, steps), 0))

    shape = jax.ShapeDtypeStruct((count // 2, width), BF16)
    return pl.pallas_call(
        functools.partial(two_dots_body, dot),
        grid=(steps,),
        in_specs=[of(a), whole(aw), of(b), whole(bw)],
        out_specs=[
            pl.BlockSpec((rows, width), lambda i: (jnp.minimum(i, half - 1), 0)),
            pl.BlockSpec((rows, width), lambda i: (jnp.maximum(i - half, 0), 0)),
        ],
        out_shape=[shape, shape],
        compiler_params=params(),
        cost_estimate=cost(
            2 * count * (aw.size + bw.size),
            count * 2 * (width + a.shape[1] + b.shape[1]) + 2 * (aw.size + bw.size),
        ),
    )(a, aw, b, bw)


def deal_first_body(planes, chips, where, up, qkv, keep, send):
    mates, n = CORES * chips, up.shape[0]
    block = up.shape[1] // (planes * mates)
    for core in range(CORES):
        for chip in range(chips):
            i = core * chips + chip
            pieces = [
                up[:, (p * mates + i) * block : (p * mates + i + 1) * block] for p in range(planes)
            ] + [
                qkv[:, (t * mates + i) * HEAD_DIM : (t * mates + i + 1) * HEAD_DIM]
                for t in range(3 * planes)
            ]
            value = jnp.concatenate(pieces, axis=1)

            @pl.when(where[CORE] == core)
            def _():
                keep[chip] = value

            @pl.when(where[CORE] != core)
            def _():
                send[chip] = value


def deal_first(where, planes, chips, up, qkv):
    out = shaped((chips, up.shape[0], (up.shape[1] + qkv.shape[1]) // (CORES * chips)))
    return kernel(
        functools.partial(deal_first_body, planes, chips),
        where,
        [up, qkv],
        [whole(up), whole(qkv)],
        [fixed(out.shape)] * 2,
        [out] * 2,
        work=(0, 4 * MIB),
    )


def deal_second_body(where, keep, came, *outs):
    core = where[CORE]
    for r, out in enumerate(outs):
        at = where[CHIP] ^ r
        out[pl.ds(core, 1)] = keep[pl.ds(at, 1)]
        out[pl.ds(1 - core, 1)] = came[pl.ds(at, 1)]


def deal_second(where, keep, came):
    chips, n, columns = keep.shape
    out = shaped((CORES, n, columns))
    return kernel(
        deal_second_body,
        where,
        [keep, came],
        [whole(keep), whole(came)],
        [fixed(out.shape)] * chips,
        [out] * chips,
        work=(0, 4 * MIB),
    )


def deal_last_body(chips, where, *refs):
    blocks, dense, (u, a) = refs[:chips], refs[chips], refs[chips + 1 :]
    n, columns = blocks[0].shape[1:]
    middle = u.shape[1]
    wide = columns - middle
    for r, block in enumerate(blocks):
        for core in range(CORES):
            rows = pl.ds(multiple(core * chips + (where[CHIP] ^ r), n), n)
            u[rows, :] = block[core, :, :middle]
            a[rows, :wide] = block[core, :, middle:]
    across = a.shape[1] - wide
    for j in range(dense.shape[1] // across):
        a[j * n : (j + 1) * n, wide:] = dense[:, j * across : (j + 1) * across]


def deal_last(where, blocks, dense, middle):
    chips = len(blocks)
    n, columns = blocks[0].shape[1:]
    mates = CORES * chips
    shapes = [
        shaped((mates * n, middle)),
        shaped((mates * n, columns - middle + dense.shape[1] // mates)),
    ]
    return kernel(
        functools.partial(deal_last_body, chips),
        where,
        [*blocks, dense],
        [whole(array) for array in (*blocks, dense)],
        [fixed(shape.shape) for shape in shapes],
        shapes,
        work=(0, 4 * MIB),
    )


def finish_body(chips, wide, where, own, middle, last, *outs):
    keep, send = outs[:2]
    n = own.shape[0]
    step = n // (CORES * chips)
    total = own[...].astype(F32) + middle[...].astype(F32) + last[...].astype(F32)
    low = total[:, :wide].astype(BF16)
    for core in range(CORES):

        @pl.when(where[CORE] == core)
        def _():
            for chip in range(chips):
                at = (core * chips + chip) * step
                keep[chip] = low[at : at + step]
                at = ((1 - core) * chips + chip) * step
                send[chip] = low[at : at + step]

    if len(outs) == 3:
        beside = outs[2]
        across = total.shape[1] - wide
        for j in range(n // step):
            beside[:, j * across : (j + 1) * across] = total[j * step : (j + 1) * step, wide:]


def finish(where, chips, wide, own, middle, last):
    n, columns = own.shape
    step = n // (CORES * chips)
    shapes = [shaped((chips, step, wide))] * 2
    if wide < columns:
        shapes.append(shaped((step, (columns - wide) * CORES * chips), F32))
    return kernel(
        functools.partial(finish_body, chips, wide),
        where,
        [own, middle, last],
        [whole(own)] * 3,
        [fixed(shape.shape) for shape in shapes],
        shapes,
        work=(0, 4 * MIB),
    )


def back_body(groups, where, *refs):
    blocks, out, held = refs[:-2], refs[-2], refs[-1]
    chips = len(blocks)
    n, columns = blocks[0].shape[1:]
    size = columns // groups
    for r, block in enumerate(blocks):
        held[pl.ds(where[CHIP] ^ r, 1)] = block[...][None]
    for group in range(groups):
        for core in range(CORES):
            start = (group * CORES + core) * chips * size
            out[:, start : start + chips * size] = jnp.concatenate(
                [held[chip, core, :, group * size : (group + 1) * size] for chip in range(chips)],
                axis=1,
            ).astype(F32)


def back(where, blocks, groups):
    chips = len(blocks)
    n, columns = blocks[0].shape[1:]
    out = shaped((n, columns * CORES * chips), F32)
    return kernel(
        functools.partial(back_body, groups),
        where,
        blocks,
        [whole(block) for block in blocks],
        fixed(out.shape),
        out,
        scratch=[pltpu.VMEM((chips,) + blocks[0].shape, BF16)],
        work=(0, 4 * MIB),
    )


def corners_body(where, *refs):
    sources, outs = refs[:-2], refs[-2:]
    for at in range(len(sources) // 4):
        for i, out in enumerate(outs):
            near, came = sources[4 * at + 2 * i], sources[4 * at + 2 * i + 1]
            rows = near.shape[0]
            total = near[...].astype(F32) + came[...].astype(F32)
            out[at * rows : (at + 1) * rows] = total.astype(BF16)


def corners(where, *sums):
    rows, width = sums[0][0].shape[0] // 8, sums[0][0].shape[1]
    out = shaped((len(sums) * rows, width))
    return kernel(
        corners_body,
        where,
        [term for terms in sums for _ in range(2) for term in terms],
        [fixed((rows, width), 6 + i) for _ in sums for i in range(2) for _ in range(2)],
        [fixed(out.shape)] * 2,
        [out] * 2,
        work=(0, 4 * MIB),
    )


def pair_halves_body(where, *refs):
    sources, outs = refs[:-2], refs[-2:]
    for at in range(len(sources) // 2):
        for i, out in enumerate(outs):
            rows = sources[0].shape[0]
            out[at * rows : (at + 1) * rows] = sources[2 * at + i][...]


def pair_halves(where, *pairs):
    rows, width = pairs[0][0].shape[0] // 2, pairs[0][0].shape[1]
    out = shaped((len(pairs) * rows, width))
    return kernel(
        pair_halves_body,
        where,
        [array for by_x, by_y in pairs for array in (by_y, by_x)],
        [fixed((rows, width), i) for _ in pairs for i in range(2)],
        [fixed(out.shape)] * 2,
        [out] * 2,
        work=(0, 4 * MIB),
    )


def sides_body(where, near_x, near_y, came_x, came_y, extra_x, extra_y, for_x, for_y):
    half = extra_x.shape[0]
    x = near_x[...].astype(F32) + came_x[...].astype(F32)
    y = near_y[...].astype(F32) + came_y[...].astype(F32)
    for_x[:half] = x[:half].astype(BF16)
    for_x[half:] = (x[half:] + extra_x[...].astype(F32)).astype(BF16)
    for_y[:half] = (y[:half] + extra_y[...].astype(F32)).astype(BF16)
    for_y[half:] = y[half:].astype(BF16)


def sides(where, near, came, extra_y, extra_x, at):
    rows, width = near.shape[0] // 4, near.shape[1]
    blocks = [fixed((rows, width), 1), fixed((rows, width), 2)]
    return kernel(
        sides_body,
        where,
        [near, near, came, came, extra_x, extra_y],
        blocks * 2 + [fixed((rows // 2, width), at)] * 2,
        [fixed((rows, width))] * 2,
        [shaped((rows, width))] * 2,
        work=(0, 8 * MIB),
    )


def norm_back_body(
    where, near, came, by_x, by_y, tokens, cot, gain, grad_tokens, gain_sum, shift_sum
):
    parts = [ref[...].astype(F32) for ref in (near, came, by_x, by_y)]
    turned = parts[0] + parts[1] + parts[2] + parts[3]
    middle = turned.shape[1] // 2
    swap = where[HALF] == 1
    lower, upper = turned[:, :middle], turned[:, middle:]
    d_hidden = jnp.concatenate(
        [jnp.where(swap, upper, lower), jnp.where(swap, lower, upper)], axis=1
    )
    inputs = tokens[...].astype(F32)
    centered = inputs - jnp.mean(inputs, axis=1, keepdims=True)
    inv_std = lax.rsqrt(jnp.mean(centered * centered, axis=1, keepdims=True) + EPSILON)
    normed = centered * inv_std
    d_norm = d_hidden * gain[...]
    d_inputs = inv_std * (
        d_norm
        - jnp.mean(d_norm, axis=1, keepdims=True)
        - normed * jnp.mean(d_norm * normed, axis=1, keepdims=True)
    )
    grad_tokens[...] = (cot[...].astype(F32) + d_inputs).astype(BF16)

    @pl.when(pl.program_id(0) == 0)
    def _():
        gain_sum[...] = jnp.zeros_like(gain_sum)
        shift_sum[...] = jnp.zeros_like(shift_sum)

    gain_sum[...] += jnp.sum(d_hidden * normed, axis=0, keepdims=True)
    shift_sum[...] += jnp.sum(d_hidden, axis=0, keepdims=True)


def norm_back(where, near, came, by_x, by_y, tokens, cot, gain, rows=128):
    count, width = tokens.shape
    block = pl.BlockSpec((rows, width), lambda i, _: (i, 0))
    return kernel(
        norm_back_body,
        where,
        [near, came, by_x, by_y, tokens, cot, gain],
        [block] * 6 + [whole(gain)],
        [block, fixed((1, width)), fixed((1, width))],
        [shaped((count, width)), shaped((1, width), F32), shaped((1, width), F32)],
        grid=(count // rows,),
        work=(0, 8 * MIB),
    )


def tied(*groups):
    return lax.optimization_barrier(groups)


def by_planes(
    planes,
    mates,
    tokens,
    lengths,
    ln_gain,
    ln_bias,
    qkv_weight,
    qkv_bias,
    dense_weight,
    dense_bias,
    up_weight,
    up_bias,
    down_weight,
    down_bias,
    cotangent,
):
    row_count, width = tokens.shape
    owners = planes * mates
    chips = mates // CORES
    rank = lax.axis_index("rep") * chips + lax.axis_index("shard")
    z, m = rank // mates, rank % mates
    c, s = m // chips, m % chips
    middle_plane = jnp.where((z == 1) | (z == 2), 1, 0)
    where = jnp.stack([z // 2, middle_plane, z % 2, c, s]).astype(jnp.int32)
    rows_own = qkv_weight.shape[0]
    ff_block = up_bias.shape[0]
    heads_width = planes * HEAD_DIM
    count = mates * row_count

    def flip(value, r):
        return lax.ppermute(
            value,
            AXES,
            [(p * mates + i, p * mates + (i ^ r)) for p in range(planes) for i in range(mates)],
        )

    def between(value, pairs):
        return lax.ppermute(
            value, AXES, [(p * mates + i, q * mates + i) for p, q in pairs for i in range(mates)]
        )

    def to_neighbour(value):
        return between(value, [(p, p ^ 1) for p in range(planes)])

    def over_middle(value):
        return between(value, [(1, 2), (2, 1)])

    def outwards(value):
        return between(value, [(1, 0), (2, 3)])

    def inwards(value):
        return between(value, [(0, 1), (3, 2)])

    def added(*terms):
        return sum(term.astype(F32) for term in terms)

    def add(*terms, dtype=BF16):
        return added(*terms).astype(dtype)

    def deal_over_chips(keep, send):
        blocks = deal_second(where, keep, flip(send, chips))
        return [blocks[0]] + [flip(blocks[r], r) for r in range(1, chips)]

    def over_planes(table):
        return table + sum(
            between(table, [(p, (p + r) % planes) for p in range(planes)])
            for r in range(1, planes)
        )

    def over_chips(table):
        return table + sum(flip(table, r) for r in range(1, chips))

    def over_chips_in_turn(table):
        for r in (1, 2):
            table = table + flip(table, r)
        return table

    def over_cores(table):
        return table + flip(table, chips)

    def turned(value):
        middle = value.shape[1] // 2
        lower, upper, first_half = value[:, :middle], value[:, middle:], z < 2
        return jnp.concatenate(
            [jnp.where(first_half, lower, upper), jnp.where(first_half, upper, lower)], axis=1
        )

    half = row_count // 2

    def near_first(block):
        return flip(block, 1), flip(block, 2)

    parts = [ln_gain, ln_bias, qkv_bias, dense_bias, up_bias, down_bias, lengths[0].astype(BF16)]
    sizes = [part.shape[0] for part in parts]
    starts = [sum(sizes[:i]) for i in range(len(sizes))]
    own_row = jnp.concatenate(parts)
    own_row = jnp.pad(own_row, (0, -len(own_row) % 128))
    first_pieces = deal_first(where, planes, chips, up_weight, qkv_weight)
    table = jnp.where(jnp.arange(owners)[:, None] == rank, own_row[None, :], 0)
    wide = 3 * heads_width
    keep, send = first_pieces
    table = over_planes(table)
    blocks, table, down_own = tied(deal_second(where, keep, flip(send, chips)), table, down_weight)
    dealt = [blocks[0]] + [flip(blocks[r], r) for r in range(1, chips)]
    w1, w2a = to_neighbour(down_own), over_middle(down_own)
    table, dealt[1], dealt[2] = tied(table, dealt[1], dealt[2])
    table = over_cores(over_chips(table))
    u_own, a_own = deal_last(where, dealt, dense_weight, planes * ff_block)
    u_own, a_own, table, w1, w2a, cot_own = tied(
        u_own, a_own, table, w1, w2a, cotangent
    )
    table = table.astype(F32)

    a1, a2a = to_neighbour(a_own), over_middle(a_own)
    cot_near = near_first(cot_own)

    def column(i):
        return table[:, starts[i] : starts[i] + sizes[i]].reshape(-1)

    gain, shift_by = column(0), column(1)
    packed_bias = lax.dynamic_index_in_dim(
        column(2).reshape(3, planes, mates, HEAD_DIM), m, 2, keepdims=False
    ).reshape(1, -1)
    upward_bias = lax.dynamic_index_in_dim(
        column(4).reshape(planes, mates, ff_block), m, 1, keepdims=False
    ).reshape(1, -1)
    out_bias = column(3) + column(5)
    all_lengths = table[:, starts[6] : starts[6] + sizes[6]].astype(jnp.int32)
    doc_sizes = jnp.stack(
        [
            lax.dynamic_index_in_dim(all_lengths, z * mates + (m ^ r), 0, keepdims=False)
            for r in range(mates)
        ]
    )

    inputs_f = tokens.astype(F32)
    average = jnp.mean(inputs_f, axis=1, keepdims=True)
    centered = inputs_f - average
    spread = jnp.mean(centered * centered, axis=1, keepdims=True)
    inv_std = lax.rsqrt(spread + EPSILON)
    normed = centered * inv_std
    hidden_own = turned((normed * gain + shift_by).astype(BF16))

    ends_at = jnp.cumsum(doc_sizes, axis=1)
    at = jnp.arange(row_count, dtype=jnp.int32)
    offsets = jnp.max(jnp.where(at[None, :, None] >= ends_at[:, None, :], ends_at[:, None, :], 0), axis=2)
    places = (at[None, :] - offsets).astype(F32).reshape(count, 1)
    lane = jnp.arange(2 * HEAD_DIM, dtype=jnp.int32) % HEAD_DIM
    inverse = jnp.power(jnp.float32(10000.0), -2.0 * (lane % (ROT // 2)).astype(F32) / ROT)
    angles = places * inverse[None, :]
    sine = jnp.sin(angles)
    cosine = jnp.where(lane < ROT, jnp.cos(angles), 1.0)
    sine_a = jnp.where(lane < ROT // 2, -sine, 0.0)
    sine_b = jnp.where((lane >= ROT // 2) & (lane < ROT), sine, 0.0)
    first = jnp.broadcast_to(offsets.reshape(count, 1), (count, 2 * HEAD_DIM))

    a1, a2a, cot_near, hidden_own, u_own = tied(a1, a2a, cot_near, hidden_own, u_own)
    a3a, a2b = outwards(a2a), over_middle(a1)
    hidden_near = near_first(hidden_own)

    a3a, a2b, hidden_near, cot_near, u_own = tied(a3a, a2b, hidden_near, cot_near, u_own)
    a3b, u2a = outwards(a2b), over_middle(u_own)
    for_x, for_y = pair_halves(where, cot_near, hidden_near)
    corner_y, corner_x = flip(for_x, 1), flip(for_y, 2)
    room = jnp.zeros((row_count, width), BF16)
    cot_most = jnp.concatenate([cot_own, *cot_near, room], axis=0)
    hidden_most = jnp.concatenate([hidden_own, *hidden_near, room], axis=0)

    a3b, u2a, corner_x, corner_y, hidden_most, cot_most, u_own, w1, cosine, sine_a, sine_b, first = tied(
        a3b, u2a, corner_x, corner_y, hidden_most, cot_most, u_own, w1, cosine, sine_a, sine_b, first
    )
    u1, w2b = to_neighbour(u_own), over_middle(w1)
    def with_corners(most, at):
        for i, corner in enumerate((corner_y, corner_x)):
            most = lax.dynamic_update_slice_in_dim(
                most, corner[at : at + half], 3 * row_count + i * half, 0
            )
        return most

    cot, hidden = with_corners(cot_most, 0), with_corners(hidden_most, half)
    hidden, cot = [hidden, flip(hidden, chips)], [cot, flip(cot, chips)]
    streams = [packed_bias, cosine, sine_a, sine_b, first]
    rows_a, g_a, (qkv_w, dense_w) = attention(
        where,
        row_count,
        mates,
        hidden[0],
        cot[0],
        [a_own, a1, a2a, a2b, a3a, a3b],
        streams,
        [],
        [],
    )

    u1, w2b, u2a, rows_a, g_a, hidden, cot = tied(u1, w2b, u2a, rows_a, g_a, hidden, cot)
    u3a, u2b = outwards(u2a), over_middle(u1)
    (context, d_packed), g_a, _ = attention(
        where, row_count, mates, hidden[1], cot[1], [qkv_w, dense_w], streams, g_a, rows_a
    )

    u3a, u2b, g_a, w2a, d_packed, hidden, cot = tied(u3a, u2b, g_a, w2a, d_packed, hidden, cot)
    u3b, q1_a_end = outwards(u2b), inwards(g_a[3])
    hidden, cot = jnp.concatenate(hidden, axis=0), jnp.concatenate(cot, axis=0)
    mine = jnp.arange(mates) == m
    packed_sum = jnp.sum(d_packed.astype(F32), axis=0).reshape(3, planes, 1, HEAD_DIM)
    packed_sum = jnp.where(mine[None, None, :, None], packed_sum, 0.0).reshape(owners, -1)
    cot_sum = jnp.sum(cotangent.astype(F32), axis=0).reshape(owners, -1)

    u3b, q1_a_end, g_a, w2a, hidden, cot, packed_sum, cot_sum = tied(
        u3b, q1_a_end, g_a, w2a, hidden, cot, packed_sum, cot_sum
    )
    w3a, q1_a_mid = outwards(w2a), inwards(g_a[2])
    active, slope, up_w, g_w = forward(
        where, hidden, cot, [u_own, u1, u2a, u2b, u3a, u3b], upward_bias
    )

    w3a, q1_a_mid, q1_a_end, g_a, g_w, w2b = tied(w3a, q1_a_mid, q1_a_end, g_a, g_w, w2b)
    w3b, q1_w_end, q2_a_end = outwards(w2b), inwards(g_w[3]), over_middle(add(g_a[3], q1_a_end))
    share_a_mid = add(g_a[2], q1_a_mid)

    w3b, q1_w_end, q2_a_end, share_a_mid, g_a, g_w, cot = tied(
        w3b, q1_w_end, q2_a_end, share_a_mid, g_a, g_w, cot
    )
    q3_a, q2_a_mid = to_neighbour(add(g_a[1], q2_a_end)), over_middle(share_a_mid)
    d_upward, upward_sum, down_w, g_u = backward(
        where, cot, hidden, [down_own, w1, w2a, w2b, w3a, w3b], slope
    )

    q3_a, q2_a_mid, g_w, g_u, d_upward, upward_sum = tied(
        q3_a, q2_a_mid, g_w, g_u, d_upward, upward_sum
    )
    q1_u_end = inwards(g_u[3])
    d_hidden_far, d_hidden_near = two_dots(nt, d_packed, qkv_w, d_upward, up_w, width)
    upward_sum = upward_sum.reshape(planes, 1, ff_block)
    upward_sum = jnp.where(mine[None, :, None], upward_sum, 0.0).reshape(owners, -1)
    keep, send, grad_dense_w = finish(where, chips, wide, g_a[0], q2_a_mid, q3_a)
    came = flip(send, chips)

    q1_u_end, d_hidden_far, d_hidden_near, g_u, g_w, context, upward_sum, keep, came = tied(
        q1_u_end, d_hidden_far, d_hidden_near, g_u, g_w, context, upward_sum, keep, came
    )
    q1_u_mid, q2_u_end = inwards(g_u[2]), over_middle(add(g_u[3], q1_u_end))
    d_hidden_came = flip(d_hidden_far, chips)
    out_far, out_near = two_dots(nn, context, dense_w, active, down_w, width)
    corner_y, corner_x = corners(where, (d_hidden_near, d_hidden_came))
    extra_y, extra_x = flip(corner_y, 1), flip(corner_x, 2)

    q1_u_mid, q2_u_end, extra_x, extra_y, out_far, out_near, g_u, g_w, keep = tied(
        q1_u_mid, q2_u_end, extra_x, extra_y, out_far, out_near, g_u, g_w, keep
    )
    q3_u, q2_u_mid = to_neighbour(add(g_u[1], q2_u_end)), over_middle(add(g_u[2], q1_u_mid))
    out_came = flip(out_far, chips)
    corner_y, corner_x = corners(where, (out_near, out_came))
    out_extra_y, out_extra_x = flip(corner_y, 1), flip(corner_x, 2)
    blocks = deal_second(where, keep, came)

    q3_u, q2_u_mid, out_extra_x, out_extra_y, g_u, g_w, q1_w_end, blocks = tied(
        q3_u, q2_u_mid, out_extra_x, out_extra_y, g_u, g_w, q1_w_end, blocks
    )
    q1_w_mid, q2_w_end = inwards(g_w[2]), over_middle(add(g_w[3], q1_w_end))
    for_x, for_y = sides(where, d_hidden_near, d_hidden_came, extra_y, extra_x, 0)
    d_hidden_last = flip(for_x, 1), flip(for_y, 2)
    block_x, block_y, block_xy = [flip(blocks[r], r) for r in range(1, chips)]
    for_x, for_y = sides(where, out_near, out_came, out_extra_y, out_extra_x, 0)
    keep, send = finish(where, chips, planes * ff_block, g_u[0], q2_u_mid, q3_u)

    (
        q1_w_mid,
        q2_w_end,
        d_hidden_last,
        for_x,
        for_y,
        g_w,
        block_x,
        block_y,
        block_xy,
        keep,
        send,
    ) = tied(
        q1_w_mid,
        q2_w_end,
        d_hidden_last,
        for_x,
        for_y,
        g_w,
        block_x,
        block_y,
        block_xy,
        keep,
        send,
    )
    q3_w, q2_w_mid = to_neighbour(add(g_w[1], q2_w_end)), over_middle(add(g_w[2], q1_w_mid))
    out_last = flip(for_x, 1), flip(for_y, 2)
    held = deal_second(where, keep, flip(send, chips))
    grad_tokens, gain_sum, shift_sum = norm_back(
        where,
        d_hidden_near,
        d_hidden_came,
        *d_hidden_last,
        tokens,
        cotangent,
        gain.reshape(1, -1),
    )
    sums = jnp.concatenate(
        [
            gain_sum.reshape(owners, -1),
            shift_sum.reshape(owners, -1),
            cot_sum,
            packed_sum,
            upward_sum,
        ],
        axis=1,
    )

    sums = over_cores(sums)
    q3_w, q2_w_mid, g_w, out_last, sums, held = tied(q3_w, q2_w_mid, g_w, out_last, sums, held)
    received = [flip(held[r], r) for r in range(1, chips)]
    for r in (1, 2):
        sums = sums + between(sums, [(p, p ^ r) for p in range(planes)])
    grad_qkv_w = back(where, [blocks[0], block_x, block_y, block_xy], 3 * planes)
    output = added(out_near[:row_count], out_came[:row_count], *out_last)
    output = (inputs_f + output + out_bias).astype(BF16)
    grad_down_w = add(g_w[0], q2_w_mid, q3_w, dtype=F32)
    received, sums, grad_qkv_w, output, grad_down_w = tied(
        received, sums, grad_qkv_w, output, grad_down_w
    )
    sums = over_chips(sums)
    grad_up_w = back(where, [held[0]] + received, planes)
    total = lax.dynamic_index_in_dim(sums, rank, 0, keepdims=False)
    grad_gain, grad_shift, grad_out_b, grad_packed_b, grad_up_b = jnp.split(
        total,
        [
            sizes[0],
            sizes[0] + sizes[1],
            sizes[0] + sizes[1] + sizes[3],
            sizes[0] + sizes[1] + sizes[3] + sizes[2],
        ],
    )
    return (
        output,
        grad_tokens,
        grad_gain,
        grad_shift,
        grad_qkv_w,
        grad_packed_b,
        grad_dense_w,
        grad_out_b,
        grad_up_w,
        grad_up_b,
        grad_down_w,
        grad_out_b,
    )


def solution(mesh):
    planes, mates = mesh.shape["rep"] // CORES, CORES * mesh.shape["shard"]
    rows, vector = P(AXES, None), P(AXES)

    def layer(*arrays):
        width = arrays[0].shape[1]
        if mesh.shape["shard"] == 4 and planes * mates * HEAD_DIM == width:
            return by_planes(planes, mates, *arrays)
        return gathered_whole(*arrays)

    return jax.shard_map(
        layer,
        mesh=mesh,
        in_specs=(
            rows, rows, vector, vector, rows, vector, rows, vector, rows, vector, rows, vector, rows,
        ),
        out_specs=(
            rows, rows, vector, vector, rows, vector, rows, vector, rows, vector, rows, vector,
        ),
        check_vma=False,
    )
```
